32 devices in a mesh: seq: 8 (over z, x), tensor: 4 (over y, core).
Axes of the slice: x: 2, y: 2, z: 4, core: 2. Of those that a mesh axis runs over, the one named last changes fastest.
Arguments:
- query_rows: bfloat16 [2048, 4096], P('seq', 'tensor'), may hold values from -5 to 5
- key_rows: bfloat16 [2048, 4096], P('seq', 'tensor'), may hold values from -5 to 5
- value_rows: bfloat16 [2048, 4096], P('seq', 'tensor'), may hold values from -6 to 6
- query_tan: bfloat16 [2048, 4096], P('seq', 'tensor'), may hold values from -6 to 6
- key_tan: bfloat16 [2048, 4096], P('seq', 'tensor'), may hold values from -6 to 6
- value_tan: bfloat16 [2048, 4096], P('seq', 'tensor'), may hold values from -6 to 6
- routes: int32 [2048, 32], P('seq', 'tensor'), may hold values from 0 to 2047, as said below
- out_weight: bfloat16 [4096, 4096], P('tensor'), may hold values from -0.125 to 0.125
Outputs:
- output: bfloat16 [2048, 4096], P('seq', 'tensor')
- output_tan: bfloat16 [2048, 4096], P('seq', 'tensor')
The draws below stay inside these ranges and needn't reach their ends.
Inputs may be any that keep to these rules, and one draw needn't show every extreme that they name: `routes`: each head's column holds every slot of 0 to 2047 once; slot // 256 is the token's cluster. Every aligned block of 256 tokens puts exactly 32 of its tokens into each aligned block of 256 slots, for every head.
All inputs are finite; a program needn't handle non-finite values.
Results may differ from the reference program's by a relative error of at most 0.0058.
Values may be sent and summed in bfloat16 or wider, within the bound.
A program may use at most 64 MiB of HBM per device.

```python
import jax
import jax.numpy as jnp
from jax import lax

D = 4096
HEADS = 32
HEAD_SIZE = 128
CLUSTER = 256
TOK_DEV = 256
TOKENS = 2048


def paired_rows(key):
    shape = (TOKENS, HEADS, HEAD_SIZE)
    query_stream = jax.random.fold_in(key, 101)
    key_stream = jax.random.fold_in(key, 102)
    queries = jnp.clip(jax.random.normal(query_stream, shape, jnp.float32), -5.0, 5.0)
    key_vals = jnp.clip(jax.random.normal(key_stream, shape, jnp.float32), -5.0, 5.0)
    return (queries.reshape(TOKENS, HEADS * HEAD_SIZE), key_vals.reshape(TOKENS, HEADS * HEAD_SIZE))


def draw_query_rows(key, part):
    return paired_rows(key)[0].astype(jnp.bfloat16)


def draw_key_rows(key, part):
    return paired_rows(key)[1].astype(jnp.bfloat16)


def shuffled(subkey):
    return jax.random.permutation(subkey, TOK_DEV)


def route_head(key):
    groups = TOKENS // TOK_DEV
    per_peer = TOK_DEV // groups
    within = jax.vmap(shuffled)(jax.random.split(jax.random.fold_in(key, 1), groups))
    assign = jax.vmap(shuffled)(jax.random.split(jax.random.fold_in(key, 2), groups))
    target = assign // per_peer
    inside = assign % per_peer
    source = jnp.arange(groups, dtype=jnp.int32)[:, None]
    local_slot = within[target, source * per_peer + inside]
    return (target * TOK_DEV + local_slot).reshape(TOKENS)


def draw_routes(key, part):
    head_keys = jax.random.split(jax.random.fold_in(key, 7), HEADS)
    return jax.vmap(route_head)(head_keys).T.astype(jnp.int32)


def spiked(array, own_key, source, target, parts, factor):
    def block_of(axis_at):
        return (jnp.arange(array.shape[axis_at]) // (array.shape[axis_at] // parts)).reshape((-1,) + (1,) * (array.ndim - 1 - axis_at))

    one_side = jax.random.permutation(own_key, parts)[block_of(target)]
    other_side = (block_of(target) + parts // 2) % parts
    return jnp.where((block_of(source) == one_side) | (block_of(source) == other_side), factor * array, array)


def shard_levels(stream_key, shape, shards, smallest, largest):
    factor_of, own = 1.0, jax.random.fold_in(stream_key, 6)
    for position, blocks in shards:
        heights = jnp.exp(jax.random.uniform(jax.random.fold_in(own, position), (blocks,), jnp.float32, smallest / len(shards), largest / len(shards)))
        factor_of = factor_of * jnp.repeat(heights, shape[position] // blocks).reshape([-1 if axis == position else 1 for axis in range(len(shape))])
    return factor_of


def noise(rng, extent, deviation, most, cuts=(), kind=jnp.bfloat16):
    values = deviation * jax.random.normal(rng, extent, jnp.float32)
    if cuts:
        values = values * shard_levels(rng, extent, cuts, -0.22, 0.18)
    return jnp.clip(values, -most, most).astype(kind)


def gaussian_with(stream_key, extent, deviation, limit, shards, heavy, held_as=jnp.bfloat16):
    drawn = deviation * jax.random.normal(stream_key, extent, jnp.float32)
    if shards:
        drawn = drawn * shard_levels(stream_key, extent, shards, -0.22, 0.18)
    return jnp.clip(spiked(drawn, jax.random.fold_in(stream_key, 3), *heavy), -limit, limit).astype(held_as)


def setup_inputs(seed: int = 0) -> dict:
    seeds = jax.random.split(jax.random.key(seed), 9)
    query_rows = draw_query_rows(jax.random.fold_in(seeds[8], 71), 0)
    key_rows = draw_key_rows(jax.random.fold_in(seeds[8], 71), 0)
    value_rows = noise(seeds[2], (TOKENS, HEADS * HEAD_SIZE), 1.0, 6.0, ((0, 8), (1, 4)))
    query_tan = noise(seeds[3], (TOKENS, HEADS * HEAD_SIZE), 1.0, 6.0, ((0, 8), (1, 4)))
    key_tan = noise(seeds[4], (TOKENS, HEADS * HEAD_SIZE), 1.0, 6.0, ((0, 8), (1, 4)))
    value_tan = noise(seeds[5], (TOKENS, HEADS * HEAD_SIZE), 1.0, 6.0, ((0, 8), (1, 4)))
    routes = draw_routes(jax.random.fold_in(seeds[8], 71), 0)
    out_weight = gaussian_with(seeds[7], (HEADS * HEAD_SIZE, D), (HEADS * HEAD_SIZE) ** -0.5, 0.125, ((0, 4),), (0, 1, 4, 2.0))
    return {"query_rows": query_rows, "key_rows": key_rows, "value_rows": value_rows, "query_tan": query_tan, "key_tan": key_tan, "value_tan": value_tan, "routes": routes, "out_weight": out_weight}


def cluster_attend(query_c, key_c, value_c, query_cluster_gradient, key_cluster_gradient, value_cluster_gradient, where_pos):
    scaling_multiplier = HEAD_SIZE ** -0.5
    query_broadcast_rows = query_c.astype(jnp.float32)
    key_broadcast_rows = key_c.astype(jnp.float32)
    logit_scores = jnp.einsum("ojc,oic->oji", query_broadcast_rows, key_broadcast_rows) * scaling_multiplier
    score_tangent_values = (jnp.einsum("ojc,oic->oji", query_cluster_gradient.astype(jnp.float32), key_broadcast_rows)
                      + jnp.einsum("ojc,oic->oji", query_broadcast_rows, key_cluster_gradient.astype(jnp.float32))) * scaling_multiplier
    visible = where_pos[:, None, :] <= where_pos[:, :, None]
    masked = jnp.where(visible, logit_scores, -jnp.inf)
    top_score = jnp.max(masked, axis=-1, keepdims=True)
    expo = jnp.where(visible, jnp.exp(masked - top_score), 0.0)
    attn_probs = expo / jnp.sum(expo, axis=-1, keepdims=True)
    probs_half = lax.optimization_barrier(attn_probs.astype(jnp.bfloat16))
    value_broadcast_rows = value_c.astype(jnp.float32)
    probability_backward = probs_half.astype(jnp.float32)
    attended_values = jnp.einsum("rtv,rvy->rty", probability_backward, value_broadcast_rows).astype(jnp.bfloat16)
    tangent_probs = attn_probs * (score_tangent_values - jnp.sum(attn_probs * score_tangent_values, axis=-1, keepdims=True))
    tangent_halfway_term = lax.optimization_barrier(tangent_probs.astype(jnp.bfloat16))
    attended_tangent_sum = (jnp.einsum("rtv,rvy->rty", tangent_halfway_term.astype(jnp.float32), value_broadcast_rows)
                    + jnp.einsum("rtv,rvy->rty", probability_backward, value_cluster_gradient.astype(jnp.float32))).astype(jnp.bfloat16)
    return attended_values, attended_tangent_sum


def by_head(matrix):
    return matrix.reshape(TOKENS, HEADS, HEAD_SIZE).transpose(1, 0, 2)


def reference(query_rows, key_rows, value_rows, query_tan, key_tan, value_tan, routes, out_weight):
    stacked = tuple(by_head(matrix) for matrix in (query_rows, key_rows, value_rows, query_tan, key_tan, value_tan))
    clusters = TOKENS // CLUSTER

    def one_head(items):
        head_slots = items[0]
        token_order = jnp.argsort(head_slots).astype(jnp.int32)
        grouped = [matrix[token_order].reshape(clusters, CLUSTER, HEAD_SIZE) for matrix in items[1:]]
        attended_values, attended_tangent_sum = cluster_attend(*grouped, token_order.reshape(clusters, CLUSTER))
        inverse = jnp.argsort(token_order).astype(jnp.int32)
        return (attended_values.reshape(TOKENS, HEAD_SIZE)[inverse],
                attended_tangent_sum.reshape(TOKENS, HEAD_SIZE)[inverse])

    head_out, head_tan = lax.map(one_head, (routes.T,) + stacked)
    attended_values = head_out.transpose(1, 0, 2).reshape(TOKENS, HEADS * HEAD_SIZE)
    attended_tangent_sum = head_tan.transpose(1, 0, 2).reshape(TOKENS, HEADS * HEAD_SIZE)
    output = jnp.dot(attended_values, out_weight, preferred_element_type=jnp.float32).astype(jnp.bfloat16)
    output_tan = jnp.dot(attended_tangent_sum, out_weight, preferred_element_type=jnp.float32).astype(jnp.bfloat16)
    return (output, output_tan)
```

```python
import jax
import jax.numpy as jnp
from jax import lax
from jax.sharding import PartitionSpec as P

HEAD_SIZE = 128


def body(n, query_rows, key_rows, value_rows, query_tan, key_tan, value_tan, routes, out_weight):
    tok_dev, heads = routes.shape
    per = tok_dev // n
    member = (routes // tok_dev)[:, :, None] == jnp.arange(n)
    earlier = jnp.tril(jnp.ones((tok_dev, tok_dev), jnp.bfloat16), -1)
    rank = jnp.einsum(
        "ts,shc->thc", earlier, member.astype(jnp.bfloat16), preferred_element_type=jnp.float32
    )
    place = jnp.sum(jnp.where(member, rank + per * jnp.arange(n, dtype=jnp.float32), 0.0), -1)
    order = (place[:, :, None] == jnp.arange(tok_dev, dtype=jnp.float32)).astype(jnp.bfloat16)
    order = jnp.transpose(order, (1, 0, 2))
    rows = jnp.concatenate(
        [
            m.reshape(tok_dev, heads, HEAD_SIZE)
            for m in (query_tan, query_rows, key_rows, key_tan, value_rows, value_tan)
        ],
        -1,
    )
    sent = jnp.einsum("htp,the->phe", order, rows, preferred_element_type=jnp.float32)
    got = lax.all_to_all(
        sent.astype(jnp.bfloat16), "seq", split_axis=0, concat_axis=0, tiled=True
    )
    e = HEAD_SIZE
    query, key = got[:, :, e : 2 * e], got[:, :, 2 * e : 3 * e]
    value, values = got[:, :, 4 * e : 5 * e], got[:, :, 4 * e :]
    scale = HEAD_SIZE**-0.5
    scores = jnp.einsum("qhe,khe->hqk", query, key, preferred_element_type=jnp.float32) * scale
    tangent = (
        jnp.einsum(
            "qhe,khe->hqk",
            got[:, :, : 2 * e],
            got[:, :, 2 * e : 4 * e],
            preferred_element_type=jnp.float32,
        )
        * scale
    )
    visible = jnp.tril(jnp.ones((tok_dev, tok_dev), bool))
    masked = jnp.where(visible, scores, -jnp.inf)
    expo = jnp.exp(masked - jnp.max(masked, -1, keepdims=True))
    probs = expo / jnp.sum(expo, -1, keepdims=True)
    tangent_probs = probs * (tangent - jnp.sum(probs * tangent, -1, keepdims=True))
    both = jnp.einsum(
        "hqk,khe->qhe", probs.astype(jnp.bfloat16), values, preferred_element_type=jnp.float32
    )
    extra = jnp.einsum(
        "hqk,khe->qhe", tangent_probs.astype(jnp.bfloat16), value, preferred_element_type=jnp.float32
    )
    result = jnp.concatenate([both[:, :, :e], both[:, :, e:] + extra], -1).astype(jnp.bfloat16)
    back = lax.all_to_all(result, "seq", split_axis=0, concat_axis=0, tiled=True)
    home = jnp.einsum("htp,phe->the", order, back, preferred_element_type=jnp.float32)
    home = home.astype(jnp.bfloat16)
    stacked = jnp.concatenate(
        [home[:, :, :e].reshape(tok_dev, -1), home[:, :, e:].reshape(tok_dev, -1)], 0
    )
    partial = jnp.dot(stacked, out_weight, preferred_element_type=jnp.float32)
    total = lax.psum_scatter(
        partial.astype(jnp.bfloat16), "tensor", scatter_dimension=1, tiled=True
    )
    return (total[:tok_dev], total[tok_dev:])


def solution(mesh):
    n = mesh.shape["seq"]
    return jax.shard_map(
        lambda *args: body(n, *args),
        mesh=mesh,
        in_specs=(P("seq", "tensor"),) * 7 + (P("tensor", None),),
        out_specs=(P("seq", "tensor"), P("seq", "tensor")),
        check_vma=False,
    )
```

```python
import functools

import jax
import jax.numpy as jnp
from jax import lax
from jax.experimental import pallas as pl
from jax.experimental.pallas import tpu as pltpu
from jax.sharding import PartitionSpec as P

HEAD_SIZE = 128
MESH = pl.DeviceIdType.MESH


def dot(a, b, contract):
    return lax.dot_general(
        a, b, (((contract[0],), (contract[1],)), ((), ())), preferred_element_type=jnp.float32
    )


def attend(rows):
    e = HEAD_SIZE
    scale = e**-0.5
    count = rows.shape[0]
    query, key = rows[:, e : 2 * e], rows[:, 2 * e : 3 * e]
    scores = dot(query, key, (1, 1)) * scale
    tangent = dot(rows[:, : 2 * e], rows[:, 2 * e : 4 * e], (1, 1)) * scale
    visible = lax.broadcasted_iota(jnp.int32, (count, count), 1) <= lax.broadcasted_iota(
        jnp.int32, (count, count), 0
    )
    masked = jnp.where(visible, scores, -jnp.inf)
    expo = jnp.exp(masked - jnp.max(masked, -1, keepdims=True))
    probs = expo / jnp.sum(expo, -1, keepdims=True)
    slope = probs * (tangent - jnp.sum(probs * tangent, -1, keepdims=True))
    both = dot(probs.astype(jnp.bfloat16), rows[:, 4 * e :], (1, 0))
    extra = dot(slope.astype(jnp.bfloat16), rows[:, 4 * e : 5 * e], (1, 0))
    return jnp.concatenate([both[:, :e], both[:, e:] + extra], 1).astype(jnp.bfloat16)


def kernel(
    n,
    parts,
    q_ref,
    k_ref,
    v_ref,
    dq_ref,
    dk_ref,
    dv_ref,
    routes_ref,
    weight_hbm,
    out_ref,
    tan_ref,
    order,
    sent,
    got,
    result,
    back,
    weight,
    acts,
    own,
    pair_send,
    pair_recv,
    far_send,
    far_recv,
    weight_sem,
    go_send,
    go_recv,
    back_send,
    back_recv,
    pair_sems,
    far_sems,
):
    e = HEAD_SIZE
    tok, width = q_ref.shape
    heads = width // e
    per = tok // n
    groups = parts // 2
    me = lax.axis_index("seq")
    mine = lax.axis_index("tensor")
    group, core = lax.div(mine, 2), lax.rem(mine, 2)
    mate = 2 * group + 1 - core

    barrier = pltpu.get_barrier_semaphore()
    for d in range(1, n):
        pl.semaphore_signal(
            barrier, inc=1, device_id={"seq": lax.rem(me + d, n)}, device_id_type=MESH
        )
    pl.semaphore_signal(barrier, inc=1, device_id={"tensor": mate}, device_id_type=MESH)
    for d in range(1, groups):
        pl.semaphore_signal(
            barrier,
            inc=1,
            device_id={"tensor": 2 * lax.rem(group + d, groups) + core},
            device_id_type=MESH,
        )
    load = pltpu.make_async_copy(weight_hbm, weight, weight_sem)
    load.start()

    row_at = lax.broadcasted_iota(jnp.int32, (tok, tok), 0)
    earlier = (row_at < lax.broadcasted_iota(jnp.int32, (tok, tok), 1)).astype(jnp.float32)
    earlier = earlier.astype(jnp.bfloat16)
    cluster = lax.broadcasted_iota(jnp.int32, (n, tok), 0)

    def place(h, _):
        dest = jnp.right_shift(routes_ref[h], tok.bit_length() - 1)
        member = (dest == cluster).astype(jnp.float32)
        rank = dot(member.astype(jnp.bfloat16), earlier, (1, 0))
        at = jnp.sum(member * (rank + (per * cluster).astype(jnp.float32)), 0, keepdims=True)
        order[h] = (row_at.astype(jnp.float32) == at).astype(jnp.float32).astype(jnp.bfloat16)
        return 0

    lax.fori_loop(0, heads, place, 0)
    pl.semaphore_wait(barrier, n - 1 + groups)

    def go(h, d):
        peer = lax.rem(me + d, n)
        return pltpu.make_async_remote_copy(
            src_ref=sent.at[h, peer],
            dst_ref=got.at[h, me],
            send_sem=go_send.at[h, d],
            recv_sem=go_recv.at[h, d],
            device_id={"seq": peer},
            device_id_type=MESH,
        )

    def come(h, d):
        peer = lax.rem(me + d, n)
        return pltpu.make_async_remote_copy(
            src_ref=result.at[h, peer],
            dst_ref=back.at[h, me],
            send_sem=back_send.at[h, d],
            recv_sem=back_recv.at[h, d],
            device_id={"seq": peer},
            device_id_type=MESH,
        )

    def scatter(h, _):
        cols = pl.ds(pl.multiple_of(h * e, e), e)
        rows = jnp.concatenate(
            [r[:, cols] for r in (dq_ref, q_ref, k_ref, dk_ref, v_ref, dv_ref)], 1
        )
        placed = dot(order[h], rows, (1, 0)).astype(jnp.bfloat16)
        sent[h] = placed.reshape(n, per, 6 * e)
        got[h, me] = sent[h, me]

        def start(d, _):
            go(h, d).start()
            return 0

        lax.fori_loop(1, n, start, 0)
        return 0

    lax.fori_loop(0, heads, scatter, 0)

    def work(h, _):
        def wait(d, _):
            go(h, d).wait()
            return 0

        lax.fori_loop(1, n, wait, 0)
        result[h] = attend(got[h].reshape(tok, 6 * e)).reshape(n, per, 2 * e)
        back[h, me] = result[h, me]

        def start(d, _):
            come(h, d).start()
            return 0

        lax.fori_loop(1, n, start, 0)
        return 0

    lax.fori_loop(0, heads, work, 0)

    def home(h, _):
        def wait(d, _):
            come(h, d).wait()
            return 0

        lax.fori_loop(1, n, wait, 0)
        rows = dot(order[h], back[h].reshape(tok, 2 * e), (0, 0)).astype(jnp.bfloat16)
        cols = pl.ds(pl.multiple_of(h * e, e), e)
        acts[:tok, cols] = rows[:, :e]
        acts[tok:, cols] = rows[:, e:]
        return 0

    lax.fori_loop(0, heads, home, 0)
    load.wait()
    project(groups, group, core, mate, weight, acts, own, pair_send, pair_recv, far_send,
            far_recv, pair_sems, far_sems, out_ref, tan_ref)


def project(groups, group, core, mate, weight, acts, own, pair_send, pair_recv, far_send,
            far_recv, pair_sems, far_sems, out_ref, tan_ref):
    tok, width = out_ref.shape
    tile = min(256, width)

    def product(block, store):
        def step(i, _):
            at = pl.multiple_of(i * tile, tile)
            source = pl.ds(pl.multiple_of(block * width + at, tile), tile)
            store(pl.ds(at, tile), dot(acts[...], weight[:, source], (1, 0)))
            return 0

        lax.fori_loop(0, width // tile, step, 0)

    def to_mate(i):
        return pltpu.make_async_remote_copy(
            src_ref=pair_send.at[i],
            dst_ref=pair_recv.at[i],
            send_sem=pair_sems.at[0, i],
            recv_sem=pair_sems.at[1, i],
            device_id={"tensor": mate},
            device_id_type=MESH,
        )

    def to_far(i):
        return pltpu.make_async_remote_copy(
            src_ref=far_send.at[i],
            dst_ref=far_recv.at[i],
            send_sem=far_sems.at[0, i],
            recv_sem=far_sems.at[1, i],
            device_id={"tensor": 2 * lax.rem(group + 1 + i, groups) + core},
            device_id_type=MESH,
        )

    for i in range(groups):
        there = lax.rem(group + 1 + i, groups)

        def keep_pair(cols, value, i=i):
            pair_send[i, :, cols] = value.astype(jnp.bfloat16)

        product(2 * there + 1 - core, keep_pair)
        to_mate(i).start()

        def keep_own(cols, value, i=i):
            own[i, :, cols] = value

        product(2 * there + core, keep_own)
        if i < groups - 1:
            to_mate(i).wait()
            far_send[i] = (own[i] + pair_recv[i].astype(jnp.float32)).astype(jnp.bfloat16)
            to_far(i).start()
    last = groups - 1
    to_mate(last).wait()
    own[last] = own[last] + pair_recv[last].astype(jnp.float32)
    for i in range(groups - 1):
        to_far(i).wait()
        own[last] = own[last] + far_recv[i].astype(jnp.float32)
    out_ref[...] = own[last, :tok].astype(jnp.bfloat16)
    tan_ref[...] = own[last, tok:].astype(jnp.bfloat16)


def body(n, parts, q, k, v, dq, dk, dv, routes, weight):
    tok, heads = routes.shape
    e = HEAD_SIZE
    per = tok // n
    groups = parts // 2
    width = weight.shape[1] // parts
    half = jnp.bfloat16
    vmem = pl.BlockSpec(memory_space=pltpu.VMEM)
    dma = pltpu.SemaphoreType.DMA
    shape = jax.ShapeDtypeStruct((tok, width), half)
    return pl.pallas_call(
        functools.partial(kernel, n, parts),
        out_shape=(shape, shape),
        in_specs=[vmem] * 7 + [pl.BlockSpec(memory_space=pl.ANY)],
        out_specs=(vmem, vmem),
        scratch_shapes=[
            pltpu.VMEM((heads, tok, tok), half),
            pltpu.VMEM((heads, n, per, 6 * e), half),
            pltpu.VMEM((heads, n, per, 6 * e), half),
            pltpu.VMEM((heads, n, per, 2 * e), half),
            pltpu.VMEM((heads, n, per, 2 * e), half),
            pltpu.VMEM(weight.shape, half),
            pltpu.VMEM((2 * tok, heads * e), half),
            pltpu.VMEM((groups, 2 * tok, width), jnp.float32),
            pltpu.VMEM((groups, 2 * tok, width), half),
            pltpu.VMEM((groups, 2 * tok, width), half),
            pltpu.VMEM((max(groups - 1, 1), 2 * tok, width), half),
            pltpu.VMEM((max(groups - 1, 1), 2 * tok, width), half),
            dma,
            dma((heads, n)),
            dma((heads, n)),
            dma((heads, n)),
            dma((heads, n)),
            dma((2, groups)),
            dma((2, max(groups - 1, 1))),
        ],
        compiler_params=pltpu.CompilerParams(
            collective_id=0, has_side_effects=True, vmem_limit_bytes=56 * 2**20
        ),
    )(q, k, v, dq, dk, dv, routes.T.reshape(heads, 1, tok), weight)


def solution(mesh):
    n, parts = mesh.shape["seq"], mesh.shape["tensor"]
    return jax.shard_map(
        lambda *args: body(n, parts, *args),
        mesh=mesh,
        in_specs=(P("seq", "tensor"),) * 7 + (P("tensor", None),),
        out_specs=(P("seq", "tensor"), P("seq", "tensor")),
        check_vma=False,
    )
```

```python
import functools

import jax
import jax.numpy as jnp
from jax import lax
from jax.experimental import pallas as pl
from jax.experimental.pallas import tpu as pltpu
from jax.sharding import PartitionSpec as P

HEAD_SIZE = 128
MESH = pl.DeviceIdType.MESH


def dot(a, b, contract):
    return lax.dot_general(
        a, b, (((contract[0],), (contract[1],)), ((), ())), preferred_element_type=jnp.float32
    )


def attend(rows):
    e = HEAD_SIZE
    scale = e**-0.5
    count = rows.shape[0]
    query, key = rows[:, e : 2 * e], rows[:, 2 * e : 3 * e]
    scores = dot(query, key, (1, 1)) * scale
    tangent = dot(rows[:, : 2 * e], rows[:, 2 * e : 4 * e], (1, 1)) * scale
    visible = lax.broadcasted_iota(jnp.int32, (count, count), 1) <= lax.broadcasted_iota(
        jnp.int32, (count, count), 0
    )
    masked = jnp.where(visible, scores, -jnp.inf)
    expo = jnp.exp(masked - jnp.max(masked, -1, keepdims=True))
    probs = expo / jnp.sum(expo, -1, keepdims=True)
    slope = probs * (tangent - jnp.sum(probs * tangent, -1, keepdims=True))
    both = dot(probs.astype(jnp.bfloat16), rows[:, 4 * e :], (1, 0))
    extra = dot(slope.astype(jnp.bfloat16), rows[:, 4 * e : 5 * e], (1, 0))
    return jnp.concatenate([both[:, :e], both[:, e:] + extra], 1).astype(jnp.bfloat16)


def kernel(
    n,
    parts,
    q_ref,
    k_ref,
    v_ref,
    dq_ref,
    dk_ref,
    dv_ref,
    routes_ref,
    weight_hbm,
    out_ref,
    tan_ref,
    order,
    sent,
    got,
    result,
    back,
    weight,
    acts,
    own,
    pair_send,
    pair_recv,
    far_send,
    far_recv,
    weight_sem,
    go_send,
    go_recv,
    back_send,
    back_recv,
    pair_sems,
    far_sems,
):
    e = HEAD_SIZE
    tok, width = q_ref.shape
    heads = width // e
    per = tok // n
    groups = parts // 2
    me = lax.axis_index("seq")
    mine = lax.axis_index("tensor")
    group, core = lax.div(mine, 2), lax.rem(mine, 2)
    mate = 2 * group + 1 - core

    barrier = pltpu.get_barrier_semaphore()
    for d in range(1, n):
        pl.semaphore_signal(
            barrier, inc=1, device_id={"seq": lax.rem(me + d, n)}, device_id_type=MESH
        )
    pl.semaphore_signal(barrier, inc=1, device_id={"tensor": mate}, device_id_type=MESH)
    for d in range(1, groups):
        pl.semaphore_signal(
            barrier,
            inc=1,
            device_id={"tensor": 2 * lax.rem(group + d, groups) + core},
            device_id_type=MESH,
        )
    load = pltpu.make_async_copy(weight_hbm, weight, weight_sem)
    load.start()

    row_at = lax.broadcasted_iota(jnp.int32, (tok, tok), 0)
    earlier = (row_at < lax.broadcasted_iota(jnp.int32, (tok, tok), 1)).astype(jnp.float32)
    earlier = earlier.astype(jnp.bfloat16)
    cluster = lax.broadcasted_iota(jnp.int32, (n, tok), 0)

    def place(h, _):
        dest = jnp.right_shift(routes_ref[h], tok.bit_length() - 1)
        member = (dest == cluster).astype(jnp.float32)
        rank = dot(member.astype(jnp.bfloat16), earlier, (1, 0))
        at = jnp.sum(member * (rank + (per * cluster).astype(jnp.float32)), 0, keepdims=True)
        order[h] = (row_at.astype(jnp.float32) == at).astype(jnp.float32).astype(jnp.bfloat16)
        return 0

    lax.fori_loop(0, heads, place, 0)
    pl.semaphore_wait(barrier, n - 1 + groups)

    def go(h, d):
        peer = lax.rem(me + d, n)
        return pltpu.make_async_remote_copy(
            src_ref=sent.at[h, peer],
            dst_ref=got.at[h, me],
            send_sem=go_send.at[h, d],
            recv_sem=go_recv.at[h, d],
            device_id={"seq": peer},
            device_id_type=MESH,
        )

    def come(h, d):
        peer = lax.rem(me + d, n)
        return pltpu.make_async_remote_copy(
            src_ref=result.at[h, peer],
            dst_ref=back.at[h, me],
            send_sem=back_send.at[h, d],
            recv_sem=back_recv.at[h, d],
            device_id={"seq": peer},
            device_id_type=MESH,
        )

    def scatter(h, _):
        cols = pl.ds(pl.multiple_of(h * e, e), e)
        rows = jnp.concatenate(
            [r[:, cols] for r in (dq_ref, q_ref, k_ref, dk_ref, v_ref, dv_ref)], 1
        )
        placed = dot(order[h], rows, (1, 0)).astype(jnp.bfloat16)
        sent[h] = placed.reshape(n, per, 6 * e)
        got[h, me] = sent[h, me]

        def start(d, _):
            go(h, d).start()
            return 0

        lax.fori_loop(1, n, start, 0)
        return 0

    lax.fori_loop(0, heads, scatter, 0)

    def work(h, _):
        def wait(d, _):
            go(h, d).wait()
            return 0

        lax.fori_loop(1, n, wait, 0)
        result[h] = attend(got[h].reshape(tok, 6 * e)).reshape(n, per, 2 * e)
        back[h, me] = result[h, me]

        def start(d, _):
            come(h, d).start()
            return 0

        lax.fori_loop(1, n, start, 0)
        return 0

    lax.fori_loop(0, heads, work, 0)

    def home(h, _):
        def wait(d, _):
            come(h, d).wait()
            return 0

        lax.fori_loop(1, n, wait, 0)
        rows = dot(order[h], back[h].reshape(tok, 2 * e), (0, 0)).astype(jnp.bfloat16)
        cols = pl.ds(pl.multiple_of(h * e, e), e)
        acts[:tok, cols] = rows[:, :e]
        acts[tok:, cols] = rows[:, e:]
        return 0

    lax.fori_loop(0, heads, home, 0)
    load.wait()
    project(groups, group, core, mate, weight, acts, own, pair_send, pair_recv, far_send,
            far_recv, pair_sems, far_sems, out_ref, tan_ref)


def project(groups, group, core, mate, weight, acts, own, pair_send, pair_recv, far_send,
            far_recv, pair_sems, far_sems, out_ref, tan_ref):
    tok, width = out_ref.shape
    tile = min(256, width)

    def product(block, store):
        def step(i, _):
            at = pl.multiple_of(i * tile, tile)
            source = pl.ds(pl.multiple_of(block * width + at, tile), tile)
            store(pl.ds(at, tile), dot(acts[...], weight[:, source], (1, 0)))
            return 0

        lax.fori_loop(0, width // tile, step, 0)

    def to_mate(i):
        return pltpu.make_async_remote_copy(
            src_ref=pair_send.at[i],
            dst_ref=pair_recv.at[i],
            send_sem=pair_sems.at[0, i],
            recv_sem=pair_sems.at[1, i],
            device_id={"tensor": mate},
            device_id_type=MESH,
        )

    def to_far(i):
        return pltpu.make_async_remote_copy(
            src_ref=far_send.at[i],
            dst_ref=far_recv.at[i],
            send_sem=far_sems.at[0, i],
            recv_sem=far_sems.at[1, i],
            device_id={"tensor": 2 * lax.rem(group + 1 + i, groups) + core},
            device_id_type=MESH,
        )

    for i in range(groups):
        there = lax.rem(group + 1 + i, groups)

        def keep_pair(cols, value, i=i):
            pair_send[i, :, cols] = value.astype(jnp.bfloat16)

        product(2 * there + 1 - core, keep_pair)
        to_mate(i).start()

        def keep_own(cols, value, i=i):
            own[i, :, cols] = value

        product(2 * there + core, keep_own)
        if i < groups - 1:
            to_mate(i).wait()
            far_send[i] = (own[i] + pair_recv[i].astype(jnp.float32)).astype(jnp.bfloat16)
            to_far(i).start()
    last = groups - 1
    to_mate(last).wait()
    own[last] = own[last] + pair_recv[last].astype(jnp.float32)
    for i in range(groups - 1):
        to_far(i).wait()
        own[last] = own[last] + far_recv[i].astype(jnp.float32)
    out_ref[...] = own[last, :tok].astype(jnp.bfloat16)
    tan_ref[...] = own[last, tok:].astype(jnp.bfloat16)


def body(n, parts, q, k, v, dq, dk, dv, routes, weight):
    tok, heads = routes.shape
    e = HEAD_SIZE
    per = tok // n
    groups = parts // 2
    width = weight.shape[1] // parts
    half = jnp.bfloat16
    vmem = pl.BlockSpec(memory_space=pltpu.VMEM)
    dma = pltpu.SemaphoreType.DMA
    shape = jax.ShapeDtypeStruct((tok, width), half)
    return pl.pallas_call(
        functools.partial(kernel, n, parts),
        out_shape=(shape, shape),
        in_specs=[vmem] * 7 + [pl.BlockSpec(memory_space=pl.ANY)],
        out_specs=(vmem, vmem),
        scratch_shapes=[
            pltpu.VMEM((heads, tok, tok), half),
            pltpu.VMEM((heads, n, per, 6 * e), half),
            pltpu.VMEM((heads, n, per, 6 * e), half),
            pltpu.VMEM((heads, n, per, 2 * e), half),
            pltpu.VMEM((heads, n, per, 2 * e), half),
            pltpu.VMEM(weight.shape, half),
            pltpu.VMEM((2 * tok, heads * e), half),
            pltpu.VMEM((groups, 2 * tok, width), jnp.float32),
            pltpu.VMEM((groups, 2 * tok, width), half),
            pltpu.VMEM((groups, 2 * tok, width), half),
            pltpu.VMEM((max(groups - 1, 1), 2 * tok, width), half),
            pltpu.VMEM((max(groups - 1, 1), 2 * tok, width), half),
            dma,
            dma((heads, n)),
            dma((heads, n)),
            dma((heads, n)),
            dma((heads, n)),
            dma((2, groups)),
            dma((2, max(groups - 1, 1))),
        ],
        compiler_params=pltpu.CompilerParams(
            collective_id=0, has_side_effects=True, vmem_limit_bytes=56 * 2**20
        ),
    )(q, k, v, dq, dk, dv, routes.T.reshape(heads, 1, tok), weight)


LEVELS = 4


def soft_rows(query, keys, offset):
    e = HEAD_SIZE
    scale = e**-0.5
    shape = (query.shape[0], keys.shape[0])
    scores = dot(query[:, e:], keys[:, :e], (1, 1)) * scale
    tangent = dot(query, keys[:, : 2 * e], (1, 1)) * scale
    visible = (
        lax.broadcasted_iota(jnp.int32, shape, 1)
        <= lax.broadcasted_iota(jnp.int32, shape, 0) + offset
    )
    masked = jnp.where(visible, scores, -jnp.inf)
    top = jnp.max(masked, -1, keepdims=True)
    expo = jnp.exp(masked - top)
    total = jnp.sum(expo, -1, keepdims=True)
    probs = expo / total
    mean = jnp.sum(probs * tangent, -1, keepdims=True)
    slope = probs * (tangent - mean)
    both = dot(probs.astype(jnp.bfloat16), keys[:, 2 * e :], (1, 0))
    extra = dot(slope.astype(jnp.bfloat16), keys[:, 2 * e : 3 * e], (1, 0))
    rows = jnp.concatenate([both[:, :e], both[:, e:] + extra], 1)
    return rows, top + jnp.log(total), mean


def pack_stats(level, mean):
    lane = lax.broadcasted_iota(jnp.int32, (level.shape[0], 128), 1)
    return jnp.where(lane == 0, level, jnp.where(lane == 1, mean, 0.0))


def merge(pieces):
    e = HEAD_SIZE
    top = functools.reduce(jnp.maximum, [level for _, level, _ in pieces])
    weights = [jnp.exp(level - top) for _, level, _ in pieces]
    total = functools.reduce(jnp.add, weights)
    weights = [w / total for w in weights]
    mean = sum(w * m for w, (_, _, m) in zip(weights, pieces))
    value = sum(w * rows[:, :e] for w, (rows, _, _) in zip(weights, pieces))
    slope = sum(
        w * (rows[:, e:] + (m - mean) * rows[:, :e]) for w, (rows, _, m) in zip(weights, pieces)
    )
    return jnp.concatenate([value, slope], 1)


def level_kernel(
    parts,
    q_ref,
    k_ref,
    v_ref,
    dq_ref,
    dk_ref,
    dv_ref,
    routes_ref,
    weight_hbm,
    out_ref,
    tan_ref,
    order,
    sent,
    rows_here,
    keys_in,
    query_in,
    piece_out,
    piece_in,
    stats_out,
    stats_in,
    own_piece,
    own_stats,
    result,
    back,
    weight,
    acts,
    own,
    pair_send,
    pair_recv,
    far_send,
    far_recv,
    weight_sem,
    side_sems,
    key_sems,
    query_sems,
    piece_sems,
    stats_sems,
    back_sems,
    pair_sems,
    far_sems,
):
    e = HEAD_SIZE
    tok, width = q_ref.shape
    heads = width // e
    n = 2 * LEVELS
    per = tok // n
    here = heads // 2
    steps = 2 * here
    some = n // 2
    groups = parts // 2
    me = lax.axis_index("seq")
    mine = lax.axis_index("tensor")
    level, side = lax.div(me, 2), lax.rem(me, 2)
    group, core = lax.div(mine, 2), lax.rem(mine, 2)
    mate = 2 * group + 1 - core

    barrier = pltpu.get_barrier_semaphore()
    for d in range(1, LEVELS):
        peer = 2 * lax.rem(level + d, LEVELS) + side
        pl.semaphore_signal(barrier, inc=1, device_id={"seq": peer}, device_id_type=MESH)
    pl.semaphore_signal(
        barrier, inc=1, device_id={"seq": 2 * level + 1 - side}, device_id_type=MESH
    )
    pl.semaphore_signal(barrier, inc=1, device_id={"tensor": mate}, device_id_type=MESH)
    for d in range(1, groups):
        pl.semaphore_signal(
            barrier,
            inc=1,
            device_id={"tensor": 2 * lax.rem(group + d, groups) + core},
            device_id_type=MESH,
        )
    load = pltpu.make_async_copy(weight_hbm, weight, weight_sem)
    load.start()

    row_at = lax.broadcasted_iota(jnp.int32, (tok, tok), 0)
    earlier = (row_at < lax.broadcasted_iota(jnp.int32, (tok, tok), 1)).astype(jnp.float32)
    earlier = earlier.astype(jnp.bfloat16)
    cluster = lax.broadcasted_iota(jnp.int32, (n, tok), 0)

    def place(h, _):
        dest = jnp.right_shift(routes_ref[h], tok.bit_length() - 1)
        member = (dest == cluster).astype(jnp.float32)
        rank = dot(member.astype(jnp.bfloat16), earlier, (1, 0))
        at = jnp.sum(member * (rank + (per * cluster).astype(jnp.float32)), 0, keepdims=True)
        order[h] = (row_at.astype(jnp.float32) == at).astype(jnp.float32).astype(jnp.bfloat16)
        return 0

    lax.fori_loop(0, heads, place, 0)
    pl.semaphore_wait(barrier, LEVELS + groups)

    def remote(src, dst, sems, at, device):
        return pltpu.make_async_remote_copy(
            src_ref=src,
            dst_ref=dst,
            send_sem=sems.at[(0, *at)],
            recv_sem=sems.at[(1, *at)],
            device_id=device,
            device_id_type=MESH,
        )

    across = {"seq": 2 * level + 1 - side}

    def at_level(z):
        return {"seq": 2 * z + side}

    def side_copy(c):
        return remote(sent.at[c], rows_here.at[c, side], side_sems, (c,), across)

    def key_copy(c):
        keys = rows_here.at[c, :, :, :, pl.ds(2 * e, 4 * e)]
        return remote(keys, keys_in.at[c], key_sems, (c,), at_level(1))

    def query_copy(slot, c, z):
        queries = rows_here.at[c, :, :, :, pl.ds(0, 2 * e)]
        return remote(queries, query_in.at[slot, c], query_sems, (slot, c), at_level(z))

    def piece_copies(slot, c, z):
        return (
            remote(piece_out.at[slot, c], piece_in.at[slot, c], piece_sems, (slot, c), at_level(z)),
            remote(stats_out.at[slot, c], stats_in.at[slot, c], stats_sems, (slot, c), at_level(z)),
        )

    def back_copy(c):
        return remote(result.at[c, 1 - side], back.at[c], back_sems, (c,), across)

    def placed(h, c):
        cols = pl.ds(pl.multiple_of(h * e, e), e)
        rows = jnp.concatenate(
            [r[:, cols] for r in (dq_ref, q_ref, k_ref, dk_ref, v_ref, dv_ref)], 1
        )
        half = pl.ds(pl.multiple_of(lax.rem(c, 2) * (tok // 2), tok // 2), tok // 2)
        moved = dot(order[h, half, :], rows, (1, 0)).astype(jnp.bfloat16)
        return moved.reshape(some, per, 6 * e)

    def scatter(c, _):
        sent[c] = placed((1 - side) * here + lax.div(c, 2), c)
        side_copy(c).start()
        return 0

    lax.fori_loop(0, steps, scatter, 0)

    def pair_of(ref, i):
        return jnp.concatenate([ref[0, i], ref[1, i]], 0)

    def finish(c, i, rows):
        rows = rows.astype(jnp.bfloat16)
        result[c, 0, i] = rows[:per]
        result[c, 1, i] = rows[per:]

    def hand_on(slot, c, z, parts_of):
        for i, (rows, _, _) in enumerate(parts_of):
            piece_out[slot, c, i] = rows.astype(jnp.bfloat16)
        packed = pack_stats(
            jnp.concatenate([p[1] for p in parts_of], 0),
            jnp.concatenate([p[2] for p in parts_of], 0),
        )
        stats_out[slot, c] = packed.T[:8]
        for copy in piece_copies(slot, c, z):
            copy.start()

    def keep(c, parts_of):
        own_piece[c] = jnp.concatenate([p[0] for p in parts_of], 0)
        own_stats[c] = pack_stats(
            jnp.concatenate([p[1] for p in parts_of], 0),
            jnp.concatenate([p[2] for p in parts_of], 0),
        )

    def advance(c):
        rows_here[c, side] = placed(side * here + lax.div(c, 2), c)
        side_copy(c).wait_recv()

        @pl.when(level == 0)
        def _():
            key_copy(c).start()

        @pl.when(level == 2)
        def _():
            query_copy(0, c, 1).start()

        @pl.when(level == 3)
        def _():
            query_copy(0, c, 2).start()
            query_copy(1, c, 1).start()

    def work(c):
        own_rows = rows_here.at[c]
        size = 2 * per

        def cut(piece, j):
            return tuple(x[j * size : (j + 1) * size] for x in piece)

        @pl.when(level == 0)
        def _():
            for i in range(some):
                rows = pair_of(own_rows, i)
                finish(c, i, soft_rows(rows[:, : 2 * e], rows[:, 2 * e :], 0)[0])
            back_copy(c).start()

        @pl.when(level == 1)
        def _():
            key_copy(c).wait_recv()
            query_copy(0, c, 1).wait_recv()
            query_copy(1, c, 1).wait_recv()
            pieces = []
            for i in range(some):
                rows = pair_of(own_rows, i)
                queries = jnp.concatenate(
                    [
                        rows[:, : 2 * e],
                        pair_of(query_in.at[0, c], i),
                        pair_of(query_in.at[1, c], i),
                    ],
                    0,
                )
                keys = jnp.concatenate([pair_of(keys_in.at[c], i), rows[:, 2 * e :]], 0)
                pieces.append(soft_rows(queries, keys, size))
            hand_on(1, c, 3, [cut(p, 2) for p in pieces])
            hand_on(0, c, 2, [cut(p, 1) for p in pieces])
            for i in range(some):
                finish(c, i, pieces[i][0][:size])
            back_copy(c).start()

        @pl.when(level == 2)
        def _():
            query_copy(0, c, 1).wait_recv()
            pieces = []
            for i in range(some):
                rows = pair_of(own_rows, i)
                queries = jnp.concatenate([rows[:, : 2 * e], pair_of(query_in.at[0, c], i)], 0)
                pieces.append(soft_rows(queries, rows[:, 2 * e :], 0))
            hand_on(0, c, 3, [cut(p, 1) for p in pieces])
            keep(c, [cut(p, 0) for p in pieces])

        @pl.when(level == 3)
        def _():
            pieces = []
            for i in range(some):
                rows = pair_of(own_rows, i)
                pieces.append(soft_rows(rows[:, : 2 * e], rows[:, 2 * e :], 0))
            keep(c, pieces)

    ahead = min(2, steps)
    for c in range(ahead):
        advance(c)

    def turn(c, _):
        @pl.when(c + ahead < steps)
        def _():
            advance(c + ahead)

        work(c)
        return 0

    lax.fori_loop(0, steps, turn, 0)

    def gather(c, slots):
        pieces = [(own_piece[c], own_stats[c, :, 0:1], own_stats[c, :, 1:2])]
        for slot in slots:
            for copy in piece_copies(slot, c, 2):
                copy.wait_recv()
            stats = stats_in[slot, c]
            stats = jnp.concatenate([stats, jnp.zeros((120, stats.shape[1]), jnp.float32)], 0).T
            rows = piece_in[slot, c].reshape(some * 2 * per, 2 * e).astype(jnp.float32)
            pieces.append((rows, stats[:, 0:1], stats[:, 1:2]))
        rows = merge(pieces)
        for i in range(some):
            finish(c, i, rows[i * 2 * per : (i + 1) * 2 * per])
        back_copy(c).start()

    @pl.when(level == 2)
    def _():
        lax.fori_loop(0, steps, lambda c, _: (gather(c, (0,)), 0)[1], 0)

    @pl.when(level == 3)
    def _():
        lax.fori_loop(0, steps, lambda c, _: (gather(c, (0, 1)), 0)[1], 0)

    def to_acts(h, rows):
        rows = dot(order[h], rows, (0, 0)).astype(jnp.bfloat16)
        cols = pl.ds(pl.multiple_of(h * e, e), e)
        acts[:tok, cols] = rows[:, :e]
        acts[tok:, cols] = rows[:, e:]

    def both_halves(first, second):
        return jnp.concatenate([first.reshape(tok // 2, 2 * e), second.reshape(tok // 2, 2 * e)], 0)

    def home(j, _):
        to_acts(side * here + j, both_halves(result[2 * j, side], result[2 * j + 1, side]))
        back_copy(2 * j).wait_recv()
        back_copy(2 * j + 1).wait_recv()
        to_acts((1 - side) * here + j, both_halves(back[2 * j], back[2 * j + 1]))
        return 0

    lax.fori_loop(0, here, home, 0)
    load.wait()
    project(groups, group, core, mate, weight, acts, own, pair_send, pair_recv, far_send,
            far_recv, pair_sems, far_sems, out_ref, tan_ref)

    def drain(c, _):
        side_copy(c).wait_send()
        back_copy(c).wait_send()

        @pl.when(level == 0)
        def _():
            key_copy(c).wait_send()

        @pl.when(level == 1)
        def _():
            for slot in (0, 1):
                for copy in piece_copies(slot, c, 2 + slot):
                    copy.wait_send()

        @pl.when(level == 2)
        def _():
            query_copy(0, c, 1).wait_send()
            for copy in piece_copies(0, c, 3):
                copy.wait_send()

        @pl.when(level == 3)
        def _():
            query_copy(0, c, 2).wait_send()
            query_copy(1, c, 1).wait_send()

        return 0

    lax.fori_loop(0, steps, drain, 0)


def level_body(parts, q, k, v, dq, dk, dv, routes, weight):
    tok, heads = routes.shape
    e = HEAD_SIZE
    n = 2 * LEVELS
    per = tok // n
    steps = heads
    some = n // 2
    rows = some * 2 * per
    groups = parts // 2
    width = weight.shape[1] // parts
    half = jnp.bfloat16
    vmem = pl.BlockSpec(memory_space=pltpu.VMEM)
    dma = pltpu.SemaphoreType.DMA
    shape = jax.ShapeDtypeStruct((tok, width), half)
    return pl.pallas_call(
        functools.partial(level_kernel, parts),
        out_shape=(shape, shape),
        in_specs=[vmem] * 7 + [pl.BlockSpec(memory_space=pl.ANY)],
        out_specs=(vmem, vmem),
        scratch_shapes=[
            pltpu.VMEM((heads, tok, tok), half),
            pltpu.VMEM((steps, some, per, 6 * e), half),
            pltpu.VMEM((steps, 2, some, per, 6 * e), half),
            pltpu.VMEM((steps, 2, some, per, 4 * e), half),
            pltpu.VMEM((2, steps, 2, some, per, 2 * e), half),
            pltpu.VMEM((2, steps, some, 2 * per, 2 * e), half),
            pltpu.VMEM((2, steps, some, 2 * per, 2 * e), half),
            pltpu.VMEM((2, steps, 8, rows), jnp.float32),
            pltpu.VMEM((2, steps, 8, rows), jnp.float32),
            pltpu.VMEM((steps, rows, 2 * e), jnp.float32),
            pltpu.VMEM((steps, rows, 128), jnp.float32),
            pltpu.VMEM((steps, 2, some, per, 2 * e), half),
            pltpu.VMEM((steps, some, per, 2 * e), half),
            pltpu.VMEM(weight.shape, half),
            pltpu.VMEM((2 * tok, heads * e), half),
            pltpu.VMEM((groups, 2 * tok, width), jnp.float32),
            pltpu.VMEM((groups, 2 * tok, width), half),
            pltpu.VMEM((groups, 2 * tok, width), half),
            pltpu.VMEM((max(groups - 1, 1), 2 * tok, width), half),
            pltpu.VMEM((max(groups - 1, 1), 2 * tok, width), half),
            dma,
            dma((2, steps)),
            dma((2, steps)),
            dma((2, 2, steps)),
            dma((2, 2, steps)),
            dma((2, 2, steps)),
            dma((2, steps)),
            dma((2, groups)),
            dma((2, max(groups - 1, 1))),
        ],
        compiler_params=pltpu.CompilerParams(
            collective_id=1, has_side_effects=True, vmem_limit_bytes=58 * 2**20
        ),
    )(q, k, v, dq, dk, dv, routes.T.reshape(heads, 1, tok), weight)


def solution(mesh):
    n, parts = mesh.shape["seq"], mesh.shape["tensor"]

    def run(*args):
        if n == 2 * LEVELS and args[6].shape[1] % 2 == 0:
            return level_body(parts, *args)
        return body(n, parts, *args)

    return jax.shard_map(
        run,
        mesh=mesh,
        in_specs=(P("seq", "tensor"),) * 7 + (P("tensor", None),),
        out_specs=(P("seq", "tensor"), P("seq", "tensor")),
        check_vma=False,
    )
```

```python
import functools

import jax
import jax.numpy as jnp
from jax import lax
from jax.experimental import pallas as pl
from jax.experimental.pallas import tpu as pltpu
from jax.sharding import PartitionSpec as P

HEAD_SIZE = 128
MESH = pl.DeviceIdType.MESH
HALVES = 2


def dot(a, b, contract):
    return lax.dot_general(
        a, b, (((contract[0],), (contract[1],)), ((), ())), preferred_element_type=jnp.float32
    )


def attend(rows):
    e = HEAD_SIZE
    scale = e**-0.5
    count = rows.shape[0]
    query, key = rows[:, e : 2 * e], rows[:, 2 * e : 3 * e]
    scores = dot(query, key, (1, 1)) * scale
    tangent = dot(rows[:, : 2 * e], rows[:, 2 * e : 4 * e], (1, 1)) * scale
    visible = lax.broadcasted_iota(jnp.int32, (count, count), 1) <= lax.broadcasted_iota(
        jnp.int32, (count, count), 0
    )
    masked = jnp.where(visible, scores, -jnp.inf)
    expo = jnp.exp(masked - jnp.max(masked, -1, keepdims=True))
    probs = expo / jnp.sum(expo, -1, keepdims=True)
    slope = probs * (tangent - jnp.sum(probs * tangent, -1, keepdims=True))
    both = dot(probs.astype(jnp.bfloat16), rows[:, 4 * e :], (1, 0))
    extra = dot(slope.astype(jnp.bfloat16), rows[:, 4 * e : 5 * e], (1, 0))
    return jnp.concatenate([both[:, :e], both[:, e:] + extra], 1).astype(jnp.bfloat16)


def kernel(
    n,
    parts,
    q_ref,
    k_ref,
    v_ref,
    dq_ref,
    dk_ref,
    dv_ref,
    routes_ref,
    weight_hbm,
    out_ref,
    dest,
    order,
    sent,
    got,
    result,
    back,
    weight,
    acts,
    own,
    pair_send,
    pair_recv,
    far_send,
    far_recv,
    weight_sem,
    go_send,
    go_recv,
    back_send,
    back_recv,
    pair_sems,
    far_sems,
):
    e = HEAD_SIZE
    tok, width = q_ref.shape
    heads = width // e
    per = tok // n
    groups = parts // 2
    me = lax.axis_index("seq")
    mine = lax.axis_index("tensor")
    group, core = lax.div(mine, 2), lax.rem(mine, 2)
    mate = 2 * group + 1 - core

    barrier = pltpu.get_barrier_semaphore()
    for d in range(1, n):
        pl.semaphore_signal(
            barrier, inc=1, device_id={"seq": lax.rem(me + d, n)}, device_id_type=MESH
        )
    pl.semaphore_signal(barrier, inc=1, device_id={"tensor": mate}, device_id_type=MESH)
    for d in range(1, groups):
        pl.semaphore_signal(
            barrier,
            inc=1,
            device_id={"tensor": 2 * lax.rem(group + d, groups) + core},
            device_id_type=MESH,
        )
    load = pltpu.make_async_copy(weight_hbm, weight, weight_sem)
    load.start()

    row_at = lax.broadcasted_iota(jnp.int32, (tok, tok), 0)
    earlier = (row_at < lax.broadcasted_iota(jnp.int32, (tok, tok), 1)).astype(jnp.float32)
    earlier = earlier.astype(jnp.bfloat16)
    cluster = lax.broadcasted_iota(jnp.int32, (n, tok), 0)
    owner = jnp.right_shift(routes_ref[...], tok.bit_length() - 1).astype(jnp.float32)
    same = (row_at == lax.broadcasted_iota(jnp.int32, (tok, tok), 1)).astype(jnp.float32)
    dest[...] = dot(owner.astype(jnp.bfloat16), same.astype(jnp.bfloat16), (0, 0))

    def place(h, _):
        member = (dest[pl.ds(h, 1), :] == cluster.astype(jnp.float32)).astype(jnp.float32)
        rank = dot(member.astype(jnp.bfloat16), earlier, (1, 0))
        at = jnp.sum(member * (rank + (per * cluster).astype(jnp.float32)), 0, keepdims=True)
        order[h] = (row_at.astype(jnp.float32) == at).astype(jnp.float32).astype(jnp.bfloat16)
        return 0

    lax.fori_loop(0, heads, place, 0)
    pl.semaphore_wait(barrier, n - 1 + groups)

    def go(h, d):
        peer = lax.rem(me + d, n)
        return pltpu.make_async_remote_copy(
            src_ref=sent.at[h, peer],
            dst_ref=got.at[h, me],
            send_sem=go_send.at[h, d],
            recv_sem=go_recv.at[h, d],
            device_id={"seq": peer},
            device_id_type=MESH,
        )

    def come(h, d):
        peer = lax.rem(me + d, n)
        return pltpu.make_async_remote_copy(
            src_ref=result.at[h, peer],
            dst_ref=back.at[h, me],
            send_sem=back_send.at[h, d],
            recv_sem=back_recv.at[h, d],
            device_id={"seq": peer},
            device_id_type=MESH,
        )

    def scatter(h, _):
        cols = pl.ds(pl.multiple_of(h * e, e), e)
        rows = jnp.concatenate(
            [r[:, cols] for r in (dq_ref, q_ref, k_ref, dk_ref, v_ref, dv_ref)], 1
        )
        placed = dot(order[h], rows, (1, 0)).astype(jnp.bfloat16)
        sent[h] = placed.reshape(n, per, 6 * e)
        got[h, me] = sent[h, me]

        def start(d, _):
            go(h, d).start()
            return 0

        lax.fori_loop(1, n, start, 0)
        return 0

    lax.fori_loop(0, heads, scatter, 0)

    def work(h, _):
        def wait(d, _):
            go(h, d).wait()
            return 0

        lax.fori_loop(1, n, wait, 0)
        result[h] = attend(got[h].reshape(tok, 6 * e)).reshape(n, per, 2 * e)
        back[h, me] = result[h, me]

        def start(d, _):
            come(h, d).start()
            return 0

        lax.fori_loop(1, n, start, 0)
        return 0

    lax.fori_loop(0, heads, work, 0)

    def home(h, _):
        def wait(d, _):
            come(h, d).wait()
            return 0

        lax.fori_loop(1, n, wait, 0)
        rows = dot(order[h], back[h].reshape(tok, 2 * e), (0, 0)).astype(jnp.bfloat16)
        cols = pl.ds(pl.multiple_of(h * e, e), e)
        acts[:tok, cols] = rows[:, :e]
        acts[tok:, cols] = rows[:, e:]
        return 0

    lax.fori_loop(0, heads, home, 0)
    load.wait()
    project(groups, group, core, mate, weight, acts, own, pair_send, pair_recv, far_send,
            far_recv, pair_sems, far_sems, out_ref)


def project(groups, group, core, mate, weight, acts, own, pair_send, pair_recv, far_send,
            far_recv, pair_sems, far_sems, out_ref):
    wide = out_ref.shape[1] // HALVES
    tile = min(256, wide)

    def product(block, half, store):
        def step(i, _):
            at = pl.multiple_of(i * tile, tile)
            first = (block * HALVES + half) * wide
            source = pl.ds(pl.multiple_of(first + at, tile), tile)
            store(pl.ds(at, tile), dot(acts[...], weight[:, source], (1, 0)))
            return 0

        lax.fori_loop(0, wide // tile, step, 0)

    def to_mate(i, k):
        return pltpu.make_async_remote_copy(
            src_ref=pair_send.at[i, k],
            dst_ref=pair_recv.at[i, k],
            send_sem=pair_sems.at[0, i, k],
            recv_sem=pair_sems.at[1, i, k],
            device_id={"tensor": mate},
            device_id_type=MESH,
        )

    def to_far(i, k):
        return pltpu.make_async_remote_copy(
            src_ref=far_send.at[i, k],
            dst_ref=far_recv.at[i, k],
            send_sem=far_sems.at[0, i, k],
            recv_sem=far_sems.at[1, i, k],
            device_id={"tensor": 2 * lax.rem(group + 1 + i, groups) + core},
            device_id_type=MESH,
        )

    last = groups - 1
    for i in range(groups):
        there = lax.rem(group + 1 + i, groups)
        for k in range(HALVES):

            def keep_pair(cols, value, i=i, k=k):
                pair_send[i, k, :, cols] = value.astype(jnp.bfloat16)

            product(2 * there + 1 - core, k, keep_pair)
            to_mate(i, k).start()
        for k in range(HALVES):

            def keep_own(cols, value, i=i, k=k):
                own[i, k, :, cols] = value

            product(2 * there + core, k, keep_own)
            if i < last:
                to_mate(i, k).wait()
                total = own[i, k] + pair_recv[i, k].astype(jnp.float32)
                far_send[i, k] = total.astype(jnp.bfloat16)
                to_far(i, k).start()
    for k in range(HALVES):
        to_mate(last, k).wait()
        own[last, k] = own[last, k] + pair_recv[last, k].astype(jnp.float32)
    for k in range(HALVES):
        total = own[last, k]
        for i in range(last):
            to_far(i, k).wait()
            total = total + far_recv[i, k].astype(jnp.float32)
        out_ref[:, k * wide : (k + 1) * wide] = total.astype(jnp.bfloat16)


def split_kernel(both_ref, out_ref, tan_ref):
    tok = out_ref.shape[0]
    out_ref[...] = both_ref[:tok]
    tan_ref[...] = both_ref[tok:]


def split(both):
    vmem = pl.BlockSpec(memory_space=pltpu.VMEM)
    shape = jax.ShapeDtypeStruct((both.shape[0] // 2, both.shape[1]), both.dtype)
    return pl.pallas_call(
        split_kernel, out_shape=(shape, shape), in_specs=[vmem], out_specs=(vmem, vmem)
    )(both)


def body(n, parts, q, k, v, dq, dk, dv, routes, weight):
    tok, heads = routes.shape
    e = HEAD_SIZE
    per = tok // n
    groups = parts // 2
    width = weight.shape[1] // parts
    half = jnp.bfloat16
    vmem = pl.BlockSpec(memory_space=pltpu.VMEM)
    dma = pltpu.SemaphoreType.DMA
    shape = jax.ShapeDtypeStruct((2 * tok, width), half)
    both = pl.pallas_call(
        functools.partial(kernel, n, parts),
        out_shape=shape,
        in_specs=[vmem] * 7 + [pl.BlockSpec(memory_space=pl.ANY)],
        out_specs=vmem,
        scratch_shapes=[
            pltpu.VMEM((heads, tok), jnp.float32),
            pltpu.VMEM((heads, tok, tok), half),
            pltpu.VMEM((heads, n, per, 6 * e), half),
            pltpu.VMEM((heads, n, per, 6 * e), half),
            pltpu.VMEM((heads, n, per, 2 * e), half),
            pltpu.VMEM((heads, n, per, 2 * e), half),
            pltpu.VMEM(weight.shape, half),
            pltpu.VMEM((2 * tok, heads * e), half),
            pltpu.VMEM((groups, HALVES, 2 * tok, width // HALVES), jnp.float32),
            pltpu.VMEM((groups, HALVES, 2 * tok, width // HALVES), half),
            pltpu.VMEM((groups, HALVES, 2 * tok, width // HALVES), half),
            pltpu.VMEM((max(groups - 1, 1), HALVES, 2 * tok, width // HALVES), half),
            pltpu.VMEM((max(groups - 1, 1), HALVES, 2 * tok, width // HALVES), half),
            dma,
            dma((heads, n)),
            dma((heads, n)),
            dma((heads, n)),
            dma((heads, n)),
            dma((2, groups, HALVES)),
            dma((2, max(groups - 1, 1), HALVES)),
        ],
        compiler_params=pltpu.CompilerParams(
            collective_id=0, has_side_effects=True, vmem_limit_bytes=56 * 2**20
        ),
    )(q, k, v, dq, dk, dv, routes, weight)
    return split(both)


LEVELS = 4
CUTS = 4


def soft_rows(query, keys, offset):
    e = HEAD_SIZE
    scale = e**-0.5
    shape = (query.shape[0], keys.shape[0])
    scores = dot(query[:, e:], keys[:, :e], (1, 1)) * scale
    tangent = dot(query, keys[:, : 2 * e], (1, 1)) * scale
    visible = (
        lax.broadcasted_iota(jnp.int32, shape, 1)
        <= lax.broadcasted_iota(jnp.int32, shape, 0) + offset
    )
    masked = jnp.where(visible, scores, -jnp.inf)
    top = jnp.max(masked, -1, keepdims=True)
    expo = jnp.exp(masked - top)
    total = jnp.sum(expo, -1, keepdims=True)
    probs = expo / total
    mean = jnp.sum(probs * tangent, -1, keepdims=True)
    slope = probs * (tangent - mean)
    both = dot(probs.astype(jnp.bfloat16), keys[:, 2 * e :], (1, 0))
    extra = dot(slope.astype(jnp.bfloat16), keys[:, 2 * e : 3 * e], (1, 0))
    rows = jnp.concatenate([both[:, :e], both[:, e:] + extra], 1)
    return rows, top + jnp.log(total), mean


def pack_stats(level, mean):
    lane = lax.broadcasted_iota(jnp.int32, (level.shape[0], 128), 1)
    return jnp.where(lane == 0, level, jnp.where(lane == 1, mean, 0.0))


def merge(pieces):
    e = HEAD_SIZE
    top = functools.reduce(jnp.maximum, [level for _, level, _ in pieces])
    weights = [jnp.exp(level - top) for _, level, _ in pieces]
    total = functools.reduce(jnp.add, weights)
    weights = [w / total for w in weights]
    mean = sum(w * m for w, (_, _, m) in zip(weights, pieces))
    value = sum(w * rows[:, :e] for w, (rows, _, _) in zip(weights, pieces))
    slope = sum(
        w * (rows[:, e:] + (m - mean) * rows[:, :e]) for w, (rows, _, m) in zip(weights, pieces)
    )
    return jnp.concatenate([value, slope], 1)


def level_kernel(
    parts,
    q_ref,
    k_ref,
    v_ref,
    dq_ref,
    dk_ref,
    dv_ref,
    routes_ref,
    weight_hbm,
    out_ref,
    dest,
    order,
    sent,
    rows_here,
    keys_in,
    query_in,
    piece_out,
    piece_in,
    stats_out,
    stats_in,
    own_piece,
    own_stats,
    result,
    back,
    weight,
    acts,
    own,
    pair_send,
    pair_recv,
    far_send,
    far_recv,
    weight_sem,
    side_sems,
    key_sems,
    query_sems,
    piece_sems,
    stats_sems,
    back_sems,
    pair_sems,
    far_sems,
):
    e = HEAD_SIZE
    tok, width = q_ref.shape
    heads = width // e
    n = 2 * LEVELS
    per = tok // n
    here = heads // 2
    steps = CUTS * here
    some = n // CUTS
    groups = parts // 2
    me = lax.axis_index("seq")
    mine = lax.axis_index("tensor")
    level, side = lax.div(me, 2), lax.rem(me, 2)
    group, core = lax.div(mine, 2), lax.rem(mine, 2)
    mate = 2 * group + 1 - core

    barrier = pltpu.get_barrier_semaphore()
    for d in range(1, LEVELS):
        peer = 2 * lax.rem(level + d, LEVELS) + side
        pl.semaphore_signal(barrier, inc=1, device_id={"seq": peer}, device_id_type=MESH)
    pl.semaphore_signal(
        barrier, inc=1, device_id={"seq": 2 * level + 1 - side}, device_id_type=MESH
    )
    pl.semaphore_signal(barrier, inc=1, device_id={"tensor": mate}, device_id_type=MESH)
    for d in range(1, groups):
        pl.semaphore_signal(
            barrier,
            inc=1,
            device_id={"tensor": 2 * lax.rem(group + d, groups) + core},
            device_id_type=MESH,
        )
    load = pltpu.make_async_copy(weight_hbm, weight, weight_sem)
    load.start()

    row_at = lax.broadcasted_iota(jnp.int32, (tok, tok), 0)
    earlier = (row_at < lax.broadcasted_iota(jnp.int32, (tok, tok), 1)).astype(jnp.float32)
    earlier = earlier.astype(jnp.bfloat16)
    cluster = lax.broadcasted_iota(jnp.int32, (n, tok), 0)
    owner = jnp.right_shift(routes_ref[...], tok.bit_length() - 1).astype(jnp.float32)
    same = (row_at == lax.broadcasted_iota(jnp.int32, (tok, tok), 1)).astype(jnp.float32)
    dest[...] = dot(owner.astype(jnp.bfloat16), same.astype(jnp.bfloat16), (0, 0))

    def place(h, _):
        member = (dest[pl.ds(h, 1), :] == cluster.astype(jnp.float32)).astype(jnp.float32)
        rank = dot(member.astype(jnp.bfloat16), earlier, (1, 0))
        at = jnp.sum(member * (rank + (per * cluster).astype(jnp.float32)), 0, keepdims=True)
        order[h] = (row_at.astype(jnp.float32) == at).astype(jnp.float32).astype(jnp.bfloat16)
        return 0

    lax.fori_loop(0, heads, place, 0)
    pl.semaphore_wait(barrier, LEVELS + groups)

    def remote(src, dst, sems, at, device):
        return pltpu.make_async_remote_copy(
            src_ref=src,
            dst_ref=dst,
            send_sem=sems.at[(0, *at)],
            recv_sem=sems.at[(1, *at)],
            device_id=device,
            device_id_type=MESH,
        )

    across = {"seq": 2 * level + 1 - side}

    def at_level(z):
        return {"seq": 2 * z + side}

    def side_copy(c):
        return remote(sent.at[c], rows_here.at[c, side], side_sems, (c,), across)

    def key_copy(c):
        keys = rows_here.at[c, :, :, :, pl.ds(2 * e, 4 * e)]
        return remote(keys, keys_in.at[c], key_sems, (c,), at_level(1))

    def query_copy(slot, c, z):
        queries = rows_here.at[c, :, :, :, pl.ds(0, 2 * e)]
        return remote(queries, query_in.at[slot, c], query_sems, (slot, c), at_level(z))

    def piece_copies(slot, c, z):
        return (
            remote(piece_out.at[slot, c], piece_in.at[slot, c], piece_sems, (slot, c), at_level(z)),
            remote(stats_out.at[slot, c], stats_in.at[slot, c], stats_sems, (slot, c), at_level(z)),
        )

    def back_copy(c):
        return remote(result.at[c, 1 - side], back.at[c], back_sems, (c,), across)

    def placed(h, c):
        cols = pl.ds(pl.multiple_of(h * e, e), e)
        rows = jnp.concatenate(
            [r[:, cols] for r in (dq_ref, q_ref, k_ref, dk_ref, v_ref, dv_ref)], 1
        )
        size = tok // CUTS
        cut = pl.ds(pl.multiple_of(lax.rem(c, CUTS) * size, size), size)
        moved = dot(order[h, cut, :], rows, (1, 0)).astype(jnp.bfloat16)
        return moved.reshape(some, per, 6 * e)

    def scatter(c, _):
        sent[c] = placed((1 - side) * here + lax.div(c, CUTS), c)
        side_copy(c).start()
        return 0

    lax.fori_loop(0, steps, scatter, 0)

    def pair_of(ref, i):
        return jnp.concatenate([ref[0, i], ref[1, i]], 0)

    def finish(c, i, rows):
        rows = rows.astype(jnp.bfloat16)
        result[c, 0, i] = rows[:per]
        result[c, 1, i] = rows[per:]

    def hand_on(slot, c, z, parts_of):
        for i, (rows, _, _) in enumerate(parts_of):
            piece_out[slot, c, i] = rows.astype(jnp.bfloat16)
        packed = pack_stats(
            jnp.concatenate([p[1] for p in parts_of], 0),
            jnp.concatenate([p[2] for p in parts_of], 0),
        )
        stats_out[slot, c] = packed.T[:8]
        for copy in piece_copies(slot, c, z):
            copy.start()

    def keep(c, parts_of):
        own_piece[c] = jnp.concatenate([p[0] for p in parts_of], 0)
        own_stats[c] = pack_stats(
            jnp.concatenate([p[1] for p in parts_of], 0),
            jnp.concatenate([p[2] for p in parts_of], 0),
        )

    def advance(c):
        rows_here[c, side] = placed(side * here + lax.div(c, CUTS), c)
        side_copy(c).wait_recv()

        @pl.when(level == 0)
        def _():
            key_copy(c).start()

        @pl.when(level == 2)
        def _():
            query_copy(0, c, 1).start()

        @pl.when(level == 3)
        def _():
            query_copy(0, c, 2).start()
            query_copy(1, c, 1).start()

    def work(c):
        own_rows = rows_here.at[c]
        size = 2 * per

        def cut(piece, j):
            return tuple(x[j * size : (j + 1) * size] for x in piece)

        @pl.when(level == 0)
        def _():
            for i in range(some):
                rows = pair_of(own_rows, i)
                finish(c, i, soft_rows(rows[:, : 2 * e], rows[:, 2 * e :], 0)[0])
            back_copy(c).start()

        @pl.when(level == 1)
        def _():
            key_copy(c).wait_recv()
            query_copy(0, c, 1).wait_recv()
            query_copy(1, c, 1).wait_recv()
            pieces = []
            for i in range(some):
                rows = pair_of(own_rows, i)
                queries = jnp.concatenate(
                    [
                        rows[:, : 2 * e],
                        pair_of(query_in.at[0, c], i),
                        pair_of(query_in.at[1, c], i),
                    ],
                    0,
                )
                keys = jnp.concatenate([pair_of(keys_in.at[c], i), rows[:, 2 * e :]], 0)
                pieces.append(soft_rows(queries, keys, size))
            hand_on(1, c, 3, [cut(p, 2) for p in pieces])
            hand_on(0, c, 2, [cut(p, 1) for p in pieces])
            for i in range(some):
                finish(c, i, pieces[i][0][:size])
            back_copy(c).start()

        @pl.when(level == 2)
        def _():
            query_copy(0, c, 1).wait_recv()
            pieces = []
            for i in range(some):
                rows = pair_of(own_rows, i)
                queries = jnp.concatenate([rows[:, : 2 * e], pair_of(query_in.at[0, c], i)], 0)
                pieces.append(soft_rows(queries, rows[:, 2 * e :], 0))
            hand_on(0, c, 3, [cut(p, 1) for p in pieces])
            keep(c, [cut(p, 0) for p in pieces])

        @pl.when(level == 3)
        def _():
            pieces = []
            for i in range(some):
                rows = pair_of(own_rows, i)
                pieces.append(soft_rows(rows[:, : 2 * e], rows[:, 2 * e :], 0))
            keep(c, pieces)

    ahead = min(2, steps)
    for c in range(ahead):
        advance(c)

    def turn(c, _):
        @pl.when(c + ahead < steps)
        def _():
            advance(c + ahead)

        work(c)
        return 0

    lax.fori_loop(0, steps, turn, 0)

    def gather(c, slots):
        pieces = [(own_piece[c], own_stats[c, :, 0:1], own_stats[c, :, 1:2])]
        for slot in slots:
            for copy in piece_copies(slot, c, 2):
                copy.wait_recv()
            stats = stats_in[slot, c]
            stats = jnp.concatenate([stats, jnp.zeros((120, stats.shape[1]), jnp.float32)], 0).T
            rows = piece_in[slot, c].reshape(some * 2 * per, 2 * e).astype(jnp.float32)
            pieces.append((rows, stats[:, 0:1], stats[:, 1:2]))
        rows = merge(pieces)
        for i in range(some):
            finish(c, i, rows[i * 2 * per : (i + 1) * 2 * per])
        back_copy(c).start()

    @pl.when(level == 2)
    def _():
        lax.fori_loop(0, steps, lambda c, _: (gather(c, (0,)), 0)[1], 0)

    @pl.when(level == 3)
    def _():
        lax.fori_loop(0, steps, lambda c, _: (gather(c, (0, 1)), 0)[1], 0)

    def to_acts(h, rows):
        rows = dot(order[h], rows, (0, 0)).astype(jnp.bfloat16)
        cols = pl.ds(pl.multiple_of(h * e, e), e)
        acts[:tok, cols] = rows[:, :e]
        acts[tok:, cols] = rows[:, e:]

    def home(j, _):
        def whole(at):
            return jnp.concatenate(
                [at(CUTS * j + p).reshape(tok // CUTS, 2 * e) for p in range(CUTS)], 0
            )

        to_acts(side * here + j, whole(lambda c: result[c, side]))
        for p in range(CUTS):
            back_copy(CUTS * j + p).wait_recv()
        to_acts((1 - side) * here + j, whole(lambda c: back[c]))
        return 0

    lax.fori_loop(0, here, home, 0)
    load.wait()
    project(groups, group, core, mate, weight, acts, own, pair_send, pair_recv, far_send,
            far_recv, pair_sems, far_sems, out_ref)

    def drain(c, _):
        side_copy(c).wait_send()
        back_copy(c).wait_send()

        @pl.when(level == 0)
        def _():
            key_copy(c).wait_send()

        @pl.when(level == 1)
        def _():
            for slot in (0, 1):
                for copy in piece_copies(slot, c, 2 + slot):
                    copy.wait_send()

        @pl.when(level == 2)
        def _():
            query_copy(0, c, 1).wait_send()
            for copy in piece_copies(0, c, 3):
                copy.wait_send()

        @pl.when(level == 3)
        def _():
            query_copy(0, c, 2).wait_send()
            query_copy(1, c, 1).wait_send()

        return 0

    lax.fori_loop(0, steps, drain, 0)


def level_body(parts, q, k, v, dq, dk, dv, routes, weight):
    tok, heads = routes.shape
    e = HEAD_SIZE
    n = 2 * LEVELS
    per = tok // n
    steps = CUTS * (heads // 2)
    some = n // CUTS
    rows = some * 2 * per
    groups = parts // 2
    width = weight.shape[1] // parts
    half = jnp.bfloat16
    vmem = pl.BlockSpec(memory_space=pltpu.VMEM)
    dma = pltpu.SemaphoreType.DMA
    shape = jax.ShapeDtypeStruct((2 * tok, width), half)
    both = pl.pallas_call(
        functools.partial(level_kernel, parts),
        out_shape=shape,
        in_specs=[vmem] * 7 + [pl.BlockSpec(memory_space=pl.ANY)],
        out_specs=vmem,
        scratch_shapes=[
            pltpu.VMEM((heads, tok), jnp.float32),
            pltpu.VMEM((heads, tok, tok), half),
            pltpu.VMEM((steps, some, per, 6 * e), half),
            pltpu.VMEM((steps, 2, some, per, 6 * e), half),
            pltpu.VMEM((steps, 2, some, per, 4 * e), half),
            pltpu.VMEM((2, steps, 2, some, per, 2 * e), half),
            pltpu.VMEM((2, steps, some, 2 * per, 2 * e), half),
            pltpu.VMEM((2, steps, some, 2 * per, 2 * e), half),
            pltpu.VMEM((2, steps, 8, rows), jnp.float32),
            pltpu.VMEM((2, steps, 8, rows), jnp.float32),
            pltpu.VMEM((steps, rows, 2 * e), jnp.float32),
            pltpu.VMEM((steps, rows, 128), jnp.float32),
            pltpu.VMEM((steps, 2, some, per, 2 * e), half),
            pltpu.VMEM((steps, some, per, 2 * e), half),
            pltpu.VMEM(weight.shape, half),
            pltpu.VMEM((2 * tok, heads * e), half),
            pltpu.VMEM((groups, HALVES, 2 * tok, width // HALVES), jnp.float32),
            pltpu.VMEM((groups, HALVES, 2 * tok, width // HALVES), half),
            pltpu.VMEM((groups, HALVES, 2 * tok, width // HALVES), half),
            pltpu.VMEM((max(groups - 1, 1), HALVES, 2 * tok, width // HALVES), half),
            pltpu.VMEM((max(groups - 1, 1), HALVES, 2 * tok, width // HALVES), half),
            dma,
            dma((2, steps)),
            dma((2, steps)),
            dma((2, 2, steps)),
            dma((2, 2, steps)),
            dma((2, 2, steps)),
            dma((2, steps)),
            dma((2, groups, HALVES)),
            dma((2, max(groups - 1, 1), HALVES)),
        ],
        compiler_params=pltpu.CompilerParams(
            collective_id=1, has_side_effects=True, vmem_limit_bytes=58 * 2**20
        ),
    )(q, k, v, dq, dk, dv, routes, weight)
    return split(both)


def solution(mesh):
    n, parts = mesh.shape["seq"], mesh.shape["tensor"]

    def run(*args):
        if n == 2 * LEVELS and args[6].shape[1] % 2 == 0:
            return level_body(parts, *args)
        return body(n, parts, *args)

    return jax.shard_map(
        run,
        mesh=mesh,
        in_specs=(P("seq", "tensor"),) * 7 + (P("tensor", None),),
        out_specs=(P("seq", "tensor"), P("seq", "tensor")),
        check_vma=False,
    )
```

```python
import functools

import jax
import jax.numpy as jnp
from jax import lax
from jax.experimental import pallas as pl
from jax.experimental.pallas import tpu as pltpu
from jax.sharding import PartitionSpec as P

HEAD_SIZE = 128
MESH = pl.DeviceIdType.MESH
HALVES = 2


def dot(a, b, contract):
    return lax.dot_general(
        a, b, (((contract[0],), (contract[1],)), ((), ())), preferred_element_type=jnp.float32
    )


def attend(rows):
    e = HEAD_SIZE
    scale = e**-0.5
    count = rows.shape[0]
    query, key = rows[:, e : 2 * e], rows[:, 2 * e : 3 * e]
    scores = dot(query, key, (1, 1)) * scale
    tangent = dot(rows[:, : 2 * e], rows[:, 2 * e : 4 * e], (1, 1)) * scale
    visible = lax.broadcasted_iota(jnp.int32, (count, count), 1) <= lax.broadcasted_iota(
        jnp.int32, (count, count), 0
    )
    masked = jnp.where(visible, scores, -jnp.inf)
    expo = jnp.exp(masked - jnp.max(masked, -1, keepdims=True))
    probs = expo / jnp.sum(expo, -1, keepdims=True)
    slope = probs * (tangent - jnp.sum(probs * tangent, -1, keepdims=True))
    both = dot(probs.astype(jnp.bfloat16), rows[:, 4 * e :], (1, 0))
    extra = dot(slope.astype(jnp.bfloat16), rows[:, 4 * e : 5 * e], (1, 0))
    return jnp.concatenate([both[:, :e], both[:, e:] + extra], 1).astype(jnp.bfloat16)


def kernel(
    n,
    parts,
    q_ref,
    k_ref,
    v_ref,
    dq_ref,
    dk_ref,
    dv_ref,
    routes_ref,
    weight_hbm,
    out_ref,
    dest,
    order,
    sent,
    got,
    result,
    back,
    weight,
    acts,
    own,
    pair_send,
    pair_recv,
    far_send,
    far_recv,
    weight_sem,
    go_send,
    go_recv,
    back_send,
    back_recv,
    pair_sems,
    far_sems,
):
    e = HEAD_SIZE
    tok, width = q_ref.shape
    heads = width // e
    per = tok // n
    groups = parts // 2
    me = lax.axis_index("seq")
    mine = lax.axis_index("tensor")
    group, core = lax.div(mine, 2), lax.rem(mine, 2)
    mate = 2 * group + 1 - core

    barrier = pltpu.get_barrier_semaphore()
    for d in range(1, n):
        pl.semaphore_signal(
            barrier, inc=1, device_id={"seq": lax.rem(me + d, n)}, device_id_type=MESH
        )
    pl.semaphore_signal(barrier, inc=1, device_id={"tensor": mate}, device_id_type=MESH)
    for d in range(1, groups):
        pl.semaphore_signal(
            barrier,
            inc=1,
            device_id={"tensor": 2 * lax.rem(group + d, groups) + core},
            device_id_type=MESH,
        )
    load = pltpu.make_async_copy(weight_hbm, weight, weight_sem)
    load.start()

    row_at = lax.broadcasted_iota(jnp.int32, (tok, tok), 0)
    earlier = (row_at < lax.broadcasted_iota(jnp.int32, (tok, tok), 1)).astype(jnp.float32)
    earlier = earlier.astype(jnp.bfloat16)
    cluster = lax.broadcasted_iota(jnp.int32, (n, tok), 0)
    dest[...] = jnp.right_shift(routes_ref[...], tok.bit_length() - 1).astype(jnp.float32)

    def place(h, _):
        member = (dest[pl.ds(h, 1), :] == cluster.astype(jnp.float32)).astype(jnp.float32)
        rank = dot(member.astype(jnp.bfloat16), earlier, (1, 0))
        at = jnp.sum(member * (rank + (per * cluster).astype(jnp.float32)), 0, keepdims=True)
        order[h] = (row_at.astype(jnp.float32) == at).astype(jnp.float32).astype(jnp.bfloat16)
        return 0

    lax.fori_loop(0, heads, place, 0)
    pl.semaphore_wait(barrier, n - 1 + groups)

    def go(h, d):
        peer = lax.rem(me + d, n)
        return pltpu.make_async_remote_copy(
            src_ref=sent.at[h, peer],
            dst_ref=got.at[h, me],
            send_sem=go_send.at[h, d],
            recv_sem=go_recv.at[h, d],
            device_id={"seq": peer},
            device_id_type=MESH,
        )

    def come(h, d):
        peer = lax.rem(me + d, n)
        return pltpu.make_async_remote_copy(
            src_ref=result.at[h, peer],
            dst_ref=back.at[h, me],
            send_sem=back_send.at[h, d],
            recv_sem=back_recv.at[h, d],
            device_id={"seq": peer},
            device_id_type=MESH,
        )

    def scatter(h, _):
        cols = pl.ds(pl.multiple_of(h * e, e), e)
        rows = jnp.concatenate(
            [r[:, cols] for r in (dq_ref, q_ref, k_ref, dk_ref, v_ref, dv_ref)], 1
        )
        placed = dot(order[h], rows, (1, 0)).astype(jnp.bfloat16)
        sent[h] = placed.reshape(n, per, 6 * e)
        got[h, me] = sent[h, me]

        def start(d, _):
            go(h, d).start()
            return 0

        lax.fori_loop(1, n, start, 0)
        return 0

    lax.fori_loop(0, heads, scatter, 0)

    def work(h, _):
        def wait(d, _):
            go(h, d).wait()
            return 0

        lax.fori_loop(1, n, wait, 0)
        result[h] = attend(got[h].reshape(tok, 6 * e)).reshape(n, per, 2 * e)
        back[h, me] = result[h, me]

        def start(d, _):
            come(h, d).start()
            return 0

        lax.fori_loop(1, n, start, 0)
        return 0

    lax.fori_loop(0, heads, work, 0)

    def home(h, _):
        def wait(d, _):
            come(h, d).wait()
            return 0

        lax.fori_loop(1, n, wait, 0)
        rows = dot(order[h], back[h].reshape(tok, 2 * e), (0, 0)).astype(jnp.bfloat16)
        cols = pl.ds(pl.multiple_of(h * e, e), e)
        acts[:tok, cols] = rows[:, :e]
        acts[tok:, cols] = rows[:, e:]
        return 0

    lax.fori_loop(0, heads, home, 0)
    load.wait()
    project(groups, group, core, mate, weight, acts, own, pair_send, pair_recv, far_send,
            far_recv, pair_sems, far_sems, out_ref)


def project(groups, group, core, mate, weight, acts, own, pair_send, pair_recv, far_send,
            far_recv, pair_sems, far_sems, out_ref):
    wide = out_ref.shape[1] // HALVES
    tile = min(256, wide)

    def product(block, half, store):
        def step(i, _):
            at = pl.multiple_of(i * tile, tile)
            first = (block * HALVES + half) * wide
            source = pl.ds(pl.multiple_of(first + at, tile), tile)
            store(pl.ds(at, tile), dot(acts[...], weight[:, source], (1, 0)))
            return 0

        lax.fori_loop(0, wide // tile, step, 0)

    def to_mate(i, k):
        return pltpu.make_async_remote_copy(
            src_ref=pair_send.at[i, k],
            dst_ref=pair_recv.at[i, k],
            send_sem=pair_sems.at[0, i, k],
            recv_sem=pair_sems.at[1, i, k],
            device_id={"tensor": mate},
            device_id_type=MESH,
        )

    def to_far(i, k):
        return pltpu.make_async_remote_copy(
            src_ref=far_send.at[i, k],
            dst_ref=far_recv.at[i, k],
            send_sem=far_sems.at[0, i, k],
            recv_sem=far_sems.at[1, i, k],
            device_id={"tensor": 2 * lax.rem(group + 1 + i, groups) + core},
            device_id_type=MESH,
        )

    last = groups - 1
    for i in range(groups):
        there = lax.rem(group + 1 + i, groups)
        for k in range(HALVES):

            def keep_pair(cols, value, i=i, k=k):
                pair_send[i, k, :, cols] = value.astype(jnp.bfloat16)

            product(2 * there + 1 - core, k, keep_pair)
            to_mate(i, k).start()
        for k in range(HALVES):

            def keep_own(cols, value, i=i, k=k):
                own[i, k, :, cols] = value

            product(2 * there + core, k, keep_own)
            if i < last:
                to_mate(i, k).wait()
                total = own[i, k] + pair_recv[i, k].astype(jnp.float32)
                far_send[i, k] = total.astype(jnp.bfloat16)
                to_far(i, k).start()
    for k in range(HALVES):
        to_mate(last, k).wait()
        own[last, k] = own[last, k] + pair_recv[last, k].astype(jnp.float32)
    for k in range(HALVES):
        total = own[last, k]
        for i in range(last):
            to_far(i, k).wait()
            total = total + far_recv[i, k].astype(jnp.float32)
        out_ref[:, k * wide : (k + 1) * wide] = total.astype(jnp.bfloat16)


def split_kernel(both_ref, out_ref, tan_ref):
    tok = out_ref.shape[0]
    out_ref[...] = both_ref[:tok]
    tan_ref[...] = both_ref[tok:]


def split(both):
    vmem = pl.BlockSpec(memory_space=pltpu.VMEM)
    shape = jax.ShapeDtypeStruct((both.shape[0] // 2, both.shape[1]), both.dtype)
    return pl.pallas_call(
        split_kernel, out_shape=(shape, shape), in_specs=[vmem], out_specs=(vmem, vmem)
    )(both)


def body(n, parts, q, k, v, dq, dk, dv, routes, weight):
    tok, heads = routes.shape
    e = HEAD_SIZE
    per = tok // n
    groups = parts // 2
    width = weight.shape[1] // parts
    half = jnp.bfloat16
    vmem = pl.BlockSpec(memory_space=pltpu.VMEM)
    dma = pltpu.SemaphoreType.DMA
    shape = jax.ShapeDtypeStruct((2 * tok, width), half)
    both = pl.pallas_call(
        functools.partial(kernel, n, parts),
        out_shape=shape,
        in_specs=[vmem] * 7 + [pl.BlockSpec(memory_space=pl.ANY)],
        out_specs=vmem,
        scratch_shapes=[
            pltpu.VMEM((heads, tok), jnp.float32),
            pltpu.VMEM((heads, tok, tok), half),
            pltpu.VMEM((heads, n, per, 6 * e), half),
            pltpu.VMEM((heads, n, per, 6 * e), half),
            pltpu.VMEM((heads, n, per, 2 * e), half),
            pltpu.VMEM((heads, n, per, 2 * e), half),
            pltpu.VMEM(weight.shape, half),
            pltpu.VMEM((2 * tok, heads * e), half),
            pltpu.VMEM((groups, HALVES, 2 * tok, width // HALVES), jnp.float32),
            pltpu.VMEM((groups, HALVES, 2 * tok, width // HALVES), half),
            pltpu.VMEM((groups, HALVES, 2 * tok, width // HALVES), half),
            pltpu.VMEM((max(groups - 1, 1), HALVES, 2 * tok, width // HALVES), half),
            pltpu.VMEM((max(groups - 1, 1), HALVES, 2 * tok, width // HALVES), half),
            dma,
            dma((heads, n)),
            dma((heads, n)),
            dma((heads, n)),
            dma((heads, n)),
            dma((2, groups, HALVES)),
            dma((2, max(groups - 1, 1), HALVES)),
        ],
        compiler_params=pltpu.CompilerParams(
            collective_id=0, has_side_effects=True, vmem_limit_bytes=56 * 2**20
        ),
    )(q, k, v, dq, dk, dv, routes.T, weight)
    return split(both)


LEVELS = 4
CUTS = 4


def soft_rows(query, keys, offset):
    e = HEAD_SIZE
    scale = e**-0.5
    shape = (query.shape[0], keys.shape[0])
    scores = dot(query[:, e:], keys[:, :e], (1, 1)) * scale
    tangent = dot(query, keys[:, : 2 * e], (1, 1)) * scale
    visible = (
        lax.broadcasted_iota(jnp.int32, shape, 1)
        <= lax.broadcasted_iota(jnp.int32, shape, 0) + offset
    )
    masked = jnp.where(visible, scores, -jnp.inf)
    top = jnp.max(masked, -1, keepdims=True)
    expo = jnp.exp(masked - top)
    total = jnp.sum(expo, -1, keepdims=True)
    probs = expo / total
    mean = jnp.sum(probs * tangent, -1, keepdims=True)
    slope = probs * (tangent - mean)
    both = dot(probs.astype(jnp.bfloat16), keys[:, 2 * e :], (1, 0))
    extra = dot(slope.astype(jnp.bfloat16), keys[:, 2 * e : 3 * e], (1, 0))
    rows = jnp.concatenate([both[:, :e], both[:, e:] + extra], 1)
    return rows, top + jnp.log(total), mean


def pack_stats(level, mean):
    lane = lax.broadcasted_iota(jnp.int32, (level.shape[0], 128), 1)
    return jnp.where(lane == 0, level, jnp.where(lane == 1, mean, 0.0))


def merge(pieces):
    e = HEAD_SIZE
    top = functools.reduce(jnp.maximum, [level for _, level, _ in pieces])
    weights = [jnp.exp(level - top) for _, level, _ in pieces]
    total = functools.reduce(jnp.add, weights)
    weights = [w / total for w in weights]
    mean = sum(w * m for w, (_, _, m) in zip(weights, pieces))
    value = sum(w * rows[:, :e] for w, (rows, _, _) in zip(weights, pieces))
    slope = sum(
        w * (rows[:, e:] + (m - mean) * rows[:, :e]) for w, (rows, _, m) in zip(weights, pieces)
    )
    return jnp.concatenate([value, slope], 1)


def level_kernel(
    parts,
    q_ref,
    k_ref,
    v_ref,
    dq_ref,
    dk_ref,
    dv_ref,
    routes_ref,
    weight_hbm,
    out_ref,
    dest,
    order,
    sent,
    rows_here,
    keys_in,
    query_in,
    piece_out,
    piece_in,
    stats_out,
    stats_in,
    own_piece,
    own_stats,
    result,
    back,
    weight,
    acts,
    own,
    pair_send,
    pair_recv,
    far_send,
    far_recv,
    weight_sem,
    side_sems,
    key_sems,
    query_sems,
    piece_sems,
    stats_sems,
    back_sems,
    pair_sems,
    far_sems,
):
    e = HEAD_SIZE
    tok, width = q_ref.shape
    heads = width // e
    n = 2 * LEVELS
    per = tok // n
    here = heads // 2
    steps = CUTS * here
    some = n // CUTS
    groups = parts // 2
    me = lax.axis_index("seq")
    mine = lax.axis_index("tensor")
    level, side = lax.div(me, 2), lax.rem(me, 2)
    group, core = lax.div(mine, 2), lax.rem(mine, 2)
    mate = 2 * group + 1 - core

    barrier = pltpu.get_barrier_semaphore()
    for d in range(1, LEVELS):
        peer = 2 * lax.rem(level + d, LEVELS) + side
        pl.semaphore_signal(barrier, inc=1, device_id={"seq": peer}, device_id_type=MESH)
    pl.semaphore_signal(
        barrier, inc=1, device_id={"seq": 2 * level + 1 - side}, device_id_type=MESH
    )
    pl.semaphore_signal(barrier, inc=1, device_id={"tensor": mate}, device_id_type=MESH)
    for d in range(1, groups):
        pl.semaphore_signal(
            barrier,
            inc=1,
            device_id={"tensor": 2 * lax.rem(group + d, groups) + core},
            device_id_type=MESH,
        )
    load = pltpu.make_async_copy(weight_hbm, weight, weight_sem)
    load.start()

    row_at = lax.broadcasted_iota(jnp.int32, (tok, tok), 0)
    earlier = (row_at < lax.broadcasted_iota(jnp.int32, (tok, tok), 1)).astype(jnp.float32)
    earlier = earlier.astype(jnp.bfloat16)
    cluster = lax.broadcasted_iota(jnp.int32, (n, tok), 0)
    dest[...] = jnp.right_shift(routes_ref[...], tok.bit_length() - 1).astype(jnp.float32)

    def place(h, _):
        member = (dest[pl.ds(h, 1), :] == cluster.astype(jnp.float32)).astype(jnp.float32)
        rank = dot(member.astype(jnp.bfloat16), earlier, (1, 0))
        at = jnp.sum(member * (rank + (per * cluster).astype(jnp.float32)), 0, keepdims=True)
        order[h] = (row_at.astype(jnp.float32) == at).astype(jnp.float32).astype(jnp.bfloat16)
        return 0

    lax.fori_loop(0, heads, place, 0)
    pl.semaphore_wait(barrier, LEVELS + groups)

    def remote(src, dst, sems, at, device):
        return pltpu.make_async_remote_copy(
            src_ref=src,
            dst_ref=dst,
            send_sem=sems.at[(0, *at)],
            recv_sem=sems.at[(1, *at)],
            device_id=device,
            device_id_type=MESH,
        )

    across = {"seq": 2 * level + 1 - side}

    def at_level(z):
        return {"seq": 2 * z + side}

    def side_copy(c):
        return remote(sent.at[c], rows_here.at[c, side], side_sems, (c,), across)

    def key_copy(c):
        keys = rows_here.at[c, :, :, :, pl.ds(2 * e, 4 * e)]
        return remote(keys, keys_in.at[c], key_sems, (c,), at_level(1))

    def query_copy(slot, c, z):
        queries = rows_here.at[c, :, :, :, pl.ds(0, 2 * e)]
        return remote(queries, query_in.at[slot, c], query_sems, (slot, c), at_level(z))

    def piece_copies(slot, c, z):
        return (
            remote(piece_out.at[slot, c], piece_in.at[slot, c], piece_sems, (slot, c), at_level(z)),
            remote(stats_out.at[slot, c], stats_in.at[slot, c], stats_sems, (slot, c), at_level(z)),
        )

    def back_copy(c):
        return remote(result.at[c, 1 - side], back.at[c], back_sems, (c,), across)

    def placed(h, c):
        cols = pl.ds(pl.multiple_of(h * e, e), e)
        rows = jnp.concatenate(
            [r[:, cols] for r in (dq_ref, q_ref, k_ref, dk_ref, v_ref, dv_ref)], 1
        )
        size = tok // CUTS
        cut = pl.ds(pl.multiple_of(lax.rem(c, CUTS) * size, size), size)
        moved = dot(order[h, cut, :], rows, (1, 0)).astype(jnp.bfloat16)
        return moved.reshape(some, per, 6 * e)

    def scatter(c, _):
        sent[c] = placed((1 - side) * here + lax.div(c, CUTS), c)
        side_copy(c).start()
        return 0

    lax.fori_loop(0, steps, scatter, 0)

    def pair_of(ref, i):
        return jnp.concatenate([ref[0, i], ref[1, i]], 0)

    def finish(c, i, rows):
        rows = rows.astype(jnp.bfloat16)
        result[c, 0, i] = rows[:per]
        result[c, 1, i] = rows[per:]

    def hand_on(slot, c, z, parts_of):
        for i, (rows, _, _) in enumerate(parts_of):
            piece_out[slot, c, i] = rows.astype(jnp.bfloat16)
        packed = pack_stats(
            jnp.concatenate([p[1] for p in parts_of], 0),
            jnp.concatenate([p[2] for p in parts_of], 0),
        )
        stats_out[slot, c] = packed.T[:8]
        for copy in piece_copies(slot, c, z):
            copy.start()

    def keep(c, parts_of):
        own_piece[c] = jnp.concatenate([p[0] for p in parts_of], 0)
        own_stats[c] = pack_stats(
            jnp.concatenate([p[1] for p in parts_of], 0),
            jnp.concatenate([p[2] for p in parts_of], 0),
        )

    def advance(c):
        rows_here[c, side] = placed(side * here + lax.div(c, CUTS), c)
        side_copy(c).wait_recv()

        @pl.when(level == 0)
        def _():
            key_copy(c).start()

        @pl.when(level == 2)
        def _():
            query_copy(0, c, 1).start()

        @pl.when(level == 3)
        def _():
            query_copy(0, c, 2).start()
            query_copy(1, c, 1).start()

    def work(c):
        own_rows = rows_here.at[c]
        size = 2 * per

        def cut(piece, j):
            return tuple(x[j * size : (j + 1) * size] for x in piece)

        @pl.when(level == 0)
        def _():
            for i in range(some):
                rows = pair_of(own_rows, i)
                finish(c, i, soft_rows(rows[:, : 2 * e], rows[:, 2 * e :], 0)[0])
            back_copy(c).start()

        @pl.when(level == 1)
        def _():
            key_copy(c).wait_recv()
            query_copy(0, c, 1).wait_recv()
            query_copy(1, c, 1).wait_recv()
            pieces = []
            for i in range(some):
                rows = pair_of(own_rows, i)
                queries = jnp.concatenate(
                    [
                        rows[:, : 2 * e],
                        pair_of(query_in.at[0, c], i),
                        pair_of(query_in.at[1, c], i),
                    ],
                    0,
                )
                keys = jnp.concatenate([pair_of(keys_in.at[c], i), rows[:, 2 * e :]], 0)
                pieces.append(soft_rows(queries, keys, size))
            hand_on(1, c, 3, [cut(p, 2) for p in pieces])
            hand_on(0, c, 2, [cut(p, 1) for p in pieces])
            for i in range(some):
                finish(c, i, pieces[i][0][:size])
            back_copy(c).start()

        @pl.when(level == 2)
        def _():
            query_copy(0, c, 1).wait_recv()
            pieces = []
            for i in range(some):
                rows = pair_of(own_rows, i)
                queries = jnp.concatenate([rows[:, : 2 * e], pair_of(query_in.at[0, c], i)], 0)
                pieces.append(soft_rows(queries, rows[:, 2 * e :], 0))
            hand_on(0, c, 3, [cut(p, 1) for p in pieces])
            keep(c, [cut(p, 0) for p in pieces])

        @pl.when(level == 3)
        def _():
            pieces = []
            for i in range(some):
                rows = pair_of(own_rows, i)
                pieces.append(soft_rows(rows[:, : 2 * e], rows[:, 2 * e :], 0))
            keep(c, pieces)

    def to_acts(h, rows):
        rows = dot(order[h], rows, (0, 0)).astype(jnp.bfloat16)
        cols = pl.ds(pl.multiple_of(h * e, e), e)
        acts[:tok, cols] = rows[:, :e]
        acts[tok:, cols] = rows[:, e:]

    def home(j, _):
        def whole(at):
            return jnp.concatenate(
                [at(CUTS * j + p).reshape(tok // CUTS, 2 * e) for p in range(CUTS)], 0
            )

        to_acts(side * here + j, whole(lambda c: result[c, side]))
        for p in range(CUTS):
            back_copy(CUTS * j + p).wait_recv()
        to_acts((1 - side) * here + j, whole(lambda c: back[c]))
        return 0

    def gather(c, slots):
        pieces = [(own_piece[c], own_stats[c, :, 0:1], own_stats[c, :, 1:2])]
        for slot in slots:
            for copy in piece_copies(slot, c, 2):
                copy.wait_recv()
            stats = stats_in[slot, c]
            stats = jnp.concatenate([stats, jnp.zeros((120, stats.shape[1]), jnp.float32)], 0).T
            rows = piece_in[slot, c].reshape(some * 2 * per, 2 * e).astype(jnp.float32)
            pieces.append((rows, stats[:, 0:1], stats[:, 1:2]))
        rows = merge(pieces)
        for i in range(some):
            finish(c, i, rows[i * 2 * per : (i + 1) * 2 * per])
        back_copy(c).start()

    def collect(c):
        @pl.when(level == 2)
        def _():
            gather(c, (0,))

        @pl.when(level == 3)
        def _():
            gather(c, (0, 1))

    ahead, lag = 2, CUTS
    for c in range(ahead):
        advance(c)

    def turn(c, _):
        @pl.when(c + ahead < steps)
        def _():
            advance(c + ahead)

        work(c)

        @pl.when(c >= lag)
        def _():
            collect(c - lag)

        return 0

    lax.fori_loop(0, steps, turn, 0)
    lax.fori_loop(0, here - 1, home, 0)

    def rest(c, _):
        collect(c)
        return 0

    lax.fori_loop(steps - lag, steps, rest, 0)
    home(here - 1, 0)
    load.wait()
    project(groups, group, core, mate, weight, acts, own, pair_send, pair_recv, far_send,
            far_recv, pair_sems, far_sems, out_ref)

    def drain(c, _):
        side_copy(c).wait_send()
        back_copy(c).wait_send()

        @pl.when(level == 0)
        def _():
            key_copy(c).wait_send()

        @pl.when(level == 1)
        def _():
            for slot in (0, 1):
                for copy in piece_copies(slot, c, 2 + slot):
                    copy.wait_send()

        @pl.when(level == 2)
        def _():
            query_copy(0, c, 1).wait_send()
            for copy in piece_copies(0, c, 3):
                copy.wait_send()

        @pl.when(level == 3)
        def _():
            query_copy(0, c, 2).wait_send()
            query_copy(1, c, 1).wait_send()

        return 0

    lax.fori_loop(0, steps, drain, 0)


def level_body(parts, q, k, v, dq, dk, dv, routes, weight):
    tok, heads = routes.shape
    e = HEAD_SIZE
    n = 2 * LEVELS
    per = tok // n
    steps = CUTS * (heads // 2)
    some = n // CUTS
    rows = some * 2 * per
    groups = parts // 2
    width = weight.shape[1] // parts
    half = jnp.bfloat16
    vmem = pl.BlockSpec(memory_space=pltpu.VMEM)
    dma = pltpu.SemaphoreType.DMA
    shape = jax.ShapeDtypeStruct((2 * tok, width), half)
    both = pl.pallas_call(
        functools.partial(level_kernel, parts),
        out_shape=shape,
        in_specs=[vmem] * 7 + [pl.BlockSpec(memory_space=pl.ANY)],
        out_specs=vmem,
        scratch_shapes=[
            pltpu.VMEM((heads, tok), jnp.float32),
            pltpu.VMEM((heads, tok, tok), half),
            pltpu.VMEM((steps, some, per, 6 * e), half),
            pltpu.VMEM((steps, 2, some, per, 6 * e), half),
            pltpu.VMEM((steps, 2, some, per, 4 * e), half),
            pltpu.VMEM((2, steps, 2, some, per, 2 * e), half),
            pltpu.VMEM((2, steps, some, 2 * per, 2 * e), half),
            pltpu.VMEM((2, steps, some, 2 * per, 2 * e), half),
            pltpu.VMEM((2, steps, 8, rows), jnp.float32),
            pltpu.VMEM((2, steps, 8, rows), jnp.float32),
            pltpu.VMEM((steps, rows, 2 * e), jnp.float32),
            pltpu.VMEM((steps, rows, 128), jnp.float32),
            pltpu.VMEM((steps, 2, some, per, 2 * e), half),
            pltpu.VMEM((steps, some, per, 2 * e), half),
            pltpu.VMEM(weight.shape, half),
            pltpu.VMEM((2 * tok, heads * e), half),
            pltpu.VMEM((groups, HALVES, 2 * tok, width // HALVES), jnp.float32),
            pltpu.VMEM((groups, HALVES, 2 * tok, width // HALVES), half),
            pltpu.VMEM((groups, HALVES, 2 * tok, width // HALVES), half),
            pltpu.VMEM((max(groups - 1, 1), HALVES, 2 * tok, width // HALVES), half),
            pltpu.VMEM((max(groups - 1, 1), HALVES, 2 * tok, width // HALVES), half),
            dma,
            dma((2, steps)),
            dma((2, steps)),
            dma((2, 2, steps)),
            dma((2, 2, steps)),
            dma((2, 2, steps)),
            dma((2, steps)),
            dma((2, groups, HALVES)),
            dma((2, max(groups - 1, 1), HALVES)),
        ],
        compiler_params=pltpu.CompilerParams(
            collective_id=1, has_side_effects=True, vmem_limit_bytes=58 * 2**20
        ),
    )(q, k, v, dq, dk, dv, routes.T, weight)
    return split(both)


def solution(mesh):
    n, parts = mesh.shape["seq"], mesh.shape["tensor"]

    def run(*args):
        if n == 2 * LEVELS and args[6].shape[1] % 2 == 0:
            return level_body(parts, *args)
        return body(n, parts, *args)

    return jax.shard_map(
        run,
        mesh=mesh,
        in_specs=(P("seq", "tensor"),) * 7 + (P("tensor", None),),
        out_specs=(P("seq", "tensor"), P("seq", "tensor")),
        check_vma=False,
    )
```

```python
import functools

import jax
import jax.numpy as jnp
from jax import lax
from jax.experimental import pallas as pl
from jax.experimental.pallas import tpu as pltpu
from jax.sharding import PartitionSpec as P

HEAD_SIZE = 128
MESH = pl.DeviceIdType.MESH
HALVES = 2


def dot(a, b, contract):
    return lax.dot_general(
        a, b, (((contract[0],), (contract[1],)), ((), ())), preferred_element_type=jnp.float32
    )


def attend(rows):
    e = HEAD_SIZE
    scale = e**-0.5
    count = rows.shape[0]
    query, key = rows[:, e : 2 * e], rows[:, 2 * e : 3 * e]
    scores = dot(query, key, (1, 1)) * scale
    tangent = dot(rows[:, : 2 * e], rows[:, 2 * e : 4 * e], (1, 1)) * scale
    visible = lax.broadcasted_iota(jnp.int32, (count, count), 1) <= lax.broadcasted_iota(
        jnp.int32, (count, count), 0
    )
    masked = jnp.where(visible, scores, -jnp.inf)
    expo = jnp.exp(masked - jnp.max(masked, -1, keepdims=True))
    probs = expo / jnp.sum(expo, -1, keepdims=True)
    slope = probs * (tangent - jnp.sum(probs * tangent, -1, keepdims=True))
    both = dot(probs.astype(jnp.bfloat16), rows[:, 4 * e :], (1, 0))
    extra = dot(slope.astype(jnp.bfloat16), rows[:, 4 * e : 5 * e], (1, 0))
    return jnp.concatenate([both[:, :e], both[:, e:] + extra], 1).astype(jnp.bfloat16)


def kernel(
    n,
    parts,
    q_ref,
    k_ref,
    v_ref,
    dq_ref,
    dk_ref,
    dv_ref,
    routes_ref,
    weight_hbm,
    out_ref,
    dest,
    order,
    sent,
    got,
    result,
    back,
    weight,
    acts,
    own,
    pair_send,
    pair_recv,
    far_send,
    far_recv,
    weight_sem,
    go_send,
    go_recv,
    back_send,
    back_recv,
    pair_sems,
    far_sems,
):
    e = HEAD_SIZE
    tok, width = q_ref.shape
    heads = width // e
    per = tok // n
    groups = parts // 2
    me = lax.axis_index("seq")
    mine = lax.axis_index("tensor")
    group, core = lax.div(mine, 2), lax.rem(mine, 2)
    mate = 2 * group + 1 - core

    barrier = pltpu.get_barrier_semaphore()
    for d in range(1, n):
        pl.semaphore_signal(
            barrier, inc=1, device_id={"seq": lax.rem(me + d, n)}, device_id_type=MESH
        )
    pl.semaphore_signal(barrier, inc=1, device_id={"tensor": mate}, device_id_type=MESH)
    for d in range(1, groups):
        pl.semaphore_signal(
            barrier,
            inc=1,
            device_id={"tensor": 2 * lax.rem(group + d, groups) + core},
            device_id_type=MESH,
        )
    load = pltpu.make_async_copy(weight_hbm, weight, weight_sem)
    load.start()

    row_at = lax.broadcasted_iota(jnp.int32, (tok, tok), 0)
    earlier = (row_at < lax.broadcasted_iota(jnp.int32, (tok, tok), 1)).astype(jnp.float32)
    earlier = earlier.astype(jnp.bfloat16)
    cluster = lax.broadcasted_iota(jnp.int32, (n, tok), 0)
    dest[...] = jnp.right_shift(routes_ref[...], tok.bit_length() - 1).astype(jnp.float32)

    def place(h, _):
        member = (dest[pl.ds(h, 1), :] == cluster.astype(jnp.float32)).astype(jnp.float32)
        rank = dot(member.astype(jnp.bfloat16), earlier, (1, 0))
        at = jnp.sum(member * (rank + (per * cluster).astype(jnp.float32)), 0, keepdims=True)
        order[h] = (row_at.astype(jnp.float32) == at).astype(jnp.float32).astype(jnp.bfloat16)
        return 0

    lax.fori_loop(0, heads, place, 0)
    pl.semaphore_wait(barrier, n - 1 + groups)

    def go(h, d):
        peer = lax.rem(me + d, n)
        return pltpu.make_async_remote_copy(
            src_ref=sent.at[h, peer],
            dst_ref=got.at[h, me],
            send_sem=go_send.at[h, d],
            recv_sem=go_recv.at[h, d],
            device_id={"seq": peer},
            device_id_type=MESH,
        )

    def come(h, d):
        peer = lax.rem(me + d, n)
        return pltpu.make_async_remote_copy(
            src_ref=result.at[h, peer],
            dst_ref=back.at[h, me],
            send_sem=back_send.at[h, d],
            recv_sem=back_recv.at[h, d],
            device_id={"seq": peer},
            device_id_type=MESH,
        )

    def scatter(h, _):
        cols = pl.ds(pl.multiple_of(h * e, e), e)
        rows = jnp.concatenate(
            [r[:, cols] for r in (dq_ref, q_ref, k_ref, dk_ref, v_ref, dv_ref)], 1
        )
        placed = dot(order[h], rows, (1, 0)).astype(jnp.bfloat16)
        sent[h] = placed.reshape(n, per, 6 * e)
        got[h, me] = sent[h, me]

        def start(d, _):
            go(h, d).start()
            return 0

        lax.fori_loop(1, n, start, 0)
        return 0

    lax.fori_loop(0, heads, scatter, 0)

    def work(h, _):
        def wait(d, _):
            go(h, d).wait()
            return 0

        lax.fori_loop(1, n, wait, 0)
        result[h] = attend(got[h].reshape(tok, 6 * e)).reshape(n, per, 2 * e)
        back[h, me] = result[h, me]

        def start(d, _):
            come(h, d).start()
            return 0

        lax.fori_loop(1, n, start, 0)
        return 0

    lax.fori_loop(0, heads, work, 0)

    def home(h, _):
        def wait(d, _):
            come(h, d).wait()
            return 0

        lax.fori_loop(1, n, wait, 0)
        rows = dot(order[h], back[h].reshape(tok, 2 * e), (0, 0)).astype(jnp.bfloat16)
        cols = pl.ds(pl.multiple_of(h * e, e), e)
        acts[:tok, cols] = rows[:, :e]
        acts[tok:, cols] = rows[:, e:]
        return 0

    lax.fori_loop(0, heads, home, 0)
    load.wait()
    project(groups, group, core, mate, weight, acts, own, pair_send, pair_recv, far_send,
            far_recv, pair_sems, far_sems, out_ref)


def project(groups, group, core, mate, weight, acts, own, pair_send, pair_recv, far_send,
            far_recv, pair_sems, far_sems, out_ref):
    wide = out_ref.shape[1] // HALVES
    tile = min(256, wide)

    def product(block, half, store):
        def step(i, _):
            at = pl.multiple_of(i * tile, tile)
            first = (block * HALVES + half) * wide
            source = pl.ds(pl.multiple_of(first + at, tile), tile)
            store(pl.ds(at, tile), dot(acts[...], weight[:, source], (1, 0)))
            return 0

        lax.fori_loop(0, wide // tile, step, 0)

    def to_mate(i, k):
        return pltpu.make_async_remote_copy(
            src_ref=pair_send.at[i, k],
            dst_ref=pair_recv.at[i, k],
            send_sem=pair_sems.at[0, i, k],
            recv_sem=pair_sems.at[1, i, k],
            device_id={"tensor": mate},
            device_id_type=MESH,
        )

    def to_far(i, k):
        return pltpu.make_async_remote_copy(
            src_ref=far_send.at[i, k],
            dst_ref=far_recv.at[i, k],
            send_sem=far_sems.at[0, i, k],
            recv_sem=far_sems.at[1, i, k],
            device_id={"tensor": 2 * lax.rem(group + 1 + i, groups) + core},
            device_id_type=MESH,
        )

    last = groups - 1
    for i in range(groups):
        there = lax.rem(group + 1 + i, groups)
        for k in range(HALVES):

            def keep_pair(cols, value, i=i, k=k):
                pair_send[i, k, :, cols] = value.astype(jnp.bfloat16)

            product(2 * there + 1 - core, k, keep_pair)
            to_mate(i, k).start()
        for k in range(HALVES):

            def keep_own(cols, value, i=i, k=k):
                own[i, k, :, cols] = value

            product(2 * there + core, k, keep_own)
            if i < last:
                to_mate(i, k).wait()
                total = own[i, k] + pair_recv[i, k].astype(jnp.float32)
                far_send[i, k] = total.astype(jnp.bfloat16)
                to_far(i, k).start()
    for k in range(HALVES):
        to_mate(last, k).wait()
        own[last, k] = own[last, k] + pair_recv[last, k].astype(jnp.float32)
    for k in range(HALVES):
        total = own[last, k]
        for i in range(last):
            to_far(i, k).wait()
            total = total + far_recv[i, k].astype(jnp.float32)
        out_ref[:, k * wide : (k + 1) * wide] = total.astype(jnp.bfloat16)


def split_kernel(both_ref, out_ref, tan_ref):
    tok = out_ref.shape[0]
    out_ref[...] = both_ref[:tok]
    tan_ref[...] = both_ref[tok:]


def split(both):
    vmem = pl.BlockSpec(memory_space=pltpu.VMEM)
    shape = jax.ShapeDtypeStruct((both.shape[0] // 2, both.shape[1]), both.dtype)
    return pl.pallas_call(
        split_kernel, out_shape=(shape, shape), in_specs=[vmem], out_specs=(vmem, vmem)
    )(both)


def body(n, parts, q, k, v, dq, dk, dv, routes, weight):
    tok, heads = routes.shape
    e = HEAD_SIZE
    per = tok // n
    groups = parts // 2
    width = weight.shape[1] // parts
    half = jnp.bfloat16
    vmem = pl.BlockSpec(memory_space=pltpu.VMEM)
    dma = pltpu.SemaphoreType.DMA
    shape = jax.ShapeDtypeStruct((2 * tok, width), half)
    both = pl.pallas_call(
        functools.partial(kernel, n, parts),
        out_shape=shape,
        in_specs=[vmem] * 7 + [pl.BlockSpec(memory_space=pl.ANY)],
        out_specs=vmem,
        scratch_shapes=[
            pltpu.VMEM((heads, tok), jnp.float32),
            pltpu.VMEM((heads, tok, tok), half),
            pltpu.VMEM((heads, n, per, 6 * e), half),
            pltpu.VMEM((heads, n, per, 6 * e), half),
            pltpu.VMEM((heads, n, per, 2 * e), half),
            pltpu.VMEM((heads, n, per, 2 * e), half),
            pltpu.VMEM(weight.shape, half),
            pltpu.VMEM((2 * tok, heads * e), half),
            pltpu.VMEM((groups, HALVES, 2 * tok, width // HALVES), jnp.float32),
            pltpu.VMEM((groups, HALVES, 2 * tok, width // HALVES), half),
            pltpu.VMEM((groups, HALVES, 2 * tok, width // HALVES), half),
            pltpu.VMEM((max(groups - 1, 1), HALVES, 2 * tok, width // HALVES), half),
            pltpu.VMEM((max(groups - 1, 1), HALVES, 2 * tok, width // HALVES), half),
            dma,
            dma((heads, n)),
            dma((heads, n)),
            dma((heads, n)),
            dma((heads, n)),
            dma((2, groups, HALVES)),
            dma((2, max(groups - 1, 1), HALVES)),
        ],
        compiler_params=pltpu.CompilerParams(
            collective_id=0, has_side_effects=True, vmem_limit_bytes=56 * 2**20
        ),
    )(q, k, v, dq, dk, dv, routes.T, weight)
    return split(both)


LEVELS = 4
CUTS = 4


def soft_rows(query, keys, offset):
    e = HEAD_SIZE
    scale = e**-0.5
    shape = (query.shape[0], keys.shape[0])
    scores = dot(query[:, e:], keys[:, :e], (1, 1)) * scale
    tangent = dot(query, keys[:, : 2 * e], (1, 1)) * scale
    visible = (
        lax.broadcasted_iota(jnp.int32, shape, 1)
        <= lax.broadcasted_iota(jnp.int32, shape, 0) + offset
    )
    masked = jnp.where(visible, scores, -jnp.inf)
    top = jnp.max(masked, -1, keepdims=True)
    expo = jnp.exp(masked - top)
    total = jnp.sum(expo, -1, keepdims=True)
    probs = expo / total
    mean = jnp.sum(probs * tangent, -1, keepdims=True)
    slope = probs * (tangent - mean)
    both = dot(probs.astype(jnp.bfloat16), keys[:, 2 * e :], (1, 0))
    extra = dot(slope.astype(jnp.bfloat16), keys[:, 2 * e : 3 * e], (1, 0))
    rows = jnp.concatenate([both[:, :e], both[:, e:] + extra], 1)
    return rows, top + jnp.log(total), mean


def pack_stats(level, mean):
    lane = lax.broadcasted_iota(jnp.int32, (level.shape[0], 128), 1)
    return jnp.where(lane == 0, level, jnp.where(lane == 1, mean, 0.0))


def merge(pieces):
    e = HEAD_SIZE
    top = functools.reduce(jnp.maximum, [level for _, level, _ in pieces])
    weights = [jnp.exp(level - top) for _, level, _ in pieces]
    total = functools.reduce(jnp.add, weights)
    weights = [w / total for w in weights]
    mean = sum(w * m for w, (_, _, m) in zip(weights, pieces))
    value = sum(w * rows[:, :e] for w, (rows, _, _) in zip(weights, pieces))
    slope = sum(
        w * (rows[:, e:] + (m - mean) * rows[:, :e]) for w, (rows, _, m) in zip(weights, pieces)
    )
    return jnp.concatenate([value, slope], 1)


def level_kernel(
    parts,
    q_ref,
    k_ref,
    v_ref,
    dq_ref,
    dk_ref,
    dv_ref,
    routes_ref,
    weight_hbm,
    out_ref,
    dest,
    order,
    sent,
    rows_here,
    keys_in,
    query_in,
    piece_out,
    piece_in,
    stats_out,
    stats_in,
    own_piece,
    own_stats,
    result,
    back,
    weight,
    acts,
    own,
    pair_send,
    pair_recv,
    far_send,
    far_recv,
    weight_sem,
    side_sems,
    key_sems,
    query_sems,
    piece_sems,
    stats_sems,
    back_sems,
    pair_sems,
    far_sems,
):
    e = HEAD_SIZE
    tok, width = q_ref.shape
    heads = width // e
    n = 2 * LEVELS
    per = tok // n
    here = heads // 2
    steps = CUTS * here
    some = n // CUTS
    groups = parts // 2
    me = lax.axis_index("seq")
    mine = lax.axis_index("tensor")
    level, side = lax.div(me, 2), lax.rem(me, 2)
    group, core = lax.div(mine, 2), lax.rem(mine, 2)
    mate = 2 * group + 1 - core

    barrier = pltpu.get_barrier_semaphore()
    for d in range(1, LEVELS):
        peer = 2 * lax.rem(level + d, LEVELS) + side
        pl.semaphore_signal(barrier, inc=1, device_id={"seq": peer}, device_id_type=MESH)
    pl.semaphore_signal(
        barrier, inc=1, device_id={"seq": 2 * level + 1 - side}, device_id_type=MESH
    )
    pl.semaphore_signal(barrier, inc=1, device_id={"tensor": mate}, device_id_type=MESH)
    for d in range(1, groups):
        pl.semaphore_signal(
            barrier,
            inc=1,
            device_id={"tensor": 2 * lax.rem(group + d, groups) + core},
            device_id_type=MESH,
        )
    load = pltpu.make_async_copy(weight_hbm, weight, weight_sem)
    load.start()

    row_at = lax.broadcasted_iota(jnp.int32, (tok, tok), 0)
    earlier = (row_at < lax.broadcasted_iota(jnp.int32, (tok, tok), 1)).astype(jnp.float32)
    earlier = earlier.astype(jnp.bfloat16)
    cluster = lax.broadcasted_iota(jnp.int32, (n, tok), 0)
    dest[...] = jnp.right_shift(routes_ref[...], tok.bit_length() - 1).astype(jnp.float32)

    def place(h):
        member = (dest[pl.ds(h, 1), :] == cluster.astype(jnp.float32)).astype(jnp.float32)
        rank = dot(member.astype(jnp.bfloat16), earlier, (1, 0))
        at = jnp.sum(member * (rank + (per * cluster).astype(jnp.float32)), 0, keepdims=True)
        order[h] = (row_at.astype(jnp.float32) == at).astype(jnp.float32).astype(jnp.bfloat16)

    place((1 - side) * here)
    pl.semaphore_wait(barrier, LEVELS + groups)

    def remote(src, dst, sems, at, device):
        return pltpu.make_async_remote_copy(
            src_ref=src,
            dst_ref=dst,
            send_sem=sems.at[(0, *at)],
            recv_sem=sems.at[(1, *at)],
            device_id=device,
            device_id_type=MESH,
        )

    across = {"seq": 2 * level + 1 - side}

    def at_level(z):
        return {"seq": 2 * z + side}

    def side_copy(c):
        return remote(sent.at[c], rows_here.at[c, side], side_sems, (c,), across)

    def key_copy(c):
        keys = rows_here.at[c, :, :, :, pl.ds(2 * e, 4 * e)]
        return remote(keys, keys_in.at[c], key_sems, (c,), at_level(1))

    def query_copy(slot, c, z):
        queries = rows_here.at[c, :, :, :, pl.ds(0, 2 * e)]
        return remote(queries, query_in.at[slot, c], query_sems, (slot, c), at_level(z))

    def piece_copies(slot, c, z):
        return (
            remote(piece_out.at[slot, c], piece_in.at[slot, c], piece_sems, (slot, c), at_level(z)),
            remote(stats_out.at[slot, c], stats_in.at[slot, c], stats_sems, (slot, c), at_level(z)),
        )

    def back_copy(c):
        return remote(result.at[c, 1 - side], back.at[c], back_sems, (c,), across)

    def placed(h, c):
        cols = pl.ds(pl.multiple_of(h * e, e), e)
        rows = jnp.concatenate(
            [r[:, cols] for r in (dq_ref, q_ref, k_ref, dk_ref, v_ref, dv_ref)], 1
        )
        size = tok // CUTS
        cut = pl.ds(pl.multiple_of(lax.rem(c, CUTS) * size, size), size)
        moved = dot(order[h, cut, :], rows, (1, 0)).astype(jnp.bfloat16)
        return moved.reshape(some, per, 6 * e)

    def scatter(c, _):
        sent[c] = placed((1 - side) * here + lax.div(c, CUTS), c)
        side_copy(c).start()
        return 0

    lax.fori_loop(0, CUTS, scatter, 0)
    place(side * here)

    def pair_of(ref, i):
        return jnp.concatenate([ref[0, i], ref[1, i]], 0)

    def finish(c, i, rows):
        rows = rows.astype(jnp.bfloat16)
        result[c, 0, i] = rows[:per]
        result[c, 1, i] = rows[per:]

    def hand_on(slot, c, z, parts_of):
        for i, (rows, _, _) in enumerate(parts_of):
            piece_out[slot, c, i] = rows.astype(jnp.bfloat16)
        packed = pack_stats(
            jnp.concatenate([p[1] for p in parts_of], 0),
            jnp.concatenate([p[2] for p in parts_of], 0),
        )
        stats_out[slot, c] = packed.T[:8]
        for copy in piece_copies(slot, c, z):
            copy.start()

    def keep(c, parts_of):
        own_piece[c] = jnp.concatenate([p[0] for p in parts_of], 0)
        own_stats[c] = pack_stats(
            jnp.concatenate([p[1] for p in parts_of], 0),
            jnp.concatenate([p[2] for p in parts_of], 0),
        )

    def advance(c):
        rows_here[c, side] = placed(side * here + lax.div(c, CUTS), c)
        side_copy(c).wait_recv()

        @pl.when(level == 0)
        def _():
            key_copy(c).start()

        @pl.when(level == 2)
        def _():
            query_copy(0, c, 1).start()

        @pl.when(level == 3)
        def _():
            query_copy(0, c, 2).start()
            query_copy(1, c, 1).start()

    def work(c):
        own_rows = rows_here.at[c]
        size = 2 * per

        def cut(piece, j):
            return tuple(x[j * size : (j + 1) * size] for x in piece)

        @pl.when(level == 0)
        def _():
            for i in range(some):
                rows = pair_of(own_rows, i)
                finish(c, i, soft_rows(rows[:, : 2 * e], rows[:, 2 * e :], 0)[0])
            back_copy(c).start()

        @pl.when(level == 1)
        def _():
            key_copy(c).wait_recv()
            query_copy(0, c, 1).wait_recv()
            query_copy(1, c, 1).wait_recv()
            pieces = []
            for i in range(some):
                rows = pair_of(own_rows, i)
                queries = jnp.concatenate(
                    [
                        rows[:, : 2 * e],
                        pair_of(query_in.at[0, c], i),
                        pair_of(query_in.at[1, c], i),
                    ],
                    0,
                )
                keys = jnp.concatenate([pair_of(keys_in.at[c], i), rows[:, 2 * e :]], 0)
                pieces.append(soft_rows(queries, keys, size))
            hand_on(1, c, 3, [cut(p, 2) for p in pieces])
            hand_on(0, c, 2, [cut(p, 1) for p in pieces])
            for i in range(some):
                finish(c, i, pieces[i][0][:size])
            back_copy(c).start()

        @pl.when(level == 2)
        def _():
            query_copy(0, c, 1).wait_recv()
            pieces = []
            for i in range(some):
                rows = pair_of(own_rows, i)
                queries = jnp.concatenate([rows[:, : 2 * e], pair_of(query_in.at[0, c], i)], 0)
                pieces.append(soft_rows(queries, rows[:, 2 * e :], 0))
            hand_on(0, c, 3, [cut(p, 1) for p in pieces])
            keep(c, [cut(p, 0) for p in pieces])

        @pl.when(level == 3)
        def _():
            pieces = []
            for i in range(some):
                rows = pair_of(own_rows, i)
                pieces.append(soft_rows(rows[:, : 2 * e], rows[:, 2 * e :], 0))
            keep(c, pieces)

    def to_acts(h, rows):
        rows = dot(order[h], rows, (0, 0)).astype(jnp.bfloat16)
        cols = pl.ds(pl.multiple_of(h * e, e), e)
        acts[:tok, cols] = rows[:, :e]
        acts[tok:, cols] = rows[:, e:]

    def home(j, _):
        def whole(at):
            return jnp.concatenate(
                [at(CUTS * j + p).reshape(tok // CUTS, 2 * e) for p in range(CUTS)], 0
            )

        to_acts(side * here + j, whole(lambda c: result[c, side]))
        for p in range(CUTS):
            back_copy(CUTS * j + p).wait_recv()
        to_acts((1 - side) * here + j, whole(lambda c: back[c]))
        return 0

    def gather(c, slots):
        pieces = [(own_piece[c], own_stats[c, :, 0:1], own_stats[c, :, 1:2])]
        for slot in slots:
            for copy in piece_copies(slot, c, 2):
                copy.wait_recv()
            stats = stats_in[slot, c]
            stats = jnp.concatenate([stats, jnp.zeros((120, stats.shape[1]), jnp.float32)], 0).T
            rows = piece_in[slot, c].reshape(some * 2 * per, 2 * e).astype(jnp.float32)
            pieces.append((rows, stats[:, 0:1], stats[:, 1:2]))
        rows = merge(pieces)
        for i in range(some):
            finish(c, i, rows[i * 2 * per : (i + 1) * 2 * per])
        back_copy(c).start()

    def collect(c):
        @pl.when(level == 2)
        def _():
            gather(c, (0,))

        @pl.when(level == 3)
        def _():
            gather(c, (0, 1))

    ahead, lag = 2, CUTS
    for c in range(ahead):
        advance(c)

    def feed(j, _):
        place((1 - side) * here + j)
        lax.fori_loop(CUTS * j, CUTS * (j + 1), scatter, 0)
        place(side * here + j)
        return 0

    lax.fori_loop(1, here, feed, 0)

    def turn(c, _):
        @pl.when(c + ahead < steps)
        def _():
            advance(c + ahead)

        work(c)

        @pl.when(c >= lag)
        def _():
            collect(c - lag)

        return 0

    lax.fori_loop(0, steps, turn, 0)
    lax.fori_loop(0, here - 1, home, 0)

    def rest(c, _):
        collect(c)
        return 0

    lax.fori_loop(steps - lag, steps, rest, 0)
    home(here - 1, 0)
    load.wait()
    project(groups, group, core, mate, weight, acts, own, pair_send, pair_recv, far_send,
            far_recv, pair_sems, far_sems, out_ref)

    def drain(c, _):
        side_copy(c).wait_send()
        back_copy(c).wait_send()

        @pl.when(level == 0)
        def _():
            key_copy(c).wait_send()

        @pl.when(level == 1)
        def _():
            for slot in (0, 1):
                for copy in piece_copies(slot, c, 2 + slot):
                    copy.wait_send()

        @pl.when(level == 2)
        def _():
            query_copy(0, c, 1).wait_send()
            for copy in piece_copies(0, c, 3):
                copy.wait_send()

        @pl.when(level == 3)
        def _():
            query_copy(0, c, 2).wait_send()
            query_copy(1, c, 1).wait_send()

        return 0

    lax.fori_loop(0, steps, drain, 0)


def level_body(parts, q, k, v, dq, dk, dv, routes, weight):
    tok, heads = routes.shape
    e = HEAD_SIZE
    n = 2 * LEVELS
    per = tok // n
    steps = CUTS * (heads // 2)
    some = n // CUTS
    rows = some * 2 * per
    groups = parts // 2
    width = weight.shape[1] // parts
    half = jnp.bfloat16
    vmem = pl.BlockSpec(memory_space=pltpu.VMEM)
    dma = pltpu.SemaphoreType.DMA
    shape = jax.ShapeDtypeStruct((2 * tok, width), half)
    both = pl.pallas_call(
        functools.partial(level_kernel, parts),
        out_shape=shape,
        in_specs=[vmem] * 7 + [pl.BlockSpec(memory_space=pl.ANY)],
        out_specs=vmem,
        scratch_shapes=[
            pltpu.VMEM((heads, tok), jnp.float32),
            pltpu.VMEM((heads, tok, tok), half),
            pltpu.VMEM((steps, some, per, 6 * e), half),
            pltpu.VMEM((steps, 2, some, per, 6 * e), half),
            pltpu.VMEM((steps, 2, some, per, 4 * e), half),
            pltpu.VMEM((2, steps, 2, some, per, 2 * e), half),
            pltpu.VMEM((2, steps, some, 2 * per, 2 * e), half),
            pltpu.VMEM((2, steps, some, 2 * per, 2 * e), half),
            pltpu.VMEM((2, steps, 8, rows), jnp.float32),
            pltpu.VMEM((2, steps, 8, rows), jnp.float32),
            pltpu.VMEM((steps, rows, 2 * e), jnp.float32),
            pltpu.VMEM((steps, rows, 128), jnp.float32),
            pltpu.VMEM((steps, 2, some, per, 2 * e), half),
            pltpu.VMEM((steps, some, per, 2 * e), half),
            pltpu.VMEM(weight.shape, half),
            pltpu.VMEM((2 * tok, heads * e), half),
            pltpu.VMEM((groups, HALVES, 2 * tok, width // HALVES), jnp.float32),
            pltpu.VMEM((groups, HALVES, 2 * tok, width // HALVES), half),
            pltpu.VMEM((groups, HALVES, 2 * tok, width // HALVES), half),
            pltpu.VMEM((max(groups - 1, 1), HALVES, 2 * tok, width // HALVES), half),
            pltpu.VMEM((max(groups - 1, 1), HALVES, 2 * tok, width // HALVES), half),
            dma,
            dma((2, steps)),
            dma((2, steps)),
            dma((2, 2, steps)),
            dma((2, 2, steps)),
            dma((2, 2, steps)),
            dma((2, steps)),
            dma((2, groups, HALVES)),
            dma((2, max(groups - 1, 1), HALVES)),
        ],
        compiler_params=pltpu.CompilerParams(
            collective_id=1, has_side_effects=True, vmem_limit_bytes=58 * 2**20
        ),
    )(q, k, v, dq, dk, dv, routes.T, weight)
    return split(both)


def solution(mesh):
    n, parts = mesh.shape["seq"], mesh.shape["tensor"]

    def run(*args):
        if n == 2 * LEVELS and args[6].shape[1] % 2 == 0:
            return level_body(parts, *args)
        return body(n, parts, *args)

    return jax.shard_map(
        run,
        mesh=mesh,
        in_specs=(P("seq", "tensor"),) * 7 + (P("tensor", None),),
        out_specs=(P("seq", "tensor"), P("seq", "tensor")),
        check_vma=False,
    )
```

```python
import functools

import jax
import jax.numpy as jnp
from jax import lax
from jax.experimental import pallas as pl
from jax.experimental.pallas import tpu as pltpu
from jax.sharding import PartitionSpec as P

HEAD_SIZE = 128
MESH = pl.DeviceIdType.MESH
HALVES = 2


def dot(a, b, contract):
    return lax.dot_general(
        a, b, (((contract[0],), (contract[1],)), ((), ())), preferred_element_type=jnp.float32
    )


def attend(rows):
    e = HEAD_SIZE
    scale = e**-0.5
    count = rows.shape[0]
    query, key = rows[:, e : 2 * e], rows[:, 2 * e : 3 * e]
    scores = dot(query, key, (1, 1)) * scale
    tangent = dot(rows[:, : 2 * e], rows[:, 2 * e : 4 * e], (1, 1)) * scale
    visible = lax.broadcasted_iota(jnp.int32, (count, count), 1) <= lax.broadcasted_iota(
        jnp.int32, (count, count), 0
    )
    masked = jnp.where(visible, scores, -jnp.inf)
    expo = jnp.exp(masked - jnp.max(masked, -1, keepdims=True))
    probs = expo / jnp.sum(expo, -1, keepdims=True)
    slope = probs * (tangent - jnp.sum(probs * tangent, -1, keepdims=True))
    both = dot(probs.astype(jnp.bfloat16), rows[:, 4 * e :], (1, 0))
    extra = dot(slope.astype(jnp.bfloat16), rows[:, 4 * e : 5 * e], (1, 0))
    return jnp.concatenate([both[:, :e], both[:, e:] + extra], 1).astype(jnp.bfloat16)


def kernel(
    n,
    parts,
    q_ref,
    k_ref,
    v_ref,
    dq_ref,
    dk_ref,
    dv_ref,
    routes_ref,
    weight_hbm,
    out_ref,
    dest,
    order,
    sent,
    got,
    result,
    back,
    weight,
    acts,
    own,
    pair_send,
    pair_recv,
    far_send,
    far_recv,
    weight_sem,
    go_send,
    go_recv,
    back_send,
    back_recv,
    pair_sems,
    far_sems,
):
    e = HEAD_SIZE
    tok, width = q_ref.shape
    heads = width // e
    per = tok // n
    groups = parts // 2
    me = lax.axis_index("seq")
    mine = lax.axis_index("tensor")
    group, core = lax.div(mine, 2), lax.rem(mine, 2)
    mate = 2 * group + 1 - core

    barrier = pltpu.get_barrier_semaphore()
    for d in range(1, n):
        pl.semaphore_signal(
            barrier, inc=1, device_id={"seq": lax.rem(me + d, n)}, device_id_type=MESH
        )
    pl.semaphore_signal(barrier, inc=1, device_id={"tensor": mate}, device_id_type=MESH)
    for d in range(1, groups):
        pl.semaphore_signal(
            barrier,
            inc=1,
            device_id={"tensor": 2 * lax.rem(group + d, groups) + core},
            device_id_type=MESH,
        )
    load = pltpu.make_async_copy(weight_hbm, weight, weight_sem)
    load.start()

    row_at = lax.broadcasted_iota(jnp.int32, (tok, tok), 0)
    earlier = (row_at < lax.broadcasted_iota(jnp.int32, (tok, tok), 1)).astype(jnp.float32)
    earlier = earlier.astype(jnp.bfloat16)
    cluster = lax.broadcasted_iota(jnp.int32, (n, tok), 0)
    dest[...] = jnp.right_shift(routes_ref[...], tok.bit_length() - 1).astype(jnp.float32)

    def place(h, _):
        member = (dest[pl.ds(h, 1), :] == cluster.astype(jnp.float32)).astype(jnp.float32)
        rank = dot(member.astype(jnp.bfloat16), earlier, (1, 0))
        at = jnp.sum(member * (rank + (per * cluster).astype(jnp.float32)), 0, keepdims=True)
        order[h] = (row_at.astype(jnp.float32) == at).astype(jnp.float32).astype(jnp.bfloat16)
        return 0

    lax.fori_loop(0, heads, place, 0)
    pl.semaphore_wait(barrier, n - 1 + groups)

    def go(h, d):
        peer = lax.rem(me + d, n)
        return pltpu.make_async_remote_copy(
            src_ref=sent.at[h, peer],
            dst_ref=got.at[h, me],
            send_sem=go_send.at[h, d],
            recv_sem=go_recv.at[h, d],
            device_id={"seq": peer},
            device_id_type=MESH,
        )

    def come(h, d):
        peer = lax.rem(me + d, n)
        return pltpu.make_async_remote_copy(
            src_ref=result.at[h, peer],
            dst_ref=back.at[h, me],
            send_sem=back_send.at[h, d],
            recv_sem=back_recv.at[h, d],
            device_id={"seq": peer},
            device_id_type=MESH,
        )

    def scatter(h, _):
        cols = pl.ds(pl.multiple_of(h * e, e), e)
        rows = jnp.concatenate(
            [r[:, cols] for r in (dq_ref, q_ref, k_ref, dk_ref, v_ref, dv_ref)], 1
        )
        placed = dot(order[h], rows, (1, 0)).astype(jnp.bfloat16)
        sent[h] = placed.reshape(n, per, 6 * e)
        got[h, me] = sent[h, me]

        def start(d, _):
            go(h, d).start()
            return 0

        lax.fori_loop(1, n, start, 0)
        return 0

    lax.fori_loop(0, heads, scatter, 0)

    def work(h, _):
        def wait(d, _):
            go(h, d).wait()
            return 0

        lax.fori_loop(1, n, wait, 0)
        result[h] = attend(got[h].reshape(tok, 6 * e)).reshape(n, per, 2 * e)
        back[h, me] = result[h, me]

        def start(d, _):
            come(h, d).start()
            return 0

        lax.fori_loop(1, n, start, 0)
        return 0

    lax.fori_loop(0, heads, work, 0)

    def home(h, _):
        def wait(d, _):
            come(h, d).wait()
            return 0

        lax.fori_loop(1, n, wait, 0)
        rows = dot(order[h], back[h].reshape(tok, 2 * e), (0, 0)).astype(jnp.bfloat16)
        cols = pl.ds(pl.multiple_of(h * e, e), e)
        acts[:tok, cols] = rows[:, :e]
        acts[tok:, cols] = rows[:, e:]
        return 0

    lax.fori_loop(0, heads, home, 0)
    load.wait()
    project(groups, group, core, mate, weight, acts, own, pair_send, pair_recv, far_send,
            far_recv, pair_sems, far_sems, out_ref)


def project(groups, group, core, mate, weight, acts, own, pair_send, pair_recv, far_send,
            far_recv, pair_sems, far_sems, out_ref):
    wide = out_ref.shape[1] // HALVES
    tile = min(256, wide)

    def product(block, half, store):
        def step(i, _):
            at = pl.multiple_of(i * tile, tile)
            first = (block * HALVES + half) * wide
            source = pl.ds(pl.multiple_of(first + at, tile), tile)
            store(pl.ds(at, tile), dot(acts[...], weight[:, source], (1, 0)))
            return 0

        lax.fori_loop(0, wide // tile, step, 0)

    def to_mate(i, k):
        return pltpu.make_async_remote_copy(
            src_ref=pair_send.at[i, k],
            dst_ref=pair_recv.at[i, k],
            send_sem=pair_sems.at[0, i, k],
            recv_sem=pair_sems.at[1, i, k],
            device_id={"tensor": mate},
            device_id_type=MESH,
        )

    def to_far(i, k):
        return pltpu.make_async_remote_copy(
            src_ref=far_send.at[i, k],
            dst_ref=far_recv.at[i, k],
            send_sem=far_sems.at[0, i, k],
            recv_sem=far_sems.at[1, i, k],
            device_id={"tensor": 2 * lax.rem(group + 1 + i, groups) + core},
            device_id_type=MESH,
        )

    last = groups - 1
    for i in range(groups):
        there = lax.rem(group + 1 + i, groups)
        for k in range(HALVES):

            def keep_pair(cols, value, i=i, k=k):
                pair_send[i, k, :, cols] = value.astype(jnp.bfloat16)

            product(2 * there + 1 - core, k, keep_pair)
            to_mate(i, k).start()
        for k in range(HALVES):

            def keep_own(cols, value, i=i, k=k):
                own[i, k, :, cols] = value

            product(2 * there + core, k, keep_own)
            if i < last:
                to_mate(i, k).wait()
                total = own[i, k] + pair_recv[i, k].astype(jnp.float32)
                far_send[i, k] = total.astype(jnp.bfloat16)
                to_far(i, k).start()
    for k in range(HALVES):
        to_mate(last, k).wait()
        own[last, k] = own[last, k] + pair_recv[last, k].astype(jnp.float32)
    for k in range(HALVES):
        total = own[last, k]
        for i in range(last):
            to_far(i, k).wait()
            total = total + far_recv[i, k].astype(jnp.float32)
        out_ref[:, k * wide : (k + 1) * wide] = total.astype(jnp.bfloat16)


def split_kernel(both_ref, out_ref, tan_ref):
    tok = out_ref.shape[0]
    out_ref[...] = both_ref[:tok]
    tan_ref[...] = both_ref[tok:]


def split(both):
    vmem = pl.BlockSpec(memory_space=pltpu.VMEM)
    shape = jax.ShapeDtypeStruct((both.shape[0] // 2, both.shape[1]), both.dtype)
    return pl.pallas_call(
        split_kernel, out_shape=(shape, shape), in_specs=[vmem], out_specs=(vmem, vmem)
    )(both)


def body(n, parts, q, k, v, dq, dk, dv, routes, weight):
    tok, heads = routes.shape
    e = HEAD_SIZE
    per = tok // n
    groups = parts // 2
    width = weight.shape[1] // parts
    half = jnp.bfloat16
    vmem = pl.BlockSpec(memory_space=pltpu.VMEM)
    dma = pltpu.SemaphoreType.DMA
    shape = jax.ShapeDtypeStruct((2 * tok, width), half)
    both = pl.pallas_call(
        functools.partial(kernel, n, parts),
        out_shape=shape,
        in_specs=[vmem] * 7 + [pl.BlockSpec(memory_space=pl.ANY)],
        out_specs=vmem,
        scratch_shapes=[
            pltpu.VMEM((heads, tok), jnp.float32),
            pltpu.VMEM((heads, tok, tok), half),
            pltpu.VMEM((heads, n, per, 6 * e), half),
            pltpu.VMEM((heads, n, per, 6 * e), half),
            pltpu.VMEM((heads, n, per, 2 * e), half),
            pltpu.VMEM((heads, n, per, 2 * e), half),
            pltpu.VMEM(weight.shape, half),
            pltpu.VMEM((2 * tok, heads * e), half),
            pltpu.VMEM((groups, HALVES, 2 * tok, width // HALVES), jnp.float32),
            pltpu.VMEM((groups, HALVES, 2 * tok, width // HALVES), half),
            pltpu.VMEM((groups, HALVES, 2 * tok, width // HALVES), half),
            pltpu.VMEM((max(groups - 1, 1), HALVES, 2 * tok, width // HALVES), half),
            pltpu.VMEM((max(groups - 1, 1), HALVES, 2 * tok, width // HALVES), half),
            dma,
            dma((heads, n)),
            dma((heads, n)),
            dma((heads, n)),
            dma((heads, n)),
            dma((2, groups, HALVES)),
            dma((2, max(groups - 1, 1), HALVES)),
        ],
        compiler_params=pltpu.CompilerParams(
            collective_id=0, has_side_effects=True, vmem_limit_bytes=56 * 2**20
        ),
    )(q, k, v, dq, dk, dv, routes.T, weight)
    return split(both)


LEVELS = 4
CUTS = 4


def soft_rows(query, keys, offset):
    e = HEAD_SIZE
    scale = e**-0.5
    shape = (query.shape[0], keys.shape[0])
    scores = dot(query[:, e:], keys[:, :e], (1, 1)) * scale
    tangent = dot(query, keys[:, : 2 * e], (1, 1)) * scale
    visible = (
        lax.broadcasted_iota(jnp.int32, shape, 1)
        <= lax.broadcasted_iota(jnp.int32, shape, 0) + offset
    )
    masked = jnp.where(visible, scores, -jnp.inf)
    top = jnp.max(masked, -1, keepdims=True)
    expo = jnp.exp(masked - top)
    total = jnp.sum(expo, -1, keepdims=True)
    probs = expo / total
    mean = jnp.sum(probs * tangent, -1, keepdims=True)
    slope = probs * (tangent - mean)
    both = dot(probs.astype(jnp.bfloat16), keys[:, 2 * e :], (1, 0))
    extra = dot(slope.astype(jnp.bfloat16), keys[:, 2 * e : 3 * e], (1, 0))
    rows = jnp.concatenate([both[:, :e], both[:, e:] + extra], 1)
    return rows, top + jnp.log(total), mean


def pack_stats(level, mean):
    lane = lax.broadcasted_iota(jnp.int32, (level.shape[0], 128), 1)
    return jnp.where(lane == 0, level, jnp.where(lane == 1, mean, 0.0))


def merge(pieces):
    e = HEAD_SIZE
    top = functools.reduce(jnp.maximum, [level for _, level, _ in pieces])
    weights = [jnp.exp(level - top) for _, level, _ in pieces]
    total = functools.reduce(jnp.add, weights)
    weights = [w / total for w in weights]
    mean = sum(w * m for w, (_, _, m) in zip(weights, pieces))
    value = sum(w * rows[:, :e] for w, (rows, _, _) in zip(weights, pieces))
    slope = sum(
        w * (rows[:, e:] + (m - mean) * rows[:, :e]) for w, (rows, _, m) in zip(weights, pieces)
    )
    return jnp.concatenate([value, slope], 1)


def level_kernel(
    parts,
    q_ref,
    k_ref,
    v_ref,
    dq_ref,
    dk_ref,
    dv_ref,
    routes_ref,
    weight_hbm,
    out_ref,
    dest,
    order,
    sent,
    rows_here,
    keys_in,
    query_in,
    piece_out,
    piece_in,
    stats_out,
    stats_in,
    own_piece,
    own_stats,
    result,
    back,
    weight_early,
    weight_late,
    acts_early,
    acts_late,
    own,
    pair_send,
    pair_recv,
    far_send,
    far_recv,
    early_sems,
    late_sems,
    weight_sems,
    acts_sems,
    side_sems,
    key_sems,
    query_sems,
    piece_sems,
    stats_sems,
    back_sems,
    pair_sems,
    far_sems,
):
    e = HEAD_SIZE
    tok, width = q_ref.shape
    heads = width // e
    n = 2 * LEVELS
    per = tok // n
    here = heads // 2
    steps = CUTS * here
    some = n // CUTS
    groups = parts // 2
    me = lax.axis_index("seq")
    mine = lax.axis_index("tensor")
    level, side = lax.div(me, 2), lax.rem(me, 2)
    group, core = lax.div(mine, 2), lax.rem(mine, 2)
    mate = 2 * group + 1 - core


    def tensor_peer(slot):
        which = core if slot % 2 == 0 else 1 - core
        return 2 * lax.rem(group + slot // 2, groups) + which

    barrier = pltpu.get_barrier_semaphore()
    for d in range(1, LEVELS):
        peer = 2 * lax.rem(level + d, LEVELS) + side
        pl.semaphore_signal(barrier, inc=1, device_id={"seq": peer}, device_id_type=MESH)
    pl.semaphore_signal(
        barrier, inc=1, device_id={"seq": 2 * level + 1 - side}, device_id_type=MESH
    )
    for slot in range(1, parts):
        pl.semaphore_signal(
            barrier, inc=1, device_id={"tensor": tensor_peer(slot)}, device_id_type=MESH
        )
    early, last = here - 1, groups - 1
    sides = (0, 1)
    loads = [
        pltpu.make_async_copy(
            weight_hbm.at[pl.ds((w * here + j) * e, e), :],
            weight_early.at[pl.ds((2 * j + w) * e, e), :],
            early_sems.at[2 * j + w],
        )
        for j in range(early)
        for w in sides
    ]

    def late_weight(w, block):
        rows = pl.ds((w * here + early) * e, e)
        return weight_hbm.at[rows, pl.ds(pl.multiple_of(block * width, width), width)]

    late_loads = [
        pltpu.make_async_copy(
            late_weight(w, mine), weight_late.at[0, pl.ds(w * e, e), :], late_sems.at[w]
        )
        for w in sides
    ]
    for load in loads + late_loads:
        load.start()

    row_at = lax.broadcasted_iota(jnp.int32, (tok, tok), 0)
    earlier = (row_at < lax.broadcasted_iota(jnp.int32, (tok, tok), 1)).astype(jnp.float32)
    earlier = earlier.astype(jnp.bfloat16)
    cluster = lax.broadcasted_iota(jnp.int32, (n, tok), 0)
    dest[...] = jnp.right_shift(routes_ref[...], tok.bit_length() - 1).astype(jnp.float32)

    def place(h):
        member = (dest[pl.ds(h, 1), :] == cluster.astype(jnp.float32)).astype(jnp.float32)
        rank = dot(member.astype(jnp.bfloat16), earlier, (1, 0))
        at = jnp.sum(member * (rank + (per * cluster).astype(jnp.float32)), 0, keepdims=True)
        order[h] = (row_at.astype(jnp.float32) == at).astype(jnp.float32).astype(jnp.bfloat16)

    place((1 - side) * here)
    pl.semaphore_wait(barrier, LEVELS + parts - 1)

    def remote(src, dst, sems, at, device):
        return pltpu.make_async_remote_copy(
            src_ref=src,
            dst_ref=dst,
            send_sem=sems.at[(0, *at)],
            recv_sem=sems.at[(1, *at)],
            device_id=device,
            device_id_type=MESH,
        )

    across = {"seq": 2 * level + 1 - side}

    def at_level(z):
        return {"seq": 2 * z + side}

    def side_copy(c):
        return remote(sent.at[c], rows_here.at[c, side], side_sems, (c,), across)

    def key_copy(c):
        keys = rows_here.at[c, :, :, :, pl.ds(2 * e, 4 * e)]
        return remote(keys, keys_in.at[c], key_sems, (c,), at_level(1))

    def query_copy(slot, c, z):
        queries = rows_here.at[c, :, :, :, pl.ds(0, 2 * e)]
        return remote(queries, query_in.at[slot, c], query_sems, (slot, c), at_level(z))

    def piece_copies(slot, c, z):
        return (
            remote(piece_out.at[slot, c], piece_in.at[slot, c], piece_sems, (slot, c), at_level(z)),
            remote(stats_out.at[slot, c], stats_in.at[slot, c], stats_sems, (slot, c), at_level(z)),
        )

    def back_copy(c):
        return remote(result.at[c, 1 - side], back.at[c], back_sems, (c,), across)

    def placed(h, c):
        cols = pl.ds(pl.multiple_of(h * e, e), e)
        rows = jnp.concatenate(
            [r[:, cols] for r in (dq_ref, q_ref, k_ref, dk_ref, v_ref, dv_ref)], 1
        )
        size = tok // CUTS
        cut = pl.ds(pl.multiple_of(lax.rem(c, CUTS) * size, size), size)
        moved = dot(order[h, cut, :], rows, (1, 0)).astype(jnp.bfloat16)
        return moved.reshape(some, per, 6 * e)

    def scatter(c, _):
        sent[c] = placed((1 - side) * here + lax.div(c, CUTS), c)
        side_copy(c).start()
        return 0

    lax.fori_loop(0, CUTS, scatter, 0)
    place(side * here)

    def weight_copy(slot, w):
        peer = tensor_peer(slot)
        dst = weight_late.at[slot, pl.ds(w * e, e), :]
        return remote(late_weight(w, peer), dst, weight_sems, (slot, w), {"tensor": peer})

    def acts_copy(slot):
        device = {"tensor": tensor_peer(slot)}
        return remote(acts_late.at[0], acts_late.at[slot], acts_sems, (slot,), device)

    def forward(slot):
        device = {"tensor": mate}
        return remote(acts_late.at[slot], acts_late.at[slot + 1], acts_sems, (slot + 1,), device)

    for slot in range(1, parts):
        for w in sides:
            weight_copy(slot, w).start()

    def pair_of(ref, i):
        return jnp.concatenate([ref[0, i], ref[1, i]], 0)

    def finish(c, i, rows):
        rows = rows.astype(jnp.bfloat16)
        result[c, 0, i] = rows[:per]
        result[c, 1, i] = rows[per:]

    def hand_on(slot, c, z, parts_of):
        for i, (rows, _, _) in enumerate(parts_of):
            piece_out[slot, c, i] = rows.astype(jnp.bfloat16)
        packed = pack_stats(
            jnp.concatenate([p[1] for p in parts_of], 0),
            jnp.concatenate([p[2] for p in parts_of], 0),
        )
        stats_out[slot, c] = packed.T[:8]
        for copy in piece_copies(slot, c, z):
            copy.start()

    def keep(c, parts_of):
        own_piece[c] = jnp.concatenate([p[0] for p in parts_of], 0)
        own_stats[c] = pack_stats(
            jnp.concatenate([p[1] for p in parts_of], 0),
            jnp.concatenate([p[2] for p in parts_of], 0),
        )

    def advance(c):
        rows_here[c, side] = placed(side * here + lax.div(c, CUTS), c)
        side_copy(c).wait_recv()

        @pl.when(level == 0)
        def _():
            key_copy(c).start()

        @pl.when(level == 2)
        def _():
            query_copy(0, c, 1).start()

        @pl.when(level == 3)
        def _():
            query_copy(0, c, 2).start()
            query_copy(1, c, 1).start()

    def work(c):
        own_rows = rows_here.at[c]
        size = 2 * per

        def cut(piece, j):
            return tuple(x[j * size : (j + 1) * size] for x in piece)

        @pl.when(level == 0)
        def _():
            for i in range(some):
                rows = pair_of(own_rows, i)
                finish(c, i, soft_rows(rows[:, : 2 * e], rows[:, 2 * e :], 0)[0])
            back_copy(c).start()

        @pl.when(level == 1)
        def _():
            key_copy(c).wait_recv()
            query_copy(0, c, 1).wait_recv()
            query_copy(1, c, 1).wait_recv()
            pieces = []
            for i in range(some):
                rows = pair_of(own_rows, i)
                queries = jnp.concatenate(
                    [
                        rows[:, : 2 * e],
                        pair_of(query_in.at[0, c], i),
                        pair_of(query_in.at[1, c], i),
                    ],
                    0,
                )
                keys = jnp.concatenate([pair_of(keys_in.at[c], i), rows[:, 2 * e :]], 0)
                pieces.append(soft_rows(queries, keys, size))
            hand_on(1, c, 3, [cut(p, 2) for p in pieces])
            hand_on(0, c, 2, [cut(p, 1) for p in pieces])
            for i in range(some):
                finish(c, i, pieces[i][0][:size])
            back_copy(c).start()

        @pl.when(level == 2)
        def _():
            query_copy(0, c, 1).wait_recv()
            pieces = []
            for i in range(some):
                rows = pair_of(own_rows, i)
                queries = jnp.concatenate([rows[:, : 2 * e], pair_of(query_in.at[0, c], i)], 0)
                pieces.append(soft_rows(queries, rows[:, 2 * e :], 0))
            hand_on(0, c, 3, [cut(p, 1) for p in pieces])
            keep(c, [cut(p, 0) for p in pieces])

        @pl.when(level == 3)
        def _():
            pieces = []
            for i in range(some):
                rows = pair_of(own_rows, i)
                pieces.append(soft_rows(rows[:, : 2 * e], rows[:, 2 * e :], 0))
            keep(c, pieces)

    def home(j, put):
        def whole(at):
            return jnp.concatenate(
                [at(CUTS * j + p).reshape(tok // CUTS, 2 * e) for p in range(CUTS)], 0
            )

        def back_home(w, rows):
            rows = dot(order[w * here + j], rows, (0, 0)).astype(jnp.bfloat16)
            put(w, rows[:, :e], rows[:, e:])

        back_home(side, whole(lambda c: result[c, side]))
        for p in range(CUTS):
            back_copy(CUTS * j + p).wait_recv()
        back_home(1 - side, whole(lambda c: back[c]))

    def home_early(j, _):
        def put(w, value, slope):
            cols = pl.ds(pl.multiple_of((2 * j + w) * e, e), e)
            acts_early[:tok, cols] = value
            acts_early[tok:, cols] = slope

        home(j, put)
        return 0

    def put_late(w, value, slope):
        cols = pl.ds(pl.multiple_of(w * e, e), e)
        acts_late[0, :tok, cols] = value
        acts_late[0, tok:, cols] = slope

    wide = width // HALVES
    tile = min(256, wide)

    def product(block, half, store):
        def step(i, _):
            at = pl.multiple_of(i * tile, tile)
            first = (block * HALVES + half) * wide
            source = pl.ds(pl.multiple_of(first + at, tile), tile)
            store(pl.ds(at, tile), dot(acts_early[...], weight_early[:, source], (1, 0)))
            return 0

        lax.fori_loop(0, wide // tile, step, 0)

    def to_mate(i, k):
        device = {"tensor": mate}
        return remote(pair_send.at[i, k], pair_recv.at[i, k], pair_sems, (i, k), device)

    def to_far(i, k):
        device = {"tensor": 2 * lax.rem(group + 1 + i, groups) + core}
        return remote(far_send.at[i, k], far_recv.at[i, k], far_sems, (i, k), device)

    def project_early():
        lax.fori_loop(0, early, home_early, 0)
        for load in loads:
            load.wait()
        for i in range(groups):
            there = lax.rem(group + 1 + i, groups)
            for k in range(HALVES):

                def keep_pair(cols, value, i=i, k=k):
                    pair_send[i, k, :, cols] = value.astype(jnp.bfloat16)

                product(2 * there + 1 - core, k, keep_pair)
                to_mate(i, k).start()
            for k in range(HALVES):

                def keep_own(cols, value, i=i, k=k):
                    own[i, k, :, cols] = value

                product(2 * there + core, k, keep_own)
                if i < last:
                    to_mate(i, k).wait()
                    total = own[i, k] + pair_recv[i, k].astype(jnp.float32)
                    far_send[i, k] = total.astype(jnp.bfloat16)
                    to_far(i, k).start()

    def add_late(slot):
        for k in range(HALVES):

            def step(i, _, k=k):
                at = pl.multiple_of(i * tile, tile)
                cols = pl.ds(at, tile)
                source = pl.ds(pl.multiple_of(k * wide + at, tile), tile)
                more = dot(acts_late[slot], weight_late[slot, :, source], (1, 0))
                own[last, k, :, cols] = own[last, k, :, cols] + more
                return 0

            lax.fori_loop(0, wide // tile, step, 0)

    def project_late():
        for slot in [2 * d for d in range(1, groups)] + [1]:
            acts_copy(slot).start()
        for k in range(HALVES):
            to_mate(last, k).wait()
            own[last, k] = own[last, k] + pair_recv[last, k].astype(jnp.float32)
        for load in late_loads:
            load.wait()
        for slot in range(1, parts):
            for w in sides:
                weight_copy(slot, w).wait_recv()
        add_late(0)
        acts_copy(1).wait_recv()
        add_late(1)
        for d in range(1, groups):
            acts_copy(2 * d).wait_recv()
            forward(2 * d).start()
            add_late(2 * d)
        for d in range(1, groups):
            forward(2 * d).wait_recv()
            add_late(2 * d + 1)
        for k in range(HALVES):
            total = own[last, k]
            for i in range(last):
                to_far(i, k).wait()
                total = total + far_recv[i, k].astype(jnp.float32)
            out_ref[:, k * wide : (k + 1) * wide] = total.astype(jnp.bfloat16)

    def gather(c, slots):
        pieces = [(own_piece[c], own_stats[c, :, 0:1], own_stats[c, :, 1:2])]
        for slot in slots:
            for copy in piece_copies(slot, c, 2):
                copy.wait_recv()
            stats = stats_in[slot, c]
            stats = jnp.concatenate([stats, jnp.zeros((120, stats.shape[1]), jnp.float32)], 0).T
            rows = piece_in[slot, c].reshape(some * 2 * per, 2 * e).astype(jnp.float32)
            pieces.append((rows, stats[:, 0:1], stats[:, 1:2]))
        rows = merge(pieces)
        for i in range(some):
            finish(c, i, rows[i * 2 * per : (i + 1) * 2 * per])
        back_copy(c).start()

    def collect(c):
        @pl.when(level == 2)
        def _():
            gather(c, (0,))

        @pl.when(level == 3)
        def _():
            gather(c, (0, 1))

    ahead, lag = 2, CUTS - 1
    for c in range(ahead):
        advance(c)

    def feed(j, _):
        place((1 - side) * here + j)
        lax.fori_loop(CUTS * j, CUTS * (j + 1), scatter, 0)
        place(side * here + j)
        return 0

    lax.fori_loop(1, here, feed, 0)

    def turn(c, _):
        @pl.when(c + ahead < steps)
        def _():
            advance(c + ahead)

        work(c)

        @pl.when(c >= lag)
        def _():
            collect(c - lag)

        @pl.when(c == steps - 2)
        def _():
            project_early()

        return 0

    lax.fori_loop(0, steps, turn, 0)

    def rest(c, _):
        collect(c)
        return 0

    lax.fori_loop(steps - lag, steps, rest, 0)
    home(early, put_late)
    project_late()

    def drain(c, _):
        side_copy(c).wait_send()
        back_copy(c).wait_send()

        @pl.when(level == 0)
        def _():
            key_copy(c).wait_send()

        @pl.when(level == 1)
        def _():
            for slot in (0, 1):
                for copy in piece_copies(slot, c, 2 + slot):
                    copy.wait_send()

        @pl.when(level == 2)
        def _():
            query_copy(0, c, 1).wait_send()
            for copy in piece_copies(0, c, 3):
                copy.wait_send()

        @pl.when(level == 3)
        def _():
            query_copy(0, c, 2).wait_send()
            query_copy(1, c, 1).wait_send()

        return 0

    lax.fori_loop(0, steps, drain, 0)
    for slot in range(1, parts):
        for w in sides:
            weight_copy(slot, w).wait_send()
    acts_copy(1).wait_send()
    for d in range(1, groups):
        acts_copy(2 * d).wait_send()
        forward(2 * d).wait_send()


def level_body(parts, q, k, v, dq, dk, dv, routes, weight):
    tok, heads = routes.shape
    e = HEAD_SIZE
    n = 2 * LEVELS
    per = tok // n
    steps = CUTS * (heads // 2)
    some = n // CUTS
    rows = some * 2 * per
    groups = parts // 2
    width = weight.shape[1] // parts
    half = jnp.bfloat16
    vmem = pl.BlockSpec(memory_space=pltpu.VMEM)
    dma = pltpu.SemaphoreType.DMA
    shape = jax.ShapeDtypeStruct((2 * tok, width), half)
    both = pl.pallas_call(
        functools.partial(level_kernel, parts),
        out_shape=shape,
        in_specs=[vmem] * 7 + [pl.BlockSpec(memory_space=pl.ANY)],
        out_specs=vmem,
        scratch_shapes=[
            pltpu.VMEM((heads, tok), jnp.float32),
            pltpu.VMEM((heads, tok, tok), half),
            pltpu.VMEM((steps, some, per, 6 * e), half),
            pltpu.VMEM((steps, 2, some, per, 6 * e), half),
            pltpu.VMEM((steps, 2, some, per, 4 * e), half),
            pltpu.VMEM((2, steps, 2, some, per, 2 * e), half),
            pltpu.VMEM((2, steps, some, 2 * per, 2 * e), half),
            pltpu.VMEM((2, steps, some, 2 * per, 2 * e), half),
            pltpu.VMEM((2, steps, 8, rows), jnp.float32),
            pltpu.VMEM((2, steps, 8, rows), jnp.float32),
            pltpu.VMEM((steps, rows, 2 * e), jnp.float32),
            pltpu.VMEM((steps, rows, 128), jnp.float32),
            pltpu.VMEM((steps, 2, some, per, 2 * e), half),
            pltpu.VMEM((steps, some, per, 2 * e), half),
            pltpu.VMEM(((heads - 2) * e, weight.shape[1]), half),
            pltpu.VMEM((parts, 2 * e, width), half),
            pltpu.VMEM((2 * tok, (heads - 2) * e), half),
            pltpu.VMEM((parts, 2 * tok, 2 * e), half),
            pltpu.VMEM((groups, HALVES, 2 * tok, width // HALVES), jnp.float32),
            pltpu.VMEM((groups, HALVES, 2 * tok, width // HALVES), half),
            pltpu.VMEM((groups, HALVES, 2 * tok, width // HALVES), half),
            pltpu.VMEM((max(groups - 1, 1), HALVES, 2 * tok, width // HALVES), half),
            pltpu.VMEM((max(groups - 1, 1), HALVES, 2 * tok, width // HALVES), half),
            dma((heads - 2,)),
            dma((2,)),
            dma((2, parts, 2)),
            dma((2, parts)),
            dma((2, steps)),
            dma((2, steps)),
            dma((2, 2, steps)),
            dma((2, 2, steps)),
            dma((2, 2, steps)),
            dma((2, steps)),
            dma((2, groups, HALVES)),
            dma((2, max(groups - 1, 1), HALVES)),
        ],
        compiler_params=pltpu.CompilerParams(
            collective_id=1, has_side_effects=True, vmem_limit_bytes=58 * 2**20
        ),
    )(q, k, v, dq, dk, dv, routes.T, weight)
    return split(both)


def solution(mesh):
    n, parts = mesh.shape["seq"], mesh.shape["tensor"]

    def run(*args):
        if n == 2 * LEVELS and args[6].shape[1] % 2 == 0 and args[6].shape[1] >= 4:
            return level_body(parts, *args)
        return body(n, parts, *args)

    return jax.shard_map(
        run,
        mesh=mesh,
        in_specs=(P("seq", "tensor"),) * 7 + (P("tensor", None),),
        out_specs=(P("seq", "tensor"), P("seq", "tensor")),
        check_vma=False,
    )
```

```python
import functools

import jax
import jax.numpy as jnp
from jax import lax
from jax.experimental import pallas as pl
from jax.experimental.pallas import tpu as pltpu
from jax.sharding import PartitionSpec as P

HEAD_SIZE = 128
MESH = pl.DeviceIdType.MESH
HALVES = 2


def dot(a, b, contract):
    return lax.dot_general(
        a, b, (((contract[0],), (contract[1],)), ((), ())), preferred_element_type=jnp.float32
    )


def attend(rows):
    e = HEAD_SIZE
    scale = e**-0.5
    count = rows.shape[0]
    query, key = rows[:, e : 2 * e], rows[:, 2 * e : 3 * e]
    scores = dot(query, key, (1, 1)) * scale
    tangent = dot(rows[:, : 2 * e], rows[:, 2 * e : 4 * e], (1, 1)) * scale
    visible = lax.broadcasted_iota(jnp.int32, (count, count), 1) <= lax.broadcasted_iota(
        jnp.int32, (count, count), 0
    )
    masked = jnp.where(visible, scores, -jnp.inf)
    expo = jnp.exp(masked - jnp.max(masked, -1, keepdims=True))
    probs = expo / jnp.sum(expo, -1, keepdims=True)
    slope = probs * (tangent - jnp.sum(probs * tangent, -1, keepdims=True))
    both = dot(probs.astype(jnp.bfloat16), rows[:, 4 * e :], (1, 0))
    extra = dot(slope.astype(jnp.bfloat16), rows[:, 4 * e : 5 * e], (1, 0))
    return jnp.concatenate([both[:, :e], both[:, e:] + extra], 1).astype(jnp.bfloat16)


def kernel(
    n,
    parts,
    q_ref,
    k_ref,
    v_ref,
    dq_ref,
    dk_ref,
    dv_ref,
    routes_ref,
    weight_hbm,
    out_ref,
    dest,
    order,
    sent,
    got,
    result,
    back,
    weight,
    acts,
    own,
    pair_send,
    pair_recv,
    far_send,
    far_recv,
    weight_sem,
    go_send,
    go_recv,
    back_send,
    back_recv,
    pair_sems,
    far_sems,
):
    e = HEAD_SIZE
    tok, width = q_ref.shape
    heads = width // e
    per = tok // n
    groups = parts // 2
    me = lax.axis_index("seq")
    mine = lax.axis_index("tensor")
    group, core = lax.div(mine, 2), lax.rem(mine, 2)
    mate = 2 * group + 1 - core

    barrier = pltpu.get_barrier_semaphore()
    for d in range(1, n):
        pl.semaphore_signal(
            barrier, inc=1, device_id={"seq": lax.rem(me + d, n)}, device_id_type=MESH
        )
    pl.semaphore_signal(barrier, inc=1, device_id={"tensor": mate}, device_id_type=MESH)
    for d in range(1, groups):
        pl.semaphore_signal(
            barrier,
            inc=1,
            device_id={"tensor": 2 * lax.rem(group + d, groups) + core},
            device_id_type=MESH,
        )
    load = pltpu.make_async_copy(weight_hbm, weight, weight_sem)
    load.start()

    row_at = lax.broadcasted_iota(jnp.int32, (tok, tok), 0)
    earlier = (row_at < lax.broadcasted_iota(jnp.int32, (tok, tok), 1)).astype(jnp.float32)
    earlier = earlier.astype(jnp.bfloat16)
    cluster = lax.broadcasted_iota(jnp.int32, (n, tok), 0)
    dest[...] = jnp.right_shift(routes_ref[...], tok.bit_length() - 1).astype(jnp.float32)

    def place(h, _):
        member = (dest[pl.ds(h, 1), :] == cluster.astype(jnp.float32)).astype(jnp.float32)
        rank = dot(member.astype(jnp.bfloat16), earlier, (1, 0))
        at = jnp.sum(member * (rank + (per * cluster).astype(jnp.float32)), 0, keepdims=True)
        order[h] = (row_at.astype(jnp.float32) == at).astype(jnp.float32).astype(jnp.bfloat16)
        return 0

    lax.fori_loop(0, heads, place, 0)
    pl.semaphore_wait(barrier, n - 1 + groups)

    def go(h, d):
        peer = lax.rem(me + d, n)
        return pltpu.make_async_remote_copy(
            src_ref=sent.at[h, peer],
            dst_ref=got.at[h, me],
            send_sem=go_send.at[h, d],
            recv_sem=go_recv.at[h, d],
            device_id={"seq": peer},
            device_id_type=MESH,
        )

    def come(h, d):
        peer = lax.rem(me + d, n)
        return pltpu.make_async_remote_copy(
            src_ref=result.at[h, peer],
            dst_ref=back.at[h, me],
            send_sem=back_send.at[h, d],
            recv_sem=back_recv.at[h, d],
            device_id={"seq": peer},
            device_id_type=MESH,
        )

    def scatter(h, _):
        cols = pl.ds(pl.multiple_of(h * e, e), e)
        rows = jnp.concatenate(
            [r[:, cols] for r in (dq_ref, q_ref, k_ref, dk_ref, v_ref, dv_ref)], 1
        )
        placed = dot(order[h], rows, (1, 0)).astype(jnp.bfloat16)
        sent[h] = placed.reshape(n, per, 6 * e)
        got[h, me] = sent[h, me]

        def start(d, _):
            go(h, d).start()
            return 0

        lax.fori_loop(1, n, start, 0)
        return 0

    lax.fori_loop(0, heads, scatter, 0)

    def work(h, _):
        def wait(d, _):
            go(h, d).wait()
            return 0

        lax.fori_loop(1, n, wait, 0)
        result[h] = attend(got[h].reshape(tok, 6 * e)).reshape(n, per, 2 * e)
        back[h, me] = result[h, me]

        def start(d, _):
            come(h, d).start()
            return 0

        lax.fori_loop(1, n, start, 0)
        return 0

    lax.fori_loop(0, heads, work, 0)

    def home(h, _):
        def wait(d, _):
            come(h, d).wait()
            return 0

        lax.fori_loop(1, n, wait, 0)
        rows = dot(order[h], back[h].reshape(tok, 2 * e), (0, 0)).astype(jnp.bfloat16)
        cols = pl.ds(pl.multiple_of(h * e, e), e)
        acts[:tok, cols] = rows[:, :e]
        acts[tok:, cols] = rows[:, e:]
        return 0

    lax.fori_loop(0, heads, home, 0)
    load.wait()
    project(groups, group, core, mate, weight, acts, own, pair_send, pair_recv, far_send,
            far_recv, pair_sems, far_sems, out_ref)


def project(groups, group, core, mate, weight, acts, own, pair_send, pair_recv, far_send,
            far_recv, pair_sems, far_sems, out_ref):
    wide = out_ref.shape[1] // HALVES
    tile = min(256, wide)

    def product(block, half, store):
        def step(i, _):
            at = pl.multiple_of(i * tile, tile)
            first = (block * HALVES + half) * wide
            source = pl.ds(pl.multiple_of(first + at, tile), tile)
            store(pl.ds(at, tile), dot(acts[...], weight[:, source], (1, 0)))
            return 0

        lax.fori_loop(0, wide // tile, step, 0)

    def to_mate(i, k):
        return pltpu.make_async_remote_copy(
            src_ref=pair_send.at[i, k],
            dst_ref=pair_recv.at[i, k],
            send_sem=pair_sems.at[0, i, k],
            recv_sem=pair_sems.at[1, i, k],
            device_id={"tensor": mate},
            device_id_type=MESH,
        )

    def to_far(i, k):
        return pltpu.make_async_remote_copy(
            src_ref=far_send.at[i, k],
            dst_ref=far_recv.at[i, k],
            send_sem=far_sems.at[0, i, k],
            recv_sem=far_sems.at[1, i, k],
            device_id={"tensor": 2 * lax.rem(group + 1 + i, groups) + core},
            device_id_type=MESH,
        )

    last = groups - 1
    for i in range(groups):
        there = lax.rem(group + 1 + i, groups)
        for k in range(HALVES):

            def keep_pair(cols, value, i=i, k=k):
                pair_send[i, k, :, cols] = value.astype(jnp.bfloat16)

            product(2 * there + 1 - core, k, keep_pair)
            to_mate(i, k).start()
        for k in range(HALVES):

            def keep_own(cols, value, i=i, k=k):
                own[i, k, :, cols] = value

            product(2 * there + core, k, keep_own)
            if i < last:
                to_mate(i, k).wait()
                total = own[i, k] + pair_recv[i, k].astype(jnp.float32)
                far_send[i, k] = total.astype(jnp.bfloat16)
                to_far(i, k).start()
    for k in range(HALVES):
        to_mate(last, k).wait()
        own[last, k] = own[last, k] + pair_recv[last, k].astype(jnp.float32)
    for k in range(HALVES):
        total = own[last, k]
        for i in range(last):
            to_far(i, k).wait()
            total = total + far_recv[i, k].astype(jnp.float32)
        out_ref[:, k * wide : (k + 1) * wide] = total.astype(jnp.bfloat16)


def split_kernel(both_ref, out_ref, tan_ref):
    tok = out_ref.shape[0]
    out_ref[...] = both_ref[:tok]
    tan_ref[...] = both_ref[tok:]


def split(both):
    vmem = pl.BlockSpec(memory_space=pltpu.VMEM)
    shape = jax.ShapeDtypeStruct((both.shape[0] // 2, both.shape[1]), both.dtype)
    return pl.pallas_call(
        split_kernel, out_shape=(shape, shape), in_specs=[vmem], out_specs=(vmem, vmem)
    )(both)


def body(n, parts, q, k, v, dq, dk, dv, routes, weight):
    tok, heads = routes.shape
    e = HEAD_SIZE
    per = tok // n
    groups = parts // 2
    width = weight.shape[1] // parts
    half = jnp.bfloat16
    vmem = pl.BlockSpec(memory_space=pltpu.VMEM)
    dma = pltpu.SemaphoreType.DMA
    shape = jax.ShapeDtypeStruct((2 * tok, width), half)
    both = pl.pallas_call(
        functools.partial(kernel, n, parts),
        out_shape=shape,
        in_specs=[vmem] * 7 + [pl.BlockSpec(memory_space=pl.ANY)],
        out_specs=vmem,
        scratch_shapes=[
            pltpu.VMEM((heads, tok), jnp.float32),
            pltpu.VMEM((heads, tok, tok), half),
            pltpu.VMEM((heads, n, per, 6 * e), half),
            pltpu.VMEM((heads, n, per, 6 * e), half),
            pltpu.VMEM((heads, n, per, 2 * e), half),
            pltpu.VMEM((heads, n, per, 2 * e), half),
            pltpu.VMEM(weight.shape, half),
            pltpu.VMEM((2 * tok, heads * e), half),
            pltpu.VMEM((groups, HALVES, 2 * tok, width // HALVES), jnp.float32),
            pltpu.VMEM((groups, HALVES, 2 * tok, width // HALVES), half),
            pltpu.VMEM((groups, HALVES, 2 * tok, width // HALVES), half),
            pltpu.VMEM((max(groups - 1, 1), HALVES, 2 * tok, width // HALVES), half),
            pltpu.VMEM((max(groups - 1, 1), HALVES, 2 * tok, width // HALVES), half),
            dma,
            dma((heads, n)),
            dma((heads, n)),
            dma((heads, n)),
            dma((heads, n)),
            dma((2, groups, HALVES)),
            dma((2, max(groups - 1, 1), HALVES)),
        ],
        compiler_params=pltpu.CompilerParams(
            collective_id=0, has_side_effects=True, vmem_limit_bytes=56 * 2**20
        ),
    )(q, k, v, dq, dk, dv, routes.T, weight)
    return split(both)


LEVELS = 4
CUTS = 4


def soft_rows(query, keys, offset):
    e = HEAD_SIZE
    scale = e**-0.5
    shape = (query.shape[0], keys.shape[0])
    scores = dot(query[:, e:], keys[:, :e], (1, 1)) * scale
    tangent = dot(query, keys[:, : 2 * e], (1, 1)) * scale
    visible = (
        lax.broadcasted_iota(jnp.int32, shape, 1)
        <= lax.broadcasted_iota(jnp.int32, shape, 0) + offset
    )
    masked = jnp.where(visible, scores, -jnp.inf)
    top = jnp.max(masked, -1, keepdims=True)
    expo = jnp.exp(masked - top)
    total = jnp.sum(expo, -1, keepdims=True)
    probs = expo / total
    mean = jnp.sum(probs * tangent, -1, keepdims=True)
    slope = probs * (tangent - mean)
    both = dot(probs.astype(jnp.bfloat16), keys[:, 2 * e :], (1, 0))
    extra = dot(slope.astype(jnp.bfloat16), keys[:, 2 * e : 3 * e], (1, 0))
    rows = jnp.concatenate([both[:, :e], both[:, e:] + extra], 1)
    return rows, top + jnp.log(total), mean


def pack_stats(level, mean):
    lane = lax.broadcasted_iota(jnp.int32, (level.shape[0], 128), 1)
    return jnp.where(lane == 0, level, jnp.where(lane == 1, mean, 0.0))


def merge(pieces):
    e = HEAD_SIZE
    top = functools.reduce(jnp.maximum, [level for _, level, _ in pieces])
    weights = [jnp.exp(level - top) for _, level, _ in pieces]
    total = functools.reduce(jnp.add, weights)
    weights = [w / total for w in weights]
    mean = sum(w * m for w, (_, _, m) in zip(weights, pieces))
    value = sum(w * rows[:, :e] for w, (rows, _, _) in zip(weights, pieces))
    slope = sum(
        w * (rows[:, e:] + (m - mean) * rows[:, :e]) for w, (rows, _, m) in zip(weights, pieces)
    )
    return jnp.concatenate([value, slope], 1)


def level_kernel(
    parts,
    q_ref,
    k_ref,
    v_ref,
    dq_ref,
    dk_ref,
    dv_ref,
    routes_ref,
    weight_hbm,
    out_ref,
    dest,
    order,
    sent,
    rows_here,
    keys_in,
    query_in,
    piece_out,
    piece_in,
    stats_out,
    stats_in,
    own_piece,
    own_stats,
    result,
    back,
    weight_early,
    weight_late,
    acts_early,
    acts_late,
    own,
    pair_send,
    pair_recv,
    far_send,
    far_recv,
    early_sems,
    late_sems,
    weight_sems,
    acts_sems,
    side_sems,
    key_sems,
    query_sems,
    piece_sems,
    stats_sems,
    back_sems,
    pair_sems,
    far_sems,
):
    e = HEAD_SIZE
    tok, width = q_ref.shape
    heads = width // e
    n = 2 * LEVELS
    per = tok // n
    here = heads // 2
    steps = CUTS * here
    some = n // CUTS
    groups = parts // 2
    me = lax.axis_index("seq")
    mine = lax.axis_index("tensor")
    level, side = lax.div(me, 2), lax.rem(me, 2)
    group, core = lax.div(mine, 2), lax.rem(mine, 2)
    mate = 2 * group + 1 - core


    def tensor_peer(slot):
        which = core if slot % 2 == 0 else 1 - core
        return 2 * lax.rem(group + slot // 2, groups) + which

    barrier = pltpu.get_barrier_semaphore()
    for d in range(1, LEVELS):
        peer = 2 * lax.rem(level + d, LEVELS) + side
        pl.semaphore_signal(barrier, inc=1, device_id={"seq": peer}, device_id_type=MESH)
    pl.semaphore_signal(
        barrier, inc=1, device_id={"seq": 2 * level + 1 - side}, device_id_type=MESH
    )
    for slot in range(1, parts):
        pl.semaphore_signal(
            barrier, inc=1, device_id={"tensor": tensor_peer(slot)}, device_id_type=MESH
        )
    early, last = here - 1, groups - 1
    sides = (0, 1)
    loads = [
        pltpu.make_async_copy(
            weight_hbm.at[pl.ds((w * here + j) * e, e), :],
            weight_early.at[pl.ds((2 * j + w) * e, e), :],
            early_sems.at[2 * j + w],
        )
        for j in range(early)
        for w in sides
    ]

    def late_weight(w, block):
        rows = pl.ds((w * here + early) * e, e)
        return weight_hbm.at[rows, pl.ds(pl.multiple_of(block * width, width), width)]

    late_loads = [
        pltpu.make_async_copy(
            late_weight(w, mine), weight_late.at[0, pl.ds(w * e, e), :], late_sems.at[w]
        )
        for w in sides
    ]
    for load in loads + late_loads:
        load.start()

    row_at = lax.broadcasted_iota(jnp.int32, (tok, tok), 0)
    earlier = (row_at < lax.broadcasted_iota(jnp.int32, (tok, tok), 1)).astype(jnp.float32)
    earlier = earlier.astype(jnp.bfloat16)
    cluster = lax.broadcasted_iota(jnp.int32, (n, tok), 0)
    dest[...] = jnp.right_shift(routes_ref[...], tok.bit_length() - 1).astype(jnp.float32)

    def place(h):
        member = (dest[pl.ds(h, 1), :] == cluster.astype(jnp.float32)).astype(jnp.float32)
        rank = dot(member.astype(jnp.bfloat16), earlier, (1, 0))
        at = jnp.sum(member * (rank + (per * cluster).astype(jnp.float32)), 0, keepdims=True)
        order[h] = (row_at.astype(jnp.float32) == at).astype(jnp.float32).astype(jnp.bfloat16)

    place((1 - side) * here)
    pl.semaphore_wait(barrier, LEVELS + parts - 1)

    def remote(src, dst, sems, at, device):
        return pltpu.make_async_remote_copy(
            src_ref=src,
            dst_ref=dst,
            send_sem=sems.at[(0, *at)],
            recv_sem=sems.at[(1, *at)],
            device_id=device,
            device_id_type=MESH,
        )

    across = {"seq": 2 * level + 1 - side}

    def at_level(z):
        return {"seq": 2 * z + side}

    def side_copy(c):
        return remote(sent.at[c], rows_here.at[c, side], side_sems, (c,), across)

    def key_copy(c):
        keys = rows_here.at[c, :, :, :, pl.ds(2 * e, 4 * e)]
        return remote(keys, keys_in.at[c], key_sems, (c,), at_level(1))

    def query_copy(slot, c, z):
        queries = rows_here.at[c, :, :, :, pl.ds(0, 2 * e)]
        return remote(queries, query_in.at[slot, c], query_sems, (slot, c), at_level(z))

    def piece_copies(slot, c, z):
        return (
            remote(piece_out.at[slot, c], piece_in.at[slot, c], piece_sems, (slot, c), at_level(z)),
            remote(stats_out.at[slot, c], stats_in.at[slot, c], stats_sems, (slot, c), at_level(z)),
        )

    def back_copy(c):
        return remote(result.at[c, 1 - side], back.at[c], back_sems, (c,), across)

    def placed(h, c):
        cols = pl.ds(pl.multiple_of(h * e, e), e)
        rows = jnp.concatenate(
            [r[:, cols] for r in (dq_ref, q_ref, k_ref, dk_ref, v_ref, dv_ref)], 1
        )
        size = tok // CUTS
        cut = pl.ds(pl.multiple_of(lax.rem(c, CUTS) * size, size), size)
        moved = dot(order[h, cut, :], rows, (1, 0)).astype(jnp.bfloat16)
        return moved.reshape(some, per, 6 * e)

    def scatter(c, _):
        sent[c] = placed((1 - side) * here + lax.div(c, CUTS), c)
        side_copy(c).start()
        return 0

    lax.fori_loop(0, CUTS, scatter, 0)
    place(side * here)

    def weight_copy(slot, w):
        peer = tensor_peer(slot)
        dst = weight_late.at[slot, pl.ds(w * e, e), :]
        return remote(late_weight(w, peer), dst, weight_sems, (slot, w), {"tensor": peer})

    def acts_copy(slot):
        device = {"tensor": tensor_peer(slot)}
        return remote(acts_late.at[0], acts_late.at[slot], acts_sems, (slot,), device)

    def forward(slot):
        device = {"tensor": mate}
        return remote(acts_late.at[slot], acts_late.at[slot + 1], acts_sems, (slot + 1,), device)

    for slot in range(1, parts):
        for w in sides:
            weight_copy(slot, w).start()

    def pair_of(ref, i):
        return jnp.concatenate([ref[0, i], ref[1, i]], 0)

    def finish(c, i, rows):
        rows = rows.astype(jnp.bfloat16)
        result[c, 0, i] = rows[:per]
        result[c, 1, i] = rows[per:]

    def hand_on(slot, c, z, parts_of):
        for i, (rows, _, _) in enumerate(parts_of):
            piece_out[slot, c, i] = rows.astype(jnp.bfloat16)
        packed = pack_stats(
            jnp.concatenate([p[1] for p in parts_of], 0),
            jnp.concatenate([p[2] for p in parts_of], 0),
        )
        stats_out[slot, c] = packed.T[:2]
        for copy in piece_copies(slot, c, z):
            copy.start()

    def keep(c, parts_of):
        own_piece[c] = jnp.concatenate([p[0] for p in parts_of], 0)
        own_stats[c] = pack_stats(
            jnp.concatenate([p[1] for p in parts_of], 0),
            jnp.concatenate([p[2] for p in parts_of], 0),
        )

    def advance(c):
        rows_here[c, side] = placed(side * here + lax.div(c, CUTS), c)
        side_copy(c).wait_recv()

        @pl.when(level == 0)
        def _():
            key_copy(c).start()

        @pl.when(level == 2)
        def _():
            query_copy(0, c, 1).start()

        @pl.when(level == 3)
        def _():
            query_copy(0, c, 2).start()
            query_copy(1, c, 1).start()

    def work(c):
        own_rows = rows_here.at[c]
        size = 2 * per

        def cut(piece, j):
            return tuple(x[j * size : (j + 1) * size] for x in piece)

        @pl.when(level == 0)
        def _():
            for i in range(some):
                rows = pair_of(own_rows, i)
                finish(c, i, soft_rows(rows[:, : 2 * e], rows[:, 2 * e :], 0)[0])
            back_copy(c).start()

        @pl.when(level == 1)
        def _():
            key_copy(c).wait_recv()
            query_copy(0, c, 1).wait_recv()
            query_copy(1, c, 1).wait_recv()
            pieces = []
            for i in range(some):
                rows = pair_of(own_rows, i)
                queries = jnp.concatenate(
                    [
                        rows[:, : 2 * e],
                        pair_of(query_in.at[0, c], i),
                        pair_of(query_in.at[1, c], i),
                    ],
                    0,
                )
                keys = jnp.concatenate([pair_of(keys_in.at[c], i), rows[:, 2 * e :]], 0)
                pieces.append(soft_rows(queries, keys, size))
            hand_on(1, c, 3, [cut(p, 2) for p in pieces])
            hand_on(0, c, 2, [cut(p, 1) for p in pieces])
            for i in range(some):
                finish(c, i, pieces[i][0][:size])
            back_copy(c).start()

        @pl.when(level == 2)
        def _():
            query_copy(0, c, 1).wait_recv()
            pieces = []
            for i in range(some):
                rows = pair_of(own_rows, i)
                queries = jnp.concatenate([rows[:, : 2 * e], pair_of(query_in.at[0, c], i)], 0)
                pieces.append(soft_rows(queries, rows[:, 2 * e :], 0))
            hand_on(0, c, 3, [cut(p, 1) for p in pieces])
            keep(c, [cut(p, 0) for p in pieces])

        @pl.when(level == 3)
        def _():
            pieces = []
            for i in range(some):
                rows = pair_of(own_rows, i)
                pieces.append(soft_rows(rows[:, : 2 * e], rows[:, 2 * e :], 0))
            keep(c, pieces)

    def home(j, put):
        def whole(at):
            return jnp.concatenate(
                [at(CUTS * j + p).reshape(tok // CUTS, 2 * e) for p in range(CUTS)], 0
            )

        def back_home(w, rows):
            rows = dot(order[w * here + j], rows, (0, 0)).astype(jnp.bfloat16)
            put(w, rows[:, :e], rows[:, e:])

        back_home(side, whole(lambda c: result[c, side]))
        for p in range(CUTS):
            back_copy(CUTS * j + p).wait_recv()
        back_home(1 - side, whole(lambda c: back[c]))

    def home_early(j, _):
        def put(w, value, slope):
            cols = pl.ds(pl.multiple_of((2 * j + w) * e, e), e)
            acts_early[:tok, cols] = value
            acts_early[tok:, cols] = slope

        home(j, put)
        return 0

    def put_late(w, value, slope):
        cols = pl.ds(pl.multiple_of(w * e, e), e)
        acts_late[0, :tok, cols] = value
        acts_late[0, tok:, cols] = slope

    wide = width // HALVES
    tile = min(256, wide)

    def product(block, half, store):
        def step(i, _):
            at = pl.multiple_of(i * tile, tile)
            first = (block * HALVES + half) * wide
            source = pl.ds(pl.multiple_of(first + at, tile), tile)
            store(pl.ds(at, tile), dot(acts_early[...], weight_early[:, source], (1, 0)))
            return 0

        lax.fori_loop(0, wide // tile, step, 0)

    def to_mate(i, k):
        device = {"tensor": mate}
        return remote(pair_send.at[i, k], pair_recv.at[i, k], pair_sems, (i, k), device)

    def to_far(i, k):
        device = {"tensor": 2 * lax.rem(group + 1 + i, groups) + core}
        return remote(far_send.at[i, k], far_recv.at[i, k], far_sems, (i, k), device)

    def project_early():
        lax.fori_loop(0, early, home_early, 0)
        for load in loads:
            load.wait()
        for i in range(groups):
            there = lax.rem(group + 1 + i, groups)
            for k in range(HALVES):

                def keep_pair(cols, value, i=i, k=k):
                    pair_send[i, k, :, cols] = value.astype(jnp.bfloat16)

                product(2 * there + 1 - core, k, keep_pair)
                to_mate(i, k).start()
            for k in range(HALVES):

                def keep_own(cols, value, i=i, k=k):
                    own[i, k, :, cols] = value

                product(2 * there + core, k, keep_own)
                if i < last:
                    to_mate(i, k).wait()
                    total = own[i, k] + pair_recv[i, k].astype(jnp.float32)
                    far_send[i, k] = total.astype(jnp.bfloat16)
                    to_far(i, k).start()

    def add_late(slot):
        for k in range(HALVES):

            def step(i, _, k=k):
                at = pl.multiple_of(i * tile, tile)
                cols = pl.ds(at, tile)
                source = pl.ds(pl.multiple_of(k * wide + at, tile), tile)
                more = dot(acts_late[slot], weight_late[slot, :, source], (1, 0))
                own[last, k, :, cols] = own[last, k, :, cols] + more
                return 0

            lax.fori_loop(0, wide // tile, step, 0)

    def project_late():
        for slot in [2 * d for d in range(1, groups)] + [1]:
            acts_copy(slot).start()
        for k in range(HALVES):
            to_mate(last, k).wait()
            own[last, k] = own[last, k] + pair_recv[last, k].astype(jnp.float32)
        for load in late_loads:
            load.wait()
        for slot in range(1, parts):
            for w in sides:
                weight_copy(slot, w).wait_recv()
        add_late(0)
        acts_copy(1).wait_recv()
        add_late(1)
        for d in range(1, groups):
            acts_copy(2 * d).wait_recv()
            forward(2 * d).start()
            add_late(2 * d)
        for d in range(1, groups):
            forward(2 * d).wait_recv()
            add_late(2 * d + 1)
        for k in range(HALVES):
            total = own[last, k]
            for i in range(last):
                to_far(i, k).wait()
                total = total + far_recv[i, k].astype(jnp.float32)
            out_ref[:, k * wide : (k + 1) * wide] = total.astype(jnp.bfloat16)

    def gather(c, slots):
        pieces = [(own_piece[c], own_stats[c, :, 0:1], own_stats[c, :, 1:2])]
        for slot in slots:
            for copy in piece_copies(slot, c, 2):
                copy.wait_recv()
            stats = stats_in[slot, c]
            stats = jnp.concatenate([stats, jnp.zeros((126, stats.shape[1]), jnp.float32)], 0).T
            rows = piece_in[slot, c].reshape(some * 2 * per, 2 * e).astype(jnp.float32)
            pieces.append((rows, stats[:, 0:1], stats[:, 1:2]))
        rows = merge(pieces)
        for i in range(some):
            finish(c, i, rows[i * 2 * per : (i + 1) * 2 * per])
        back_copy(c).start()

    def collect(c):
        @pl.when(level == 2)
        def _():
            gather(c, (0,))

        @pl.when(level == 3)
        def _():
            gather(c, (0, 1))

    ahead, lag = 2, CUTS - 1
    for c in range(ahead):
        advance(c)

    def feed(j, _):
        place((1 - side) * here + j)
        lax.fori_loop(CUTS * j, CUTS * (j + 1), scatter, 0)
        place(side * here + j)
        return 0

    lax.fori_loop(1, here, feed, 0)

    def turn(c, _):
        @pl.when(c + ahead < steps)
        def _():
            advance(c + ahead)

        work(c)

        @pl.when(c >= lag)
        def _():
            collect(c - lag)

        @pl.when(c == steps - 2)
        def _():
            project_early()

        return 0

    lax.fori_loop(0, steps, turn, 0)

    def rest(c, _):
        collect(c)
        return 0

    lax.fori_loop(steps - lag, steps, rest, 0)
    home(early, put_late)
    project_late()

    def drain(c, _):
        side_copy(c).wait_send()
        back_copy(c).wait_send()

        @pl.when(level == 0)
        def _():
            key_copy(c).wait_send()

        @pl.when(level == 1)
        def _():
            for slot in (0, 1):
                for copy in piece_copies(slot, c, 2 + slot):
                    copy.wait_send()

        @pl.when(level == 2)
        def _():
            query_copy(0, c, 1).wait_send()
            for copy in piece_copies(0, c, 3):
                copy.wait_send()

        @pl.when(level == 3)
        def _():
            query_copy(0, c, 2).wait_send()
            query_copy(1, c, 1).wait_send()

        return 0

    lax.fori_loop(0, steps, drain, 0)
    for slot in range(1, parts):
        for w in sides:
            weight_copy(slot, w).wait_send()
    acts_copy(1).wait_send()
    for d in range(1, groups):
        acts_copy(2 * d).wait_send()
        forward(2 * d).wait_send()


def level_body(parts, q, k, v, dq, dk, dv, routes, weight):
    tok, heads = routes.shape
    e = HEAD_SIZE
    n = 2 * LEVELS
    per = tok // n
    steps = CUTS * (heads // 2)
    some = n // CUTS
    rows = some * 2 * per
    groups = parts // 2
    width = weight.shape[1] // parts
    half = jnp.bfloat16
    vmem = pl.BlockSpec(memory_space=pltpu.VMEM)
    dma = pltpu.SemaphoreType.DMA
    shape = jax.ShapeDtypeStruct((2 * tok, width), half)
    both = pl.pallas_call(
        functools.partial(level_kernel, parts),
        out_shape=shape,
        in_specs=[vmem] * 7 + [pl.BlockSpec(memory_space=pl.ANY)],
        out_specs=vmem,
        scratch_shapes=[
            pltpu.VMEM((heads, tok), jnp.float32),
            pltpu.VMEM((heads, tok, tok), half),
            pltpu.VMEM((steps, some, per, 6 * e), half),
            pltpu.VMEM((steps, 2, some, per, 6 * e), half),
            pltpu.VMEM((steps, 2, some, per, 4 * e), half),
            pltpu.VMEM((2, steps, 2, some, per, 2 * e), half),
            pltpu.VMEM((2, steps, some, 2 * per, 2 * e), half),
            pltpu.VMEM((2, steps, some, 2 * per, 2 * e), half),
            pltpu.VMEM((2, steps, 2, rows), jnp.float32),
            pltpu.VMEM((2, steps, 2, rows), jnp.float32),
            pltpu.VMEM((steps, rows, 2 * e), jnp.float32),
            pltpu.VMEM((steps, rows, 128), jnp.float32),
            pltpu.VMEM((steps, 2, some, per, 2 * e), half),
            pltpu.VMEM((steps, some, per, 2 * e), half),
            pltpu.VMEM(((heads - 2) * e, weight.shape[1]), half),
            pltpu.VMEM((parts, 2 * e, width), half),
            pltpu.VMEM((2 * tok, (heads - 2) * e), half),
            pltpu.VMEM((parts, 2 * tok, 2 * e), half),
            pltpu.VMEM((groups, HALVES, 2 * tok, width // HALVES), jnp.float32),
            pltpu.VMEM((groups, HALVES, 2 * tok, width // HALVES), half),
            pltpu.VMEM((groups, HALVES, 2 * tok, width // HALVES), half),
            pltpu.VMEM((max(groups - 1, 1), HALVES, 2 * tok, width // HALVES), half),
            pltpu.VMEM((max(groups - 1, 1), HALVES, 2 * tok, width // HALVES), half),
            dma((heads - 2,)),
            dma((2,)),
            dma((2, parts, 2)),
            dma((2, parts)),
            dma((2, steps)),
            dma((2, steps)),
            dma((2, 2, steps)),
            dma((2, 2, steps)),
            dma((2, 2, steps)),
            dma((2, steps)),
            dma((2, groups, HALVES)),
            dma((2, max(groups - 1, 1), HALVES)),
        ],
        compiler_params=pltpu.CompilerParams(
            collective_id=1, has_side_effects=True, vmem_limit_bytes=58 * 2**20
        ),
    )(q, k, v, dq, dk, dv, routes.T, weight)
    return split(both)


def solution(mesh):
    n, parts = mesh.shape["seq"], mesh.shape["tensor"]

    def run(*args):
        if n == 2 * LEVELS and args[6].shape[1] % 2 == 0 and args[6].shape[1] >= 4:
            return level_body(parts, *args)
        return body(n, parts, *args)

    return jax.shard_map(
        run,
        mesh=mesh,
        in_specs=(P("seq", "tensor"),) * 7 + (P("tensor", None),),
        out_specs=(P("seq", "tensor"), P("seq", "tensor")),
        check_vma=False,
    )
```
